32 devices in a mesh: parent: 4 (over x, core), child: 8 (over z, y).
Axes of the slice: x: 2, y: 2, z: 4, core: 2. Of those that a mesh axis runs over, the one named last changes fastest.
Arguments:
- parent_tracer: float32 [2, 50, 64, 192], P(None, None, 'child', 'parent'), may hold values from -6 to 6
- child_tracer: float32 [2, 50, 864, 144], P(None, None, ('parent', 'child')), may hold values from -6 to 6
- strip_cols: int32 [4, 8], replicated, may hold values from 1 to 9, 48 in all within a row
- row_offset: int32 [1], replicated, may hold values from 0 to 16
- parent_wet: int32 [64, 192], P('child', 'parent'), may hold values 0 or 1
- child_wet: int32 [864, 144], P(('parent', 'child')), may hold values 0 or 1
- vert_mix: float32 [2, 49], replicated, may hold values from 0.2 to 5
Outputs:
- parent_next: float32 [2, 50, 64, 192], P(None, None, 'child', 'parent')
- child_next: float32 [2, 50, 864, 144], P(None, None, ('parent', 'child'))
The draws below stay inside these ranges and needn't reach their ends.
Inputs may be any that keep to these rules, and one draw needn't show every extreme that they name: Each row of strip_cols sums to 48; the largest entry is 9.
All inputs are finite; a program needn't handle non-finite values. No bound on the sum of `parent_wet` or of `child_wet` on one device may be relied on, other than what follows from the above.
Results may differ from the reference program's by a relative error of at most 0.00005.
Values sent between devices are 32-bit elements; how exact they have to be, the bound alone decides.
No kernel may reach another device: no remote copies, remote signals or barrier semaphores. Data moves between devices by JAX's collectives and lax.ppermute only.
A program may use at most 192 MiB of HBM per device.

```python
import math
import jax
import jax.numpy as jnp
import numpy as np
from jax import lax

TRACERS = 2
LEVELS = 50
CAPP = 9
CAP = 27
PGX = 48
PX = 192
PY = 64
FYT = 48
CY = 144
XCT = 864
N_PARENT = 4
N_CHILD = 8


def with_ends(values, rng, least, high):
    longest = values.shape.index(max(values.shape))
    spots = []
    for shift in (0, 1):
        where = [jax.random.randint(jax.random.fold_in(rng, axis), (), 0, length) for axis, length in enumerate(values.shape)]
        where[longest] = (where[longest] + shift) % values.shape[longest]
        spots.append(tuple(where))
    return values.at[spots[0]].set(least).at[spots[1]].set(high)


def shard_levels(key, dims, pieces, smallest, largest):
    def one(axis_at, shards_of):
        steps = jax.random.uniform(jax.random.fold_in(jax.random.fold_in(key, 6), axis_at), (shards_of,), jnp.float32, smallest / len(pieces), largest / len(pieces))
        return jnp.repeat(jnp.exp(steps), dims[axis_at] // shards_of).reshape((-1,) + (1,) * (len(dims) - axis_at - 1))

    loudness = one(*pieces[0])
    for cut in pieces[1:]:
        loudness = loudness * one(*cut)
    return loudness


def length_profile(amount, total, bound, skew):
    loads = [(1 << 20) // math.isqrt(rank ** skew) + 1 for rank in range(2, amount + 1)]
    surplus, counts = total - bound - (amount - 1), [1] * (amount - 1)
    while surplus > 0:
        candidates = [i for i in range(amount - 1) if counts[i] < bound]
        pool, left = sum([loads[i] for i in candidates]), surplus
        for i in candidates:
            extra = min(bound - counts[i], max(1, left * loads[i] // pool), surplus)
            counts[i] = counts[i] + extra
            surplus = surplus - extra
    return np.array([bound] + counts)


def uneven_parts(own_key, count, total, reach, lean):
    if count == 2:
        one = jax.random.randint(own_key, (), max(1, total - reach), min(reach, total - 1) + 1)
        return jnp.stack([one, total - one])
    lengths = jnp.asarray(length_profile(count, total, reach, lean), jnp.int32)
    pairs = (count - 1) // 2
    donor, taker = lengths[1:1 + 2 * pairs:2], lengths[2:2 + 2 * pairs:2]
    slack = jnp.minimum(donor - 1, reach - taker)
    shifted = jax.random.randint(jax.random.fold_in(own_key, 1), (pairs,), 0, 1 << 20) % (slack + 1)
    lengths = lengths.at[1:1 + 2 * pairs:2].set(donor - shifted).at[2:2 + 2 * pairs:2].set(taker + shifted)
    return lengths[jax.random.permutation(jax.random.fold_in(own_key, 2), count)]


def scatter_about(key, extent, deviation, most, pieces=(), kind=jnp.bfloat16):
    loudness = shard_levels(key, extent, pieces, -0.22, 0.18) if pieces else 1.0
    entries = jax.random.normal(key, extent, jnp.float32) * deviation * loudness
    return jnp.minimum(jnp.maximum(entries, -most), most).astype(kind)


def setup_inputs(seed: int = 0) -> dict:
    splits = jax.random.split(jax.random.key(seed), 8)
    return {
        "parent_tracer": scatter_about(splits[0], (TRACERS, LEVELS, PY, PX), 1.0, 6.0, ((2, 8), (3, 4)), jnp.float32),
        "child_tracer": scatter_about(splits[1], (TRACERS, LEVELS, XCT, CY), 1.0, 6.0, ((2, 32),), jnp.float32),
        "strip_cols": jax.vmap(lambda own: uneven_parts(own, N_CHILD, PGX, CAPP, 1))(jax.random.split(splits[2], N_PARENT)).reshape((N_PARENT, N_CHILD)).astype(jnp.int32),
        "row_offset": jax.random.randint(splits[3], (1,), 0, PY - FYT + 1).astype(jnp.int32),
        "parent_wet": with_ends((jax.random.randint(splits[4], (PY, PX), 0, 8) < 7).astype(jnp.int32), jax.random.fold_in(splits[4], 1), 0, 1),
        "child_wet": with_ends((jax.random.randint(splits[5], (XCT, CY), 0, 8) < 7).astype(jnp.int32), jax.random.fold_in(splits[5], 1), 0, 1),
        "vert_mix": jnp.clip(jnp.exp(jax.random.uniform(splits[6], (TRACERS, LEVELS - 1), jnp.float32, math.log(0.2), math.log(5.0))), 0.2, 5.0),
    }


diffusion = 0.2
nudging = 0.5
one_ninth = 1.0 / 9.0

def vertical_solve(field, vert_mix):
    tracers = field.shape[0]
    levels = field.shape[1]
    coefs = vert_mix.astype(field.dtype)
    zeros_col = jnp.zeros((tracers, 1), field.dtype)
    upper_coef = jnp.concatenate([coefs, zeros_col], axis=1)
    lower_coef = jnp.concatenate([zeros_col, coefs], axis=1)
    solved = lax.linalg.tridiagonal_solve(-lower_coef, 1.0 + upper_coef + lower_coef, -upper_coef, field.reshape(tracers, levels, -1))
    return solved.reshape(field.shape)

def reference(parent_tracer, child_tracer, strip_cols, row_offset, parent_wet, child_wet, vert_mix):
    parent_mask = parent_wet.astype(parent_tracer.dtype)
    parent_start = parent_mask * parent_tracer
    padded = jnp.pad(parent_start, ((0, 0), (0, 0), (1, 1), (1, 1)))
    laplace = padded[:, :, 2:, 1:-1] + padded[:, :, :-2, 1:-1] + padded[:, :, 1:-1, 2:] + padded[:, :, 1:-1, :-2] - 4.0 * parent_start
    parent_mid = vertical_solve(parent_mask * (parent_start + diffusion * laplace), vert_mix)
    offset = row_offset[0].astype(jnp.int32)
    widths = (3 * strip_cols.reshape(-1)).astype(jnp.int32)
    strip_ends = jnp.cumsum(widths).astype(jnp.int32)
    columns = jnp.arange(3 * PX, dtype=jnp.int32)
    owners = jnp.searchsorted(strip_ends, columns, side='right').astype(jnp.int32)
    local_col = (columns - (strip_ends[owners] - widths[owners])).astype(jnp.int32)
    tiled_cols = (owners * CAP + local_col).astype(jnp.int32)
    child_cells = jnp.take(child_tracer, tiled_cols, axis=2)
    child_mask = jnp.take(child_wet, tiled_cols, axis=0).astype(child_tracer.dtype)[None, None]
    footprint = lax.dynamic_slice_in_dim(parent_mid, offset, FYT, axis=2)
    panel_full = jnp.repeat(jnp.repeat(jnp.swapaxes(footprint, 2, 3), 3, axis=2), 3, axis=3)
    begin_cells = child_mask * child_cells
    xpadded = jnp.pad(begin_cells, ((0, 0), (0, 0), (1, 1), (0, 0)))
    ypadded = jnp.concatenate([panel_full[:, :, :, :1], begin_cells, panel_full[:, :, :, -1:]], axis=3)
    laplace_child = xpadded[:, :, 2:] + xpadded[:, :, :-2] + ypadded[:, :, :, 2:] + ypadded[:, :, :, :-2] - 4.0 * begin_cells
    child_mid = vertical_solve(child_mask * (begin_cells + diffusion * laplace_child), vert_mix)
    coarse = child_mid.reshape(TRACERS, LEVELS, PX, 3, FYT, 3).sum(axis=(3, 5)) * one_ninth
    spread = jnp.repeat(jnp.repeat(coarse, 3, axis=2), 3, axis=3)
    child_new = child_mask * (child_mid + nudging * (panel_full - spread))
    child_next = jnp.zeros_like(child_tracer).at[:, :, tiled_cols, :].set(child_new)
    parent_next = parent_mask * lax.dynamic_update_slice_in_dim(parent_mid, jnp.swapaxes(coarse, 2, 3), offset, axis=2)
    return (parent_next, child_next)
```

```python
import functools

import jax
import jax.numpy as jnp
from jax import lax
from jax.experimental import pallas as pl
from jax.experimental.pallas import tpu as pltpu
from jax.sharding import PartitionSpec as P

diffusion = 0.2
nudging = 0.5
one_ninth = 1.0 / 9.0
LANES = 128
ROWS = 32
HIGH = lax.Precision.HIGHEST

VM = pl.BlockSpec(memory_space=pltpu.VMEM)
SM = pl.BlockSpec(memory_space=pltpu.SMEM)


def params(mib):
    return pltpu.CompilerParams(vmem_limit_bytes=mib << 20)


def my_strip(cols_ref, strips):
    return cols_ref[lax.axis_index("parent"), lax.axis_index("child")]


def strip_starts(cols_ref, strips):
    group = lax.axis_index("parent")
    start = jnp.int32(0)
    starts = []
    for j in range(strips):
        starts.append(start)
        start = start + cols_ref[group, j]
    return starts


def coefficient_kernel(mix_ref, weight_ref, inverse_ref, d_ref, c_ref):
    tracers, levels = mix_ref.shape[0], mix_ref.shape[1] + 1
    lane = lax.broadcasted_iota(jnp.int32, (8, LANES), 1)
    which = lane // levels

    def mixed(k):
        row = jnp.zeros((8, LANES), jnp.float32)
        for t in range(tracers):
            row = jnp.where(which == t, mix_ref[t, k], row)
        return row

    weight = None
    d = None
    for k in range(levels):
        above = mixed(k - 1) if k else jnp.zeros((8, LANES), jnp.float32)
        below = mixed(k) if k < levels - 1 else jnp.zeros((8, LANES), jnp.float32)
        if k == 0:
            weight = 1.0 / (1.0 + below)
        else:
            weight = 1.0 / (1.0 + above + below - above * (above * weight))
        unit = (lane - which * levels == k).astype(jnp.float32)
        d = (unit if k == 0 else unit + above * d) * weight
        d_ref[pl.ds(8 * k, 8), :] = d
        c_ref[pl.ds(8 * k, 8), :] = below * weight
        for t in range(tracers):
            weight_ref[t * levels + k : t * levels + k + 1, :] = jnp.broadcast_to(
                weight[:1, t * levels : t * levels + 1], (1, LANES)
            )
    inverse_ref[...] = jnp.zeros_like(inverse_ref)
    x = None
    for k in reversed(range(levels)):
        x = d_ref[pl.ds(8 * k, 8), :]
        if k < levels - 1:
            x = x + c_ref[pl.ds(8 * k, 8), :] * above_x
        above_x = x
        for t in range(tracers):
            inverse_ref[t * levels + k : t * levels + k + 1, :] = jnp.where(which == t, x, 0.0)[:1]


def prepare_kernel(
    strips, cols_ref, parent_ref, pwet_ref, child_ref, cwet_ref,
    flat_ref, forth_ref, back_ref, left_ref, right_ref, nat_ref,
):
    total, capacity, child_rows = child_ref.shape
    rows, width = pwet_ref.shape
    lane_tiles = (child_rows + LANES - 1) // LANES
    level_rows = (total + 7) // 8 * 8
    wet = pwet_ref[...].astype(jnp.float32)
    for l in range(total):
        nat_ref[l * rows : (l + 1) * rows, :width] = wet * parent_ref[l * rows : (l + 1) * rows, :]
    nat_ref[total * rows : (total + 1) * rows, :width] = wet
    nat_ref[(total + 1) * rows :, :] = jnp.zeros((LANES * rows - (total + 1) * rows, LANES), jnp.float32)
    for r in range(rows):
        turned = nat_ref[pl.ds(r, LANES, stride=rows), :].T
        flat_ref[pl.ds(r, width, stride=rows), :] = turned[:width]
    left_ref[...] = flat_ref[:rows, :]
    right_ref[...] = flat_ref[(width - 1) * rows :, :]
    last = 3 * my_strip(cols_ref, strips) - 1
    for ref, x, r in ((forth_ref, last, rows - 1), (back_ref, 0, 0)):
        cell_wet = cwet_ref[pl.ds(x, 1), :].astype(jnp.float32)
        for l in range(total):
            row = child_ref[l, pl.ds(x, 1), :] * cell_wet
            for t in range(lane_tiles):
                stop = min(child_rows, (t + 1) * LANES)
                ref[t * level_rows + l : t * level_rows + l + 1, : stop - t * LANES] = row[:, t * LANES : stop]
        base = lane_tiles * level_rows
        ref[base : base + width, :] = flat_ref[pl.ds(r, width, stride=rows), :]


def solve_kernel(
    strips, rows,
    cols_ref, offset_ref, mix_ref, flat_ref, before_ref, after_ref, left_ref, right_ref,
    weight_ref, inverse_ref, child_ref, cwet_ref,
    send_ref, pmid_ref, own_ref, cmid_ref,
    explicit_ref, wide_ref, turn_ref, long_ref, d_ref,
):
    total, capacity, child_rows = child_ref.shape
    tracers, levels = mix_ref.shape[0], mix_ref.shape[1] + 1
    width = flat_ref.shape[0] // rows
    narrow = capacity // 3
    covered = child_rows // 3
    all_rows = strips * rows
    lane_tiles = (child_rows + LANES - 1) // LANES
    level_rows = (total + 7) // 8 * 8
    base = lane_tiles * level_rows
    member = lax.axis_index("child")
    starts = strip_starts(cols_ref, strips)
    last = 3 * my_strip(cols_ref, strips) - 1
    offset = offset_ref[0]

    has_before = (member > 0).astype(jnp.float32)
    has_after = (member < strips - 1).astype(jnp.float32)
    lane = lax.broadcasted_iota(jnp.int32, (rows, LANES), 1)
    for x in range(width):
        here = flat_ref[x * rows : (x + 1) * rows, :]
        west = left_ref[...] if x == 0 else flat_ref[(x - 1) * rows : x * rows, :]
        east = right_ref[...] if x == width - 1 else flat_ref[(x + 1) * rows : (x + 2) * rows, :]
        south = jnp.concatenate([has_before * before_ref[base + x : base + x + 1, :], here[:-1]], axis=0)
        north = jnp.concatenate([here[1:], has_after * after_ref[base + x : base + x + 1, :]], axis=0)
        wet = here[:, total : total + 1]
        laplace = north + south + east + west - 4.0 * here
        explicit_ref[x * rows : (x + 1) * rows, :] = wet * (here + diffusion * laplace)
    solved = jnp.dot(explicit_ref[...], inverse_ref[...], precision=HIGH, preferred_element_type=jnp.float32)
    flat_lane = lax.broadcasted_iota(jnp.int32, (width * rows, LANES), 1)
    wide_ref[: width * rows, :] = jnp.where(flat_lane == total, flat_ref[...], solved)
    wide_ref[width * rows :, :] = jnp.zeros((narrow * rows, LANES), jnp.float32)
    pmid_ref[...] = wide_ref[: width * rows, :]
    for j in range(strips):
        send_ref[j, : narrow * rows, :] = wide_ref[pl.ds(pl.multiple_of(starts[j] * rows, rows), narrow * rows), :]

    column = lax.broadcasted_iota(jnp.int32, (capacity, 1), 0)
    is_last = (column == last).astype(jnp.float32)
    mask = cwet_ref[...].astype(jnp.float32) * (column <= last).astype(jnp.float32)
    side = jnp.zeros((capacity, 1), jnp.float32)
    end = jnp.zeros((1, child_rows), jnp.float32)

    def edge(ref, l):
        parts = []
        for t in range(lane_tiles):
            stop = min(child_rows, (t + 1) * LANES)
            parts.append(ref[pl.ds(t * level_rows + l, 1), : stop - t * LANES])
        return jnp.concatenate(parts, axis=1)

    def explicit(l):
        begin = mask * child_ref[l]
        west = jnp.concatenate([edge(before_ref, l), begin[:-1]], axis=0)
        east = jnp.concatenate([begin[1:], end], axis=0) + is_last * edge(after_ref, l)
        south = jnp.concatenate([side, begin[:, :-1]], axis=1)
        north = jnp.concatenate([begin[:, 1:], side], axis=1)
        return mask * (begin + diffusion * (east + west + north + south - 4.0 * begin))

    def forward(k, carry):
        held = []
        for t in range(tracers):
            l = t * levels + k
            above = jnp.where(k > 0, mix_ref[t, jnp.maximum(k - 1, 0)], 0.0)
            d = (explicit(l) + above * carry[t]) * weight_ref[pl.ds(l, 1), :1]
            d_ref[l] = d
            held.append(d)
        return tuple(held)

    blank = jnp.zeros((capacity, child_rows), jnp.float32)
    lax.fori_loop(0, levels, forward, (blank,) * tracers)

    def backward(step, carry):
        k = levels - 1 - step
        held = []
        for t in range(tracers):
            l = t * levels + k
            below = jnp.where(k < levels - 1, mix_ref[t, jnp.minimum(k, levels - 2)], 0.0)
            x = d_ref[l] + (below * weight_ref[pl.ds(l, 1), :1]) * carry[t]
            for tile in range(lane_tiles):
                stop = min(child_rows, (tile + 1) * LANES)
                at = pl.ds(pl.multiple_of((tile * total + l) * ROWS, ROWS), capacity)
                cmid_ref[at, : stop - tile * LANES] = x[:, tile * LANES : stop]
            held.append(x)
        return tuple(held)

    lax.fori_loop(0, levels, backward, (blank,) * tracers)

    own_ref[...] = jnp.zeros_like(own_ref)
    turn_ref[...] = jnp.zeros_like(turn_ref)
    y = lax.broadcasted_iota(jnp.int32, (1, child_rows), 1)
    at_end = ((y == 0) | (y == child_rows - 1)).astype(jnp.float32)
    for q in range(narrow):
        for t in range(lane_tiles):
            stop = min(child_rows, (t + 1) * LANES)
            part = sum(
                cmid_ref[pl.ds(t * total * ROWS + 3 * q + dx, total, stride=ROWS), :] for dx in range(3)
            )
            turn_ref[:total, t * LANES : stop] = part[:, : stop - t * LANES]
        count = (mask[3 * q : 3 * q + 1] + mask[3 * q + 1 : 3 * q + 2] + mask[3 * q + 2 : 3 * q + 3]) * at_end
        turn_ref[total : total + 1, :child_rows] = count
        for t in range(lane_tiles):
            long_ref[t * LANES : (t + 1) * LANES, :] = turn_ref[:, t * LANES : (t + 1) * LANES].T
        mean = one_ninth * (
            long_ref[pl.ds(0, covered, stride=3), :]
            + long_ref[pl.ds(1, covered, stride=3), :]
            + long_ref[pl.ds(2, covered, stride=3), :]
        )
        own_ref[pl.ds(q * all_rows + offset, covered), :] = mean
    for k in range(strips):
        for q in range(narrow):
            send_ref[k, (narrow + q) * rows : (narrow + q + 1) * rows, :] = own_ref[
                q * all_rows + k * rows : q * all_rows + (k + 1) * rows, :
            ]


def finish_kernel(
    strips, rows, total,
    cols_ref, offset_ref, got_ref, own_ref, pmid_ref, inverse_ref, cmid_ref, cwet_ref,
    pnext_ref, cnext_ref,
    panel_ref, wide_ref, ends_ref, long_ref, add_ref, turn_ref, nat_ref,
):
    capacity, child_rows = cwet_ref.shape
    width = pmid_ref.shape[0] // rows
    narrow = capacity // 3
    covered = child_rows // 3
    all_rows = strips * rows
    lane_tiles = (child_rows + LANES - 1) // LANES
    padded = (narrow + 7) // 8 * 8
    member = lax.axis_index("child")
    starts = strip_starts(cols_ref, strips)
    last = 3 * my_strip(cols_ref, strips) - 1
    offset = offset_ref[0]

    ends_ref[...] = jnp.zeros_like(ends_ref)
    for q in range(narrow):
        for k in range(strips):
            panel_ref[q * all_rows + k * rows : q * all_rows + (k + 1) * rows, :] = got_ref[
                k, q * rows : (q + 1) * rows, :
            ]
        ends_ref[q : q + 1, :] = panel_ref[pl.ds(q * all_rows + offset, 1), :]
        ends_ref[padded + q : padded + q + 1, :] = panel_ref[pl.ds(q * all_rows + offset + covered - 1, 1), :]
    solved_ends = jnp.dot(ends_ref[...], inverse_ref[...], precision=HIGH, preferred_element_type=jnp.float32)
    f = lax.broadcasted_iota(jnp.int32, (covered, 1), 0)
    first_row = (f == 0).astype(jnp.float32)
    last_row = (f == covered - 1).astype(jnp.float32)
    long_ref[...] = jnp.zeros_like(long_ref)
    for q in range(narrow):
        low = solved_ends[q : q + 1]
        high = solved_ends[padded + q : padded + q + 1]
        panel = panel_ref[pl.ds(q * all_rows + offset, covered), :]
        mean = own_ref[pl.ds(q * all_rows + offset, covered), :]
        coarse = mean + diffusion * mean[:, total : total + 1] * (first_row * low + last_row * high)
        gap = nudging * (panel - coarse)
        for dy in range(3):
            long_ref[pl.ds(dy, covered, stride=3), :] = gap
        long_ref[0:1, :] = long_ref[0:1, :] + diffusion * low
        long_ref[child_rows - 1 : child_rows, :] = long_ref[child_rows - 1 : child_rows, :] + diffusion * high
        for t in range(lane_tiles):
            turned = long_ref[t * LANES : (t + 1) * LANES, :].T
            for dx in range(3):
                add_ref[pl.ds(t * total * ROWS + 3 * q + dx, total, stride=ROWS), :] = turned[:total]
    column = lax.broadcasted_iota(jnp.int32, (capacity, 1), 0)
    mask = cwet_ref[...].astype(jnp.float32) * (column <= last).astype(jnp.float32)

    def write(l, carry):
        for t in range(lane_tiles):
            stop = min(child_rows, (t + 1) * LANES)
            at = pl.ds(pl.multiple_of((t * total + l) * ROWS, ROWS), capacity)
            lanes = slice(t * LANES, stop)
            size = stop - t * LANES
            cnext_ref[l, :, lanes] = mask[:, lanes] * (cmid_ref[at, :size] + add_ref[at, :size])
        return carry

    lax.fori_loop(0, total, write, 0)

    for j in range(strips):
        wide_ref[pl.ds(pl.multiple_of(starts[j] * rows, rows), narrow * rows), :] = got_ref[j, narrow * rows :, :]
    mean = wide_ref[: width * rows, :]
    twice = jnp.dot(pmid_ref[...], inverse_ref[...], precision=HIGH, preferred_element_type=jnp.float32)
    coarse = mean + diffusion * mean[:, total : total + 1] * twice
    row = member * rows + lax.broadcasted_iota(jnp.int32, (width * rows, 1), 0) % rows
    inside = (row >= offset) & (row < offset + covered)
    turn_ref[: width * rows, :] = pmid_ref[:, total : total + 1] * jnp.where(inside, coarse, pmid_ref[...])
    turn_ref[width * rows :, :] = jnp.zeros((turn_ref.shape[0] - width * rows, LANES), jnp.float32)
    for r in range(rows):
        turned = turn_ref[pl.ds(r, LANES, stride=rows), :].T
        nat_ref[pl.ds(r, LANES, stride=rows), :] = turned
    pnext_ref[...] = nat_ref[: total * rows, :width]


def body(parent_tracer, child_tracer, strip_cols, row_offset, parent_wet, child_wet, vert_mix):
    tracers, levels, rows, width = parent_tracer.shape
    capacity, child_rows = child_wet.shape
    strips = lax.axis_size("child")
    total = tracers * levels
    narrow = capacity // 3
    all_rows = rows * strips
    lane_tiles = (child_rows + LANES - 1) // LANES
    level_rows = (total + 7) // 8 * 8
    message = lane_tiles * level_rows + width
    f32 = lambda *s: jax.ShapeDtypeStruct(s, jnp.float32)
    mem = lambda *s: pltpu.VMEM(s, jnp.float32)
    parent_flat = parent_tracer.reshape(total * rows, width)
    child_flat = child_tracer.reshape(total, capacity, child_rows)

    flat, forth, back, left_edge, right_edge = pl.pallas_call(
        functools.partial(prepare_kernel, strips),
        in_specs=[SM, VM, VM, VM, VM],
        out_specs=[VM] * 5,
        out_shape=[
            f32(width * rows, LANES), f32(message, LANES), f32(message, LANES), f32(rows, LANES), f32(rows, LANES),
        ],
        scratch_shapes=[mem(LANES * rows, LANES)],
        compiler_params=params(24),
        name="prepare",
    )(strip_cols, parent_flat, parent_wet, child_flat, child_wet)

    groups = lax.axis_size("parent")
    devices = groups * strips
    right_edge = lax.ppermute(right_edge, "parent", [(i, i + 1) for i in range(groups - 1)])
    left_edge = lax.ppermute(left_edge, "parent", [(i + 1, i) for i in range(groups - 1)])
    forth = lax.ppermute(forth, ("parent", "child"), [(i, i + 1) for i in range(devices - 1)])
    back = lax.ppermute(back, ("parent", "child"), [(i + 1, i) for i in range(devices - 1)])

    weights, inverse = pl.pallas_call(
        coefficient_kernel,
        in_specs=[SM],
        out_specs=[VM, VM],
        out_shape=[f32(level_rows, LANES), f32(LANES, LANES)],
        scratch_shapes=[mem(8 * levels, LANES), mem(8 * levels, LANES)],
        compiler_params=params(8),
        name="coefficients",
    )(vert_mix)

    send, parent_mid, own, child_mid = pl.pallas_call(
        functools.partial(solve_kernel, strips, rows),
        in_specs=[SM, SM, SM] + [VM] * 9,
        out_specs=[VM] * 4,
        out_shape=[
            f32(strips, 2 * narrow * rows, LANES),
            f32(width * rows, LANES),
            f32(narrow * all_rows, LANES),
            f32(lane_tiles * total * ROWS, LANES),
        ],
        scratch_shapes=[
            mem(width * rows, LANES),
            mem((width + narrow) * rows, LANES),
            mem(LANES, lane_tiles * LANES),
            mem(lane_tiles * LANES, LANES),
            mem(total, capacity, child_rows),
        ],
        compiler_params=params(40),
        name="solve",
    )(
        strip_cols, row_offset, vert_mix, flat, forth, back, right_edge, left_edge,
        weights, inverse, child_flat, child_wet,
    )

    got = lax.all_to_all(send, "child", 0, 0)

    turn_rows = max(width, LANES) * rows
    parent_next, child_next = pl.pallas_call(
        functools.partial(finish_kernel, strips, rows, total),
        in_specs=[SM, SM] + [VM] * 6,
        out_specs=[VM, VM],
        out_shape=[f32(total * rows, width), f32(total, capacity, child_rows)],
        scratch_shapes=[
            mem(narrow * all_rows, LANES),
            mem((width + narrow) * rows, LANES),
            mem(2 * ((narrow + 7) // 8 * 8), LANES),
            mem(lane_tiles * LANES, LANES),
            mem(lane_tiles * total * ROWS, LANES),
            mem(turn_rows, LANES),
            mem(LANES * rows, LANES),
        ],
        compiler_params=params(40),
        name="finish",
    )(strip_cols, row_offset, got, own, parent_mid, inverse, child_mid, child_wet)
    return parent_next.reshape(parent_tracer.shape), child_next.reshape(child_tracer.shape)


def solution(mesh):
    return jax.shard_map(
        body,
        mesh=mesh,
        in_specs=(
            P(None, None, "child", "parent"),
            P(None, None, ("parent", "child"), None),
            P(),
            P(),
            P("child", "parent"),
            P(("parent", "child"), None),
            P(),
        ),
        out_specs=(P(None, None, "child", "parent"), P(None, None, ("parent", "child"), None)),
        check_vma=False,
    )
```

```python
import functools

import jax
import jax.numpy as jnp
from jax import lax
from jax.experimental import pallas as pl
from jax.experimental.pallas import tpu as pltpu
from jax.sharding import PartitionSpec as P

diffusion = 0.2
nudging = 0.5
one_ninth = 1.0 / 9.0
LANES = 128
HIGH = lax.Precision.HIGHEST

VM = pl.BlockSpec(memory_space=pltpu.VMEM)
SM = pl.BlockSpec(memory_space=pltpu.SMEM)


def params(mib):
    return pltpu.CompilerParams(vmem_limit_bytes=mib << 20)


def up(n, m):
    return (n + m - 1) // m * m


def tile_list(child_rows):
    return [(t, min(LANES, child_rows - t * LANES)) for t in range((child_rows + LANES - 1) // LANES)]


def my_cols(cols_ref):
    return cols_ref[lax.axis_index("parent"), lax.axis_index("child")]


def strip_starts(cols_ref, strips):
    group = lax.axis_index("parent")
    start = jnp.int32(0)
    starts = []
    for j in range(strips):
        starts.append(start)
        start = start + cols_ref[group, j]
    return starts


def coefficient_kernel(mix_ref, weight_ref, carry_ref, back_ref, inverse_ref, d_ref, c_ref):
    tracers, levels = mix_ref.shape[0], mix_ref.shape[1] + 1
    slot = LANES // tracers
    lane = lax.broadcasted_iota(jnp.int32, (8, LANES), 1)
    by_lane = lane // slot
    by_row = lax.broadcasted_iota(jnp.int32, (8, LANES), 0) % tracers
    none = jnp.zeros((8, LANES), jnp.float32)

    def mixed(k, which):
        row = none
        if 0 <= k < levels - 1:
            for t in range(tracers):
                row = jnp.where(which == t, mix_ref[t, k], row)
        return row

    weights = [none, none]
    d = none
    for k in range(levels):
        for n, which in enumerate((by_row, by_lane)):
            above, below = mixed(k - 1, which), mixed(k, which)
            w = 1.0 / (1.0 + above + below - above * (above * weights[n]))
            weights[n] = w
            at = pl.ds(8 * k, 8)
            if n == 0:
                weight_ref[at, :] = w
                carry_ref[at, :] = above * w
                back_ref[at, :] = below * w
            else:
                unit = (lane - which * slot == k).astype(jnp.float32)
                d = (unit + above * d) * w
                d_ref[at, :] = d
                c_ref[at, :] = below * w
    inverse_ref[...] = jnp.zeros_like(inverse_ref)
    x = none
    for k in reversed(range(levels)):
        x = d_ref[pl.ds(8 * k, 8), :] + c_ref[pl.ds(8 * k, 8), :] * x
        for t in range(tracers):
            inverse_ref[t * slot + k : t * slot + k + 1, :] = jnp.where(by_lane == t, x, 0.0)[:1]


def prepare_kernel(
    cols_ref, parent_ref, pwet_ref, child_ref, cwet_ref,
    flat_ref, forth_ref, back_ref, left_ref, right_ref, turn_ref, row_ref,
):
    levels, capacity, tracers, child_rows = child_ref.shape
    rows, width = pwet_ref.shape
    slot = LANES // tracers
    level_rows = up(tracers * levels, 8)
    tiles = tile_list(child_rows)
    turn_ref[:rows, :width] = pwet_ref[...].astype(jnp.float32)
    row_ref[...] = jnp.zeros_like(row_ref)
    wet = turn_ref[...].T
    for r in range(rows):
        cell = wet[:width, r : r + 1]
        for t in range(tracers):
            row_ref[r, :, t * slot : t * slot + levels] = cell * parent_ref[t, r]
        row_ref[r, :, levels : levels + 1] = cell
        flat_ref[pl.ds(r, width, stride=rows), :] = row_ref[r]
    left_ref[...] = flat_ref[:rows, :]
    right_ref[...] = flat_ref[(width - 1) * rows :, :]
    flat_child = child_ref.reshape(levels * capacity * tracers, child_rows)
    last = 3 * my_cols(cols_ref) - 1
    base = len(tiles) * level_rows
    for ref, x, r in ((forth_ref, last, rows - 1), (back_ref, 0, 0)):
        cell = cwet_ref[pl.ds(x, 1), :].astype(jnp.float32)
        for l in range(levels):
            pair = flat_child[pl.ds(pl.multiple_of((l * capacity + x) * tracers, tracers), tracers), :] * cell
            for n, size in tiles:
                at = n * level_rows + l * tracers
                ref[at : at + tracers, :size] = pair[:, n * LANES : n * LANES + size]
        ref[base : base + width, :] = row_ref[r]


def masks(cols_ref, cwet_ref, mask_ref, tracers):
    capacity, child_rows = cwet_ref.shape
    column = lax.broadcasted_iota(jnp.int32, (capacity, 1), 0)
    mask = cwet_ref[...].astype(jnp.float32) * (column < 3 * my_cols(cols_ref)).astype(jnp.float32)
    mask_ref[...] = jnp.zeros_like(mask_ref)
    for n, size in tile_list(child_rows):
        part = mask[:, n * LANES : n * LANES + size]
        if size < LANES:
            part = jnp.concatenate([part, jnp.zeros((capacity, LANES - size), jnp.float32)], axis=1)
        for t in range(tracers):
            mask_ref[n, pl.ds(t, capacity, stride=tracers), :] = part
    return mask


def solve_kernel(
    strips, rows,
    cols_ref, offset_ref, flat_ref, before_ref, after_ref, left_ref, right_ref,
    weight_ref, carry_ref, back_ref, inverse_ref, child_ref, cwet_ref,
    send_ref, pmid_ref, own_ref, cmid_ref,
    explicit_ref, wide_ref, mask_ref, begin_ref, d_ref, turn_ref, end_ref, long_ref,
):
    levels, capacity, tracers, child_rows = child_ref.shape
    slot = LANES // tracers
    width = flat_ref.shape[0] // rows
    narrow = capacity // 3
    covered = child_rows // 3
    all_rows = strips * rows
    tiles = tile_list(child_rows)
    level_rows = up(tracers * levels, 8)
    base = len(tiles) * level_rows
    live = capacity * tracers
    stored = up(live, 8)
    stride = begin_ref.shape[1] // levels
    member = lax.axis_index("child")
    starts = strip_starts(cols_ref, strips)
    offset = offset_ref[0]

    has_before = (member > 0).astype(jnp.float32)
    has_after = (member < strips - 1).astype(jnp.float32)
    for x in range(width):
        here = flat_ref[x * rows : (x + 1) * rows, :]
        west = left_ref[...] if x == 0 else flat_ref[(x - 1) * rows : x * rows, :]
        east = right_ref[...] if x == width - 1 else flat_ref[(x + 1) * rows : (x + 2) * rows, :]
        south = jnp.concatenate([has_before * before_ref[base + x : base + x + 1, :], here[:-1]], axis=0)
        north = jnp.concatenate([here[1:], has_after * after_ref[base + x : base + x + 1, :]], axis=0)
        wet = here[:, levels : levels + 1]
        laplace = north + south + east + west - 4.0 * here
        explicit_ref[x * rows : (x + 1) * rows, :] = wet * (here + diffusion * laplace)
    solved = jnp.dot(explicit_ref[...], inverse_ref[...], precision=HIGH, preferred_element_type=jnp.float32)
    lane = lax.broadcasted_iota(jnp.int32, (width * rows, LANES), 1)
    solved = jnp.where(lane == levels, flat_ref[...], solved)
    wide_ref[: width * rows, :] = solved
    wide_ref[width * rows :, :] = jnp.zeros((narrow * rows, LANES), jnp.float32)
    pmid_ref[...] = solved
    for j in range(strips):
        send_ref[j, : narrow * rows, :] = wide_ref[pl.ds(pl.multiple_of(starts[j] * rows, rows), narrow * rows), :]

    mask = masks(cols_ref, cwet_ref, mask_ref, tracers)
    flat_child = child_ref.reshape(levels * live, child_rows)
    lane = lax.broadcasted_iota(jnp.int32, (stored, LANES), 1)
    past = 8 + 3 * tracers * my_cols(cols_ref)
    for n, size in tiles:
        if size < LANES:
            begin_ref[n] = jnp.zeros((levels * stride, LANES), jnp.float32)

    def begin(l, carry):
        cells = flat_child[pl.ds(pl.multiple_of(l * live, 2), live), :]
        start = pl.multiple_of(l * stride, 8)
        for n, size in tiles:
            part = cells[:, n * LANES : n * LANES + size] * mask_ref[n, :live, :size]
            begin_ref[n, pl.ds(start + 8, live), :size] = part
            edge = pl.ds(n * level_rows + l * tracers, tracers)
            begin_ref[n, pl.ds(start + 8 - tracers, tracers), :size] = before_ref[edge, :size]
            begin_ref[n, pl.ds(start + past, tracers), :size] = after_ref[edge, :size]
        return carry

    lax.fori_loop(0, levels, begin, 0, unroll=2)

    def by_rows(factor, value):
        return (factor[None] * value.reshape(stored // 8, 8, LANES)).reshape(stored, LANES)

    def forward(l, carry):
        start = pl.multiple_of(l * stride, 8)
        coef = pl.ds(pl.multiple_of(l * 8, 8), 8)
        cells = [begin_ref[n, pl.ds(start + 8, stored), :] for n, _ in tiles]
        lower = [pltpu.roll(c, 1, 1) for c in cells]
        upper = [pltpu.roll(c, LANES - 1, 1) for c in cells]
        held = []
        for n, size in tiles:
            south = jnp.where(lane == 0, lower[n - 1] if n else 0.0, lower[n])
            if n + 1 < len(tiles):
                north = jnp.where(lane == LANES - 1, upper[n + 1], upper[n])
            else:
                north = jnp.where(lane == size - 1, 0.0, upper[n])
            west = begin_ref[n, pl.ds(start + 8 - tracers, stored), :]
            east = begin_ref[n, pl.ds(start + 8 + tracers, stored), :]
            explicit = (diffusion * mask_ref[n]) * (cells[n] + west + east + south + north)
            d = by_rows(weight_ref[coef, :], explicit) + by_rows(carry_ref[coef, :], carry[n])
            d_ref[n, pl.ds(pl.multiple_of(l * stored, 8), stored), :] = d
            held.append(d)
        return tuple(held)

    blank = jnp.zeros((stored, LANES), jnp.float32)
    lax.fori_loop(0, levels, forward, (blank,) * len(tiles), unroll=2)

    def backward(step, carry):
        l = levels - 1 - step
        coef = pl.ds(pl.multiple_of(l * 8, 8), 8)
        at = pl.ds(pl.multiple_of(l * stored, 8), stored)
        held = []
        for n, _ in tiles:
            x = d_ref[n, at, :] + by_rows(back_ref[coef, :], carry[n])
            cmid_ref[n, at, :] = x
            held.append(x)
        return tuple(held)

    lax.fori_loop(0, levels, backward, (blank,) * len(tiles), unroll=2)

    own_ref[...] = jnp.zeros_like(own_ref)
    turn_ref[...] = jnp.zeros_like(turn_ref)
    end_ref[...] = jnp.zeros_like(end_ref)
    y = lax.broadcasted_iota(jnp.int32, (1, child_rows), 1)
    at_end = ((y == 0) | (y == child_rows - 1)).astype(jnp.float32)
    tail, tail_size = tiles[-1]
    packs = LANES // tail_size
    for q in range(narrow):
        count = (mask[3 * q : 3 * q + 1] + mask[3 * q + 1 : 3 * q + 2] + mask[3 * q + 2 : 3 * q + 3]) * at_end
        for n, size in tiles:
            into, low = (turn_ref, 0) if n < tail else (end_ref.at[q // packs], (q % packs) * size)
            for t in range(tracers):
                part = sum(
                    cmid_ref[n, pl.ds((3 * q + dx) * tracers + t, levels, stride=stored), :] for dx in range(3)
                )
                into[t * slot : t * slot + levels, low : low + size] = part[:, :size]
            into[levels : levels + 1, low : low + size] = count[:, n * LANES : n * LANES + size]
            if n < tail:
                long_ref[q * child_rows + n * LANES : q * child_rows + n * LANES + size, :] = turn_ref[...].T
    for part in range((narrow + packs - 1) // packs):
        turned = end_ref[part].T
        for q in range(part * packs, min(narrow, (part + 1) * packs)):
            low = (q % packs) * tail_size
            high = (q + 1) * child_rows
            long_ref[high - tail_size : high, :] = turned[low : low + tail_size]
    for q in range(narrow):
        mean = one_ninth * (
            long_ref[pl.ds(q * child_rows, covered, stride=3), :]
            + long_ref[pl.ds(q * child_rows + 1, covered, stride=3), :]
            + long_ref[pl.ds(q * child_rows + 2, covered, stride=3), :]
        )
        own_ref[pl.ds(q * all_rows + offset, covered), :] = mean
    for k in range(strips):
        for q in range(narrow):
            send_ref[k, (narrow + q) * rows : (narrow + q + 1) * rows, :] = own_ref[
                q * all_rows + k * rows : q * all_rows + (k + 1) * rows, :
            ]


def finish_kernel(
    strips, rows,
    cols_ref, offset_ref, got_ref, own_ref, pmid_ref, inverse_ref, cmid_ref, cwet_ref,
    pnext_ref, cnext_ref,
    panel_ref, wide_ref, ends_ref, long_ref, end_ref, add_ref, mask_ref, next_ref,
):
    levels, capacity, tracers, child_rows = cnext_ref.shape
    slot = LANES // tracers
    width = pmid_ref.shape[0] // rows
    narrow = capacity // 3
    covered = child_rows // 3
    all_rows = strips * rows
    tiles = tile_list(child_rows)
    live = capacity * tracers
    stored = up(live, 8)
    padded = up(narrow, 8)
    member = lax.axis_index("child")
    starts = strip_starts(cols_ref, strips)
    offset = offset_ref[0]
    masks(cols_ref, cwet_ref, mask_ref, tracers)

    ends_ref[...] = jnp.zeros_like(ends_ref)
    for q in range(narrow):
        for k in range(strips):
            panel_ref[q * all_rows + k * rows : q * all_rows + (k + 1) * rows, :] = got_ref[
                k, q * rows : (q + 1) * rows, :
            ]
        ends_ref[q : q + 1, :] = panel_ref[pl.ds(q * all_rows + offset, 1), :]
        ends_ref[padded + q : padded + q + 1, :] = panel_ref[pl.ds(q * all_rows + offset + covered - 1, 1), :]
    solved_ends = jnp.dot(ends_ref[...], inverse_ref[...], precision=HIGH, preferred_element_type=jnp.float32)
    f = lax.broadcasted_iota(jnp.int32, (covered, 1), 0)
    first_row = (f == 0).astype(jnp.float32)
    last_row = (f == covered - 1).astype(jnp.float32)
    tail, tail_size = tiles[-1]
    packs = LANES // tail_size

    def spread(turned, n, q):
        for t in range(tracers):
            part = turned[t * slot : t * slot + levels]
            for dx in range(3):
                add_ref[n, pl.ds((3 * q + dx) * tracers + t, levels, stride=stored), :] = part

    for q in range(narrow):
        low = solved_ends[q : q + 1]
        high = solved_ends[padded + q : padded + q + 1]
        panel = panel_ref[pl.ds(q * all_rows + offset, covered), :]
        mean = own_ref[pl.ds(q * all_rows + offset, covered), :]
        coarse = mean + diffusion * mean[:, levels : levels + 1] * (first_row * low + last_row * high)
        gap = nudging * (panel - coarse)
        base = q * child_rows
        for dy in range(3):
            long_ref[pl.ds(base + dy, covered, stride=3), :] = gap
        long_ref[base : base + 1, :] = gap[:1] + diffusion * low
        long_ref[base + child_rows - 1 : base + child_rows, :] = gap[covered - 1 :] + diffusion * high
        for n, size in tiles[:-1]:
            spread(long_ref[base + n * LANES : base + n * LANES + size, :].T, n, q)
        at = (q % packs) * tail_size
        end_ref[q // packs, at : at + tail_size, :] = long_ref[base + child_rows - tail_size : base + child_rows, :]
    for part in range((narrow + packs - 1) // packs):
        turned = end_ref[part].T
        for q in range(part * packs, min(narrow, (part + 1) * packs)):
            shift = (q % packs) * tail_size
            spread(pltpu.roll(turned, (LANES - shift) % LANES, 1) if shift else turned, tail, q)

    flat_next = cnext_ref.reshape(levels * live, child_rows)

    def write(l, carry):
        at = pl.ds(pl.multiple_of(l * stored, 8), live)
        parts = [
            (mask_ref[n, :live, :] * (cmid_ref[n, at, :] + add_ref[n, at, :]))[:, :size] for n, size in tiles
        ]
        flat_next[pl.ds(pl.multiple_of(l * live, 2), live), :] = jnp.concatenate(parts, axis=1)
        return carry

    lax.fori_loop(0, levels, write, 0, unroll=2)

    for j in range(strips):
        wide_ref[pl.ds(pl.multiple_of(starts[j] * rows, rows), narrow * rows), :] = got_ref[j, narrow * rows :, :]
    mean = wide_ref[: width * rows, :]
    pmid = pmid_ref[...]
    twice = jnp.dot(pmid, inverse_ref[...], precision=HIGH, preferred_element_type=jnp.float32)
    coarse = mean + diffusion * mean[:, levels : levels + 1] * twice
    row = member * rows + lax.broadcasted_iota(jnp.int32, (width * rows, 1), 0) % rows
    inside = (row >= offset) & (row < offset + covered)
    next_ref[...] = pmid[:, levels : levels + 1] * jnp.where(inside, coarse, pmid)
    for r in range(rows):
        block = next_ref[pl.ds(r, width, stride=rows), :]
        for t in range(tracers):
            pnext_ref[t, r] = block[:, t * slot : t * slot + levels]


def body(parent_tracer, child_tracer, strip_cols, row_offset, parent_wet, child_wet, vert_mix):
    tracers, levels, rows, width = parent_tracer.shape
    capacity, child_rows = child_wet.shape
    strips = lax.axis_size("child")
    narrow = capacity // 3
    all_rows = rows * strips
    tiles = tile_list(child_rows)
    lane_tiles = len(tiles)
    packed = -(-narrow // (LANES // tiles[-1][1]))
    stored = up(capacity * tracers, 8)
    stride = stored + 16
    message = lane_tiles * up(tracers * levels, 8) + width
    f32 = lambda *s: jax.ShapeDtypeStruct(s, jnp.float32)
    mem = lambda *s: pltpu.VMEM(s, jnp.float32)
    parent = jnp.transpose(parent_tracer, (0, 2, 3, 1))
    child = jnp.transpose(child_tracer, (1, 2, 0, 3))

    flat, forth, back, left_edge, right_edge = pl.pallas_call(
        prepare_kernel,
        in_specs=[SM, VM, VM, VM, VM],
        out_specs=[VM] * 5,
        out_shape=[
            f32(width * rows, LANES), f32(message, LANES), f32(message, LANES), f32(rows, LANES), f32(rows, LANES),
        ],
        scratch_shapes=[mem(LANES, LANES), mem(rows, width, LANES)],
        compiler_params=params(16),
        name="prepare",
    )(strip_cols, parent, parent_wet, child, child_wet)

    groups = lax.axis_size("parent")
    devices = groups * strips
    right_edge = lax.ppermute(right_edge, "parent", [(i, i + 1) for i in range(groups - 1)])
    left_edge = lax.ppermute(left_edge, "parent", [(i + 1, i) for i in range(groups - 1)])
    forth = lax.ppermute(forth, ("parent", "child"), [(i, i + 1) for i in range(devices - 1)])
    back = lax.ppermute(back, ("parent", "child"), [(i + 1, i) for i in range(devices - 1)])

    weight, carry, below, inverse = pl.pallas_call(
        coefficient_kernel,
        in_specs=[SM],
        out_specs=[VM] * 4,
        out_shape=[f32(8 * levels, LANES)] * 3 + [f32(LANES, LANES)],
        scratch_shapes=[mem(8 * levels, LANES), mem(8 * levels, LANES)],
        compiler_params=params(8),
        name="coefficients",
    )(vert_mix)

    send, parent_mid, own, child_mid = pl.pallas_call(
        functools.partial(solve_kernel, strips, rows),
        in_specs=[SM, SM] + [VM] * 11,
        out_specs=[VM] * 4,
        out_shape=[
            f32(strips, 2 * narrow * rows, LANES),
            f32(width * rows, LANES),
            f32(narrow * all_rows, LANES),
            f32(lane_tiles, levels * stored, LANES),
        ],
        scratch_shapes=[
            mem(width * rows, LANES),
            mem((width + narrow) * rows, LANES),
            mem(lane_tiles, stored, LANES),
            mem(lane_tiles, levels * stride, LANES),
            mem(lane_tiles, levels * stored, LANES),
            mem(LANES, LANES),
            mem(packed, LANES, LANES),
            mem(narrow * child_rows, LANES),
        ],
        compiler_params=params(32),
        name="solve",
    )(
        strip_cols, row_offset, flat, forth, back, right_edge, left_edge,
        weight, carry, below, inverse, child, child_wet,
    )

    got = lax.all_to_all(send, "child", 0, 0)

    parent_next, child_next = pl.pallas_call(
        functools.partial(finish_kernel, strips, rows),
        in_specs=[SM, SM] + [VM] * 6,
        out_specs=[VM, VM],
        out_shape=[f32(*parent.shape), f32(*child.shape)],
        scratch_shapes=[
            mem(narrow * all_rows, LANES),
            mem((width + narrow) * rows, LANES),
            mem(2 * up(narrow, 8), LANES),
            mem(narrow * child_rows, LANES),
            mem(packed, LANES, LANES),
            mem(lane_tiles, levels * stored, LANES),
            mem(lane_tiles, stored, LANES),
            mem(width * rows, LANES),
        ],
        compiler_params=params(32),
        name="finish",
    )(strip_cols, row_offset, got, own, parent_mid, inverse, child_mid, child_wet)
    return jnp.transpose(parent_next, (0, 3, 1, 2)), jnp.transpose(child_next, (2, 0, 1, 3))


def solution(mesh):
    return jax.shard_map(
        body,
        mesh=mesh,
        in_specs=(
            P(None, None, "child", "parent"),
            P(None, None, ("parent", "child"), None),
            P(),
            P(),
            P("child", "parent"),
            P(("parent", "child"), None),
            P(),
        ),
        out_specs=(P(None, None, "child", "parent"), P(None, None, ("parent", "child"), None)),
        check_vma=False,
    )
```

```python
import functools

import jax
import jax.numpy as jnp
from jax import lax
from jax.experimental import pallas as pl
from jax.experimental.pallas import tpu as pltpu
from jax.sharding import PartitionSpec as P

diffusion = 0.2
nudging = 0.5
one_ninth = 1.0 / 9.0
LANES = 128
HIGH = lax.Precision.HIGHEST

VM = pl.BlockSpec(memory_space=pltpu.VMEM)
SM = pl.BlockSpec(memory_space=pltpu.SMEM)
HBM = pl.BlockSpec(memory_space=pltpu.HBM)


def params(mib):
    return pltpu.CompilerParams(vmem_limit_bytes=mib << 20)


def in_hbm(x):
    return pltpu.with_memory_space_constraint(x, pltpu.HBM)


def up(n, m):
    return (n + m - 1) // m * m


def tile_list(child_rows):
    return [(t, min(LANES, child_rows - t * LANES)) for t in range((child_rows + LANES - 1) // LANES)]


def my_cols(cols_ref):
    return cols_ref[lax.axis_index("parent"), lax.axis_index("child")]


def strip_starts(cols_ref, strips):
    group = lax.axis_index("parent")
    start = jnp.int32(0)
    starts = []
    for j in range(strips):
        starts.append(start)
        start = start + cols_ref[group, j]
    return starts


def coefficient_kernel(mix_ref, weight_ref, carry_ref, back_ref, inverse_ref, d_ref, c_ref):
    tracers, levels = mix_ref.shape[0], mix_ref.shape[1] + 1
    slot = LANES // tracers
    lane = lax.broadcasted_iota(jnp.int32, (8, LANES), 1)
    by_lane = lane // slot
    by_row = lax.broadcasted_iota(jnp.int32, (8, LANES), 0) % tracers
    none = jnp.zeros((8, LANES), jnp.float32)

    def mixed(k, which):
        row = none
        if 0 <= k < levels - 1:
            for t in range(tracers):
                row = jnp.where(which == t, mix_ref[t, k], row)
        return row

    weights = [none, none]
    d = none
    for k in range(levels):
        for n, which in enumerate((by_row, by_lane)):
            above, below = mixed(k - 1, which), mixed(k, which)
            w = 1.0 / (1.0 + above + below - above * (above * weights[n]))
            weights[n] = w
            at = pl.ds(8 * k, 8)
            if n == 0:
                weight_ref[at, :] = w
                carry_ref[at, :] = above * w
                back_ref[at, :] = below * w
            else:
                unit = (lane - which * slot == k).astype(jnp.float32)
                d = (unit + above * d) * w
                d_ref[at, :] = d
                c_ref[at, :] = below * w
    inverse_ref[...] = jnp.zeros_like(inverse_ref)
    x = none
    for k in reversed(range(levels)):
        x = d_ref[pl.ds(8 * k, 8), :] + c_ref[pl.ds(8 * k, 8), :] * x
        for t in range(tracers):
            inverse_ref[t * slot + k : t * slot + k + 1, :] = jnp.where(by_lane == t, x, 0.0)[:1]


def prepare_kernel(
    cols_hbm, parent_hbm, pwet_hbm, child_hbm, cwet_hbm,
    flat_ref, forth_ref, back_ref, left_ref, right_ref,
    cols_ref, parent_ref, pwet_ref, cwet_ref, edge_ref, turn_ref, row_ref, sems,
):
    levels, capacity, tracers, child_rows = child_hbm.shape
    rows, width = pwet_ref.shape
    slot = LANES // tracers
    level_rows = up(tracers * levels, 8)
    tiles = tile_list(child_rows)
    fetch_cols = pltpu.make_async_copy(cols_hbm, cols_ref, sems.at[0])
    fetch_pwet = pltpu.make_async_copy(pwet_hbm, pwet_ref, sems.at[1])
    fetch_parent = pltpu.make_async_copy(parent_hbm, parent_ref, sems.at[2])
    fetch_cwet = pltpu.make_async_copy(cwet_hbm, cwet_ref, sems.at[3])
    fetch_first = pltpu.make_async_copy(child_hbm.at[:, pl.ds(0, 1)], edge_ref.at[1], sems.at[4])
    for fetch in (fetch_cols, fetch_pwet, fetch_parent, fetch_first, fetch_cwet):
        fetch.start()
    fetch_cols.wait()
    last = 3 * my_cols(cols_ref) - 1
    fetch_last = pltpu.make_async_copy(child_hbm.at[:, pl.ds(last, 1)], edge_ref.at[0], sems.at[5])
    fetch_last.start()
    row_ref[...] = jnp.zeros_like(row_ref)
    fetch_pwet.wait()
    turn_ref[:rows, :width] = pwet_ref[...].astype(jnp.float32)
    wet = turn_ref[...].T
    fetch_parent.wait()
    for r in range(rows):
        cell = wet[:width, r : r + 1]
        for t in range(tracers):
            row_ref[r, :, t * slot : t * slot + levels] = cell * parent_ref[t, r]
        row_ref[r, :, levels : levels + 1] = cell
        flat_ref[pl.ds(r, width, stride=rows), :] = row_ref[r]
    left_ref[...] = flat_ref[:rows, :]
    right_ref[...] = flat_ref[(width - 1) * rows :, :]
    fetch_cwet.wait()
    base = len(tiles) * level_rows
    fetch_first.wait()
    fetch_last.wait()
    for side, (ref, x, r) in enumerate(((forth_ref, last, rows - 1), (back_ref, 0, 0))):
        cell = cwet_ref[pl.ds(x, 1), :].astype(jnp.float32)
        pairs = edge_ref.at[side].reshape(levels * tracers, child_rows)[...] * cell
        for n, size in tiles:
            ref[n * level_rows : n * level_rows + levels * tracers, :size] = pairs[:, n * LANES : n * LANES + size]
        ref[base : base + width, :] = row_ref[r]


def masks(cols_ref, cwet_ref, mask_ref, tracers):
    capacity, child_rows = cwet_ref.shape
    column = lax.broadcasted_iota(jnp.int32, (capacity, 1), 0)
    mask = cwet_ref[...].astype(jnp.float32) * (column < 3 * my_cols(cols_ref)).astype(jnp.float32)
    mask_ref[...] = jnp.zeros_like(mask_ref)
    for n, size in tile_list(child_rows):
        part = mask[:, n * LANES : n * LANES + size]
        if size < LANES:
            part = jnp.concatenate([part, jnp.zeros((capacity, LANES - size), jnp.float32)], axis=1)
        for t in range(tracers):
            mask_ref[n, pl.ds(t, capacity, stride=tracers), :] = part
    return mask


def solve_kernel(
    groups, strips, rows,
    cols_ref, offset_ref, flat_ref, before_ref, after_ref, left_ref, right_ref,
    weight_ref, carry_ref, back_ref, inverse_ref, child_hbm, cwet_ref,
    send_ref, pmid_ref, own_ref, cmid_ref,
    explicit_ref, wide_ref, mask_ref, begin_ref, d_ref, turn_ref, end_ref, long_ref, child_ref, sems,
):
    levels, capacity, tracers, child_rows = child_ref.shape
    chunks = sems.shape[0]
    step = -(-levels // chunks)
    fetches = []
    for c in range(chunks):
        part = pl.ds(c * step, min(levels, (c + 1) * step) - c * step)
        fetches.append(pltpu.make_async_copy(child_hbm.at[part], child_ref.at[part], sems.at[c]))
        fetches[-1].start()
    slot = LANES // tracers
    width = flat_ref.shape[0] // rows
    narrow = capacity // 3
    covered = child_rows // 3
    all_rows = strips * rows
    tiles = tile_list(child_rows)
    level_rows = up(tracers * levels, 8)
    base = len(tiles) * level_rows
    live = capacity * tracers
    stored = up(live, 8)
    stride = begin_ref.shape[1] // levels
    member = lax.axis_index("child")
    starts = strip_starts(cols_ref, strips)
    offset = offset_ref[0]

    group = lax.axis_index("parent")
    has_before = (member > 0).astype(jnp.float32)
    has_after = (member < strips - 1).astype(jnp.float32)
    has_left = (group > 0).astype(jnp.float32)
    has_right = (group < groups - 1).astype(jnp.float32)
    chain_before = jnp.maximum(has_before, has_left)
    chain_after = jnp.maximum(has_after, has_right)
    for x in range(width):
        here = flat_ref[x * rows : (x + 1) * rows, :]
        west = has_left * left_ref[...] if x == 0 else flat_ref[(x - 1) * rows : x * rows, :]
        east = has_right * right_ref[...] if x == width - 1 else flat_ref[(x + 1) * rows : (x + 2) * rows, :]
        south = jnp.concatenate([has_before * before_ref[base + x : base + x + 1, :], here[:-1]], axis=0)
        north = jnp.concatenate([here[1:], has_after * after_ref[base + x : base + x + 1, :]], axis=0)
        wet = here[:, levels : levels + 1]
        laplace = north + south + east + west - 4.0 * here
        explicit_ref[x * rows : (x + 1) * rows, :] = wet * (here + diffusion * laplace)
    solved = jnp.dot(explicit_ref[...], inverse_ref[...], precision=HIGH, preferred_element_type=jnp.float32)
    lane = lax.broadcasted_iota(jnp.int32, (width * rows, LANES), 1)
    solved = jnp.where(lane == levels, flat_ref[...], solved)
    wide_ref[: width * rows, :] = solved
    wide_ref[width * rows :, :] = jnp.zeros((narrow * rows, LANES), jnp.float32)
    pmid_ref[...] = solved
    for j in range(strips):
        send_ref[j, : narrow * rows, :] = wide_ref[pl.ds(pl.multiple_of(starts[j] * rows, rows), narrow * rows), :]

    mask = masks(cols_ref, cwet_ref, mask_ref, tracers)
    flat_child = child_ref.reshape(levels * live, child_rows)
    lane = lax.broadcasted_iota(jnp.int32, (stored, LANES), 1)
    past = 8 + 3 * tracers * my_cols(cols_ref)
    for n, size in tiles:
        if size < LANES:
            begin_ref[n] = jnp.zeros((levels * stride, LANES), jnp.float32)

    def begin(l, carry):
        cells = flat_child[pl.ds(pl.multiple_of(l * live, 2), live), :]
        start = pl.multiple_of(l * stride, 8)
        for n, size in tiles:
            part = cells[:, n * LANES : n * LANES + size] * mask_ref[n, :live, :size]
            begin_ref[n, pl.ds(start + 8, live), :size] = part
            edge = pl.ds(n * level_rows + l * tracers, tracers)
            begin_ref[n, pl.ds(start + 8 - tracers, tracers), :size] = chain_before * before_ref[edge, :size]
            begin_ref[n, pl.ds(start + past, tracers), :size] = chain_after * after_ref[edge, :size]
        return carry

    for c in range(chunks):
        fetches[c].wait()
        lax.fori_loop(c * step, min(levels, (c + 1) * step), begin, 0, unroll=2)

    def by_rows(factor, value):
        return (factor[None] * value.reshape(stored // 8, 8, LANES)).reshape(stored, LANES)

    def forward(l, carry):
        start = pl.multiple_of(l * stride, 8)
        coef = pl.ds(pl.multiple_of(l * 8, 8), 8)
        cells = [begin_ref[n, pl.ds(start + 8, stored), :] for n, _ in tiles]
        lower = [pltpu.roll(c, 1, 1) for c in cells]
        upper = [pltpu.roll(c, LANES - 1, 1) for c in cells]
        held = []
        for n, size in tiles:
            south = jnp.where(lane == 0, lower[n - 1] if n else 0.0, lower[n])
            if n + 1 < len(tiles):
                north = jnp.where(lane == LANES - 1, upper[n + 1], upper[n])
            else:
                north = jnp.where(lane == size - 1, 0.0, upper[n])
            west = begin_ref[n, pl.ds(start + 8 - tracers, stored), :]
            east = begin_ref[n, pl.ds(start + 8 + tracers, stored), :]
            explicit = (diffusion * mask_ref[n]) * (cells[n] + west + east + south + north)
            d = by_rows(weight_ref[coef, :], explicit) + by_rows(carry_ref[coef, :], carry[n])
            d_ref[n, pl.ds(pl.multiple_of(l * stored, 8), stored), :] = d
            held.append(d)
        return tuple(held)

    blank = jnp.zeros((stored, LANES), jnp.float32)
    lax.fori_loop(0, levels, forward, (blank,) * len(tiles), unroll=2)

    def backward(step, carry):
        l = levels - 1 - step
        coef = pl.ds(pl.multiple_of(l * 8, 8), 8)
        at = pl.ds(pl.multiple_of(l * stored, 8), stored)
        held = []
        for n, _ in tiles:
            x = d_ref[n, at, :] + by_rows(back_ref[coef, :], carry[n])
            cmid_ref[n, at, :] = x
            held.append(x)
        return tuple(held)

    lax.fori_loop(0, levels, backward, (blank,) * len(tiles), unroll=2)

    own_ref[...] = jnp.zeros_like(own_ref)
    turn_ref[...] = jnp.zeros_like(turn_ref)
    end_ref[...] = jnp.zeros_like(end_ref)
    y = lax.broadcasted_iota(jnp.int32, (1, child_rows), 1)
    at_end = ((y == 0) | (y == child_rows - 1)).astype(jnp.float32)
    tail, tail_size = tiles[-1]
    packs = LANES // tail_size
    for q in range(narrow):
        count = (mask[3 * q : 3 * q + 1] + mask[3 * q + 1 : 3 * q + 2] + mask[3 * q + 2 : 3 * q + 3]) * at_end
        for n, size in tiles:
            into, low = (turn_ref, 0) if n < tail else (end_ref.at[q // packs], (q % packs) * size)
            for t in range(tracers):
                part = sum(
                    cmid_ref[n, pl.ds((3 * q + dx) * tracers + t, levels, stride=stored), :] for dx in range(3)
                )
                into[t * slot : t * slot + levels, low : low + size] = part[:, :size]
            into[levels : levels + 1, low : low + size] = count[:, n * LANES : n * LANES + size]
            if n < tail:
                long_ref[q * child_rows + n * LANES : q * child_rows + n * LANES + size, :] = turn_ref[...].T
    for part in range((narrow + packs - 1) // packs):
        turned = end_ref[part].T
        for q in range(part * packs, min(narrow, (part + 1) * packs)):
            low = (q % packs) * tail_size
            high = (q + 1) * child_rows
            long_ref[high - tail_size : high, :] = turned[low : low + tail_size]
    for q in range(narrow):
        mean = one_ninth * (
            long_ref[pl.ds(q * child_rows, covered, stride=3), :]
            + long_ref[pl.ds(q * child_rows + 1, covered, stride=3), :]
            + long_ref[pl.ds(q * child_rows + 2, covered, stride=3), :]
        )
        own_ref[pl.ds(q * all_rows + offset, covered), :] = mean
    for k in range(strips):
        for q in range(narrow):
            send_ref[k, (narrow + q) * rows : (narrow + q + 1) * rows, :] = own_ref[
                q * all_rows + k * rows : q * all_rows + (k + 1) * rows, :
            ]


def finish_kernel(
    strips, rows, chunks,
    cols_ref, offset_ref, got_ref, own_ref, pmid_ref, inverse_ref, cmid_ref, cwet_ref,
    pnext_hbm, cnext_hbm,
    panel_ref, wide_ref, ends_ref, long_ref, end_ref, add_ref, mask_ref, next_ref, pkeep_ref, ckeep_ref, sems,
):
    levels, capacity, tracers, child_rows = cnext_hbm.shape
    slot = LANES // tracers
    width = pmid_ref.shape[0] // rows
    narrow = capacity // 3
    covered = child_rows // 3
    all_rows = strips * rows
    tiles = tile_list(child_rows)
    live = capacity * tracers
    stored = up(live, 8)
    padded = up(narrow, 8)
    member = lax.axis_index("child")
    starts = strip_starts(cols_ref, strips)
    offset = offset_ref[0]
    masks(cols_ref, cwet_ref, mask_ref, tracers)

    for j in range(strips):
        wide_ref[pl.ds(pl.multiple_of(starts[j] * rows, rows), narrow * rows), :] = got_ref[j, narrow * rows :, :]
    mean = wide_ref[: width * rows, :]
    pmid = pmid_ref[...]
    twice = jnp.dot(pmid, inverse_ref[...], precision=HIGH, preferred_element_type=jnp.float32)
    coarse = mean + diffusion * mean[:, levels : levels + 1] * twice
    row = member * rows + lax.broadcasted_iota(jnp.int32, (width * rows, 1), 0) % rows
    inside = (row >= offset) & (row < offset + covered)
    next_ref[...] = pmid[:, levels : levels + 1] * jnp.where(inside, coarse, pmid)
    for r in range(rows):
        block = next_ref[pl.ds(r, width, stride=rows), :]
        for t in range(tracers):
            pkeep_ref[t, r] = block[:, t * slot : t * slot + levels]
    send_parent = pltpu.make_async_copy(pkeep_ref, pnext_hbm, sems.at[0])
    send_parent.start()

    ends_ref[...] = jnp.zeros_like(ends_ref)
    for q in range(narrow):
        for k in range(strips):
            panel_ref[q * all_rows + k * rows : q * all_rows + (k + 1) * rows, :] = got_ref[
                k, q * rows : (q + 1) * rows, :
            ]
        ends_ref[q : q + 1, :] = panel_ref[pl.ds(q * all_rows + offset, 1), :]
        ends_ref[padded + q : padded + q + 1, :] = panel_ref[pl.ds(q * all_rows + offset + covered - 1, 1), :]
    solved_ends = jnp.dot(ends_ref[...], inverse_ref[...], precision=HIGH, preferred_element_type=jnp.float32)
    f = lax.broadcasted_iota(jnp.int32, (covered, 1), 0)
    first_row = (f == 0).astype(jnp.float32)
    last_row = (f == covered - 1).astype(jnp.float32)
    tail, tail_size = tiles[-1]
    packs = LANES // tail_size

    def spread(turned, n, q):
        for t in range(tracers):
            part = turned[t * slot : t * slot + levels]
            for dx in range(3):
                add_ref[n, pl.ds((3 * q + dx) * tracers + t, levels, stride=stored), :] = part

    for q in range(narrow):
        low = solved_ends[q : q + 1]
        high = solved_ends[padded + q : padded + q + 1]
        panel = panel_ref[pl.ds(q * all_rows + offset, covered), :]
        mean = own_ref[pl.ds(q * all_rows + offset, covered), :]
        coarse = mean + diffusion * mean[:, levels : levels + 1] * (first_row * low + last_row * high)
        gap = nudging * (panel - coarse)
        base = q * child_rows
        for dy in range(3):
            long_ref[pl.ds(base + dy, covered, stride=3), :] = gap
        long_ref[base : base + 1, :] = gap[:1] + diffusion * low
        long_ref[base + child_rows - 1 : base + child_rows, :] = gap[covered - 1 :] + diffusion * high
        for n, size in tiles[:-1]:
            spread(long_ref[base + n * LANES : base + n * LANES + size, :].T, n, q)
        at = (q % packs) * tail_size
        end_ref[q // packs, at : at + tail_size, :] = long_ref[base + child_rows - tail_size : base + child_rows, :]
    for part in range((narrow + packs - 1) // packs):
        turned = end_ref[part].T
        for q in range(part * packs, min(narrow, (part + 1) * packs)):
            shift = (q % packs) * tail_size
            spread(pltpu.roll(turned, (LANES - shift) % LANES, 1) if shift else turned, tail, q)

    flat_next = ckeep_ref.reshape(levels * live, child_rows)

    def write(l, carry):
        at = pl.ds(pl.multiple_of(l * stored, 8), live)
        parts = [
            (mask_ref[n, :live, :] * (cmid_ref[n, at, :] + add_ref[n, at, :]))[:, :size] for n, size in tiles
        ]
        flat_next[pl.ds(pl.multiple_of(l * live, 2), live), :] = jnp.concatenate(parts, axis=1)
        return carry

    sends = [send_parent]
    step = -(-levels // chunks)
    for c in range(chunks):
        low, high = c * step, min(levels, (c + 1) * step)
        lax.fori_loop(low, high, write, 0, unroll=2)
        part = pl.ds(low, high - low)
        sends.append(pltpu.make_async_copy(ckeep_ref.at[part], cnext_hbm.at[part], sems.at[1 + c]))
        sends[-1].start()
    for send in sends:
        send.wait()


def ring(block, axes, count, step):
    return lax.ppermute(block, axes, [(i, (i + step) % count) for i in range(count)])


def body(parent_tracer, child_tracer, strip_cols, row_offset, parent_wet, child_wet, vert_mix):
    tracers, levels, rows, width = parent_tracer.shape
    capacity, child_rows = child_wet.shape
    strips = lax.axis_size("child")
    narrow = capacity // 3
    all_rows = rows * strips
    tiles = tile_list(child_rows)
    lane_tiles = len(tiles)
    packed = -(-narrow // (LANES // tiles[-1][1]))
    stored = up(capacity * tracers, 8)
    stride = stored + 16
    chunks = 5
    message = lane_tiles * up(tracers * levels, 8) + width
    f32 = lambda *s: jax.ShapeDtypeStruct(s, jnp.float32)
    mem = lambda *s: pltpu.VMEM(s, jnp.float32)
    parent = jnp.transpose(parent_tracer, (0, 2, 3, 1))
    child = jnp.transpose(child_tracer, (1, 2, 0, 3))

    flat, forth, back, left_edge, right_edge = pl.pallas_call(
        prepare_kernel,
        in_specs=[HBM] * 5,
        out_specs=[VM] * 5,
        out_shape=[
            f32(width * rows, LANES), f32(message, LANES), f32(message, LANES), f32(rows, LANES), f32(rows, LANES),
        ],
        scratch_shapes=[
            pltpu.SMEM(strip_cols.shape, jnp.int32),
            mem(*parent.shape),
            pltpu.VMEM(parent_wet.shape, jnp.int32),
            pltpu.VMEM(child_wet.shape, jnp.int32),
            mem(2, levels, 1, tracers, child_rows),
            mem(LANES, LANES),
            mem(rows, width, LANES),
            pltpu.SemaphoreType.DMA((6,)),
        ],
        compiler_params=params(16),
        name="prepare",
    )(*(in_hbm(x) for x in (strip_cols, parent, parent_wet, child, child_wet)))

    groups = lax.axis_size("parent")
    devices = groups * strips
    right_edge = ring(right_edge, "parent", groups, 1)
    left_edge = ring(left_edge, "parent", groups, -1)
    forth = ring(forth, ("parent", "child"), devices, 1)
    back = ring(back, ("parent", "child"), devices, -1)

    weight, carry, below, inverse = pl.pallas_call(
        coefficient_kernel,
        in_specs=[SM],
        out_specs=[VM] * 4,
        out_shape=[f32(8 * levels, LANES)] * 3 + [f32(LANES, LANES)],
        scratch_shapes=[mem(8 * levels, LANES), mem(8 * levels, LANES)],
        compiler_params=params(8),
        name="coefficients",
    )(vert_mix)

    send, parent_mid, own, child_mid = pl.pallas_call(
        functools.partial(solve_kernel, groups, strips, rows),
        in_specs=[SM, SM] + [VM] * 9 + [HBM, VM],
        out_specs=[VM] * 4,
        out_shape=[
            f32(strips, 2 * narrow * rows, LANES),
            f32(width * rows, LANES),
            f32(narrow * all_rows, LANES),
            f32(lane_tiles, levels * stored, LANES),
        ],
        scratch_shapes=[
            mem(width * rows, LANES),
            mem((width + narrow) * rows, LANES),
            mem(lane_tiles, stored, LANES),
            mem(lane_tiles, levels * stride, LANES),
            mem(lane_tiles, levels * stored, LANES),
            mem(LANES, LANES),
            mem(packed, LANES, LANES),
            mem(narrow * child_rows, LANES),
            mem(*child.shape),
            pltpu.SemaphoreType.DMA((chunks,)),
        ],
        compiler_params=params(32),
        name="solve",
    )(
        strip_cols, row_offset, flat, forth, back, right_edge, left_edge,
        weight, carry, below, inverse, in_hbm(child), child_wet,
    )

    got = lax.all_to_all(send, "child", 0, 0)

    parent_next, child_next = pl.pallas_call(
        functools.partial(finish_kernel, strips, rows, chunks),
        in_specs=[SM, SM] + [VM] * 6,
        out_specs=[HBM, HBM],
        out_shape=[f32(*parent.shape), f32(*child.shape)],
        scratch_shapes=[
            mem(narrow * all_rows, LANES),
            mem((width + narrow) * rows, LANES),
            mem(2 * up(narrow, 8), LANES),
            mem(narrow * child_rows, LANES),
            mem(packed, LANES, LANES),
            mem(lane_tiles, levels * stored, LANES),
            mem(lane_tiles, stored, LANES),
            mem(width * rows, LANES),
            mem(*parent.shape),
            mem(*child.shape),
            pltpu.SemaphoreType.DMA((1 + chunks,)),
        ],
        compiler_params=params(32),
        name="finish",
    )(strip_cols, row_offset, got, own, parent_mid, inverse, child_mid, child_wet)
    return jnp.transpose(parent_next, (0, 3, 1, 2)), jnp.transpose(child_next, (2, 0, 1, 3))


def solution(mesh):
    return jax.shard_map(
        body,
        mesh=mesh,
        in_specs=(
            P(None, None, "child", "parent"),
            P(None, None, ("parent", "child"), None),
            P(),
            P(),
            P("child", "parent"),
            P(("parent", "child"), None),
            P(),
        ),
        out_specs=(P(None, None, "child", "parent"), P(None, None, ("parent", "child"), None)),
        check_vma=False,
    )
```

```python
import functools

import jax
import jax.numpy as jnp
from jax import lax
from jax.experimental import pallas as pl
from jax.experimental.pallas import tpu as pltpu
from jax.sharding import PartitionSpec as P

diffusion = 0.2
nudging = 0.5
one_ninth = 1.0 / 9.0
LANES = 128
HIGH = lax.Precision.HIGHEST

VM = pl.BlockSpec(memory_space=pltpu.VMEM)
SM = pl.BlockSpec(memory_space=pltpu.SMEM)
HBM = pl.BlockSpec(memory_space=pltpu.HBM)


def params(mib):
    return pltpu.CompilerParams(vmem_limit_bytes=mib << 20)


def in_hbm(x):
    return pltpu.with_memory_space_constraint(x, pltpu.HBM)


def up(n, m):
    return (n + m - 1) // m * m


def tile_list(child_rows):
    return [(t, min(LANES, child_rows - t * LANES)) for t in range((child_rows + LANES - 1) // LANES)]


def my_cols(cols_ref):
    return cols_ref[lax.axis_index("parent"), lax.axis_index("child")]


def strip_starts(cols_ref, strips):
    group = lax.axis_index("parent")
    start = jnp.int32(0)
    starts = []
    for j in range(strips):
        starts.append(start)
        start = start + cols_ref[group, j]
    return starts


def coefficients(mix_ref, weight_ref, carry_ref, back_ref, inverse_ref, d_ref, c_ref):
    tracers, levels = mix_ref.shape[0], mix_ref.shape[1] + 1
    slot = LANES // tracers
    lane = lax.broadcasted_iota(jnp.int32, (8, LANES), 1)
    by_lane = lane // slot
    by_row = lax.broadcasted_iota(jnp.int32, (8, LANES), 0) % tracers
    none = jnp.zeros((8, LANES), jnp.float32)

    def mixed(k, which):
        row = none
        if 0 <= k < levels - 1:
            for t in range(tracers):
                row = jnp.where(which == t, mix_ref[t, k], row)
        return row

    weights = [none, none]
    d = none
    for k in range(levels):
        for n, which in enumerate((by_row, by_lane)):
            above, below = mixed(k - 1, which), mixed(k, which)
            w = 1.0 / (1.0 + above + below - above * (above * weights[n]))
            weights[n] = w
            at = pl.ds(8 * k, 8)
            if n == 0:
                weight_ref[at, :] = w
                carry_ref[at, :] = above * w
                back_ref[at, :] = below * w
            else:
                unit = (lane - which * slot == k).astype(jnp.float32)
                d = (unit + above * d) * w
                d_ref[at, :] = d
                c_ref[at, :] = below * w
    inverse_ref[...] = jnp.zeros_like(inverse_ref)
    x = none
    for k in reversed(range(levels)):
        x = d_ref[pl.ds(8 * k, 8), :] + c_ref[pl.ds(8 * k, 8), :] * x
        for t in range(tracers):
            inverse_ref[t * slot + k : t * slot + k + 1, :] = jnp.where(by_lane == t, x, 0.0)[:1]


def prepare_kernel(
    cols_hbm, parent_hbm, pwet_hbm, child_hbm, cwet_hbm,
    flat_ref, forth_ref, back_ref, left_ref, right_ref,
    cols_ref, parent_ref, pwet_ref, cwet_ref, edge_ref, turn_ref, row_ref, sems,
):
    levels, capacity, tracers, child_rows = child_hbm.shape
    rows, width = pwet_ref.shape
    slot = LANES // tracers
    level_rows = up(tracers * levels, 8)
    tiles = tile_list(child_rows)
    fetch_cols = pltpu.make_async_copy(cols_hbm, cols_ref, sems.at[0])
    fetch_pwet = pltpu.make_async_copy(pwet_hbm, pwet_ref, sems.at[1])
    fetch_parent = pltpu.make_async_copy(parent_hbm, parent_ref, sems.at[2])
    fetch_cwet = pltpu.make_async_copy(cwet_hbm, cwet_ref, sems.at[3])
    fetch_first = pltpu.make_async_copy(child_hbm.at[:, pl.ds(0, 1)], edge_ref.at[1], sems.at[4])
    for fetch in (fetch_cols, fetch_pwet, fetch_parent, fetch_first, fetch_cwet):
        fetch.start()
    fetch_cols.wait()
    last = 3 * my_cols(cols_ref) - 1
    fetch_last = pltpu.make_async_copy(child_hbm.at[:, pl.ds(last, 1)], edge_ref.at[0], sems.at[5])
    fetch_last.start()
    row_ref[...] = jnp.zeros_like(row_ref)
    fetch_pwet.wait()
    turn_ref[:rows, :width] = pwet_ref[...].astype(jnp.float32)
    wet = turn_ref[...].T
    fetch_parent.wait()
    for r in range(rows):
        cell = wet[:width, r : r + 1]
        for t in range(tracers):
            row_ref[r, :, t * slot : t * slot + levels] = cell * parent_ref[t, r]
        row_ref[r, :, levels : levels + 1] = cell
        flat_ref[pl.ds(r, width, stride=rows), :] = row_ref[r]
    left_ref[...] = flat_ref[:rows, :]
    right_ref[...] = flat_ref[(width - 1) * rows :, :]
    fetch_cwet.wait()
    base = len(tiles) * level_rows
    fetch_first.wait()
    fetch_last.wait()
    for side, (ref, x, r) in enumerate(((forth_ref, last, rows - 1), (back_ref, 0, 0))):
        cell = cwet_ref[pl.ds(x, 1), :].astype(jnp.float32)
        pairs = edge_ref.at[side].reshape(levels * tracers, child_rows)[...] * cell
        for n, size in tiles:
            ref[n * level_rows : n * level_rows + levels * tracers, :size] = pairs[:, n * LANES : n * LANES + size]
        ref[base : base + width, :] = row_ref[r]


def masks(cols_ref, cwet_ref, mask_ref, tracers):
    capacity, child_rows = cwet_ref.shape
    column = lax.broadcasted_iota(jnp.int32, (capacity, 1), 0)
    mask = cwet_ref[...].astype(jnp.float32) * (column < 3 * my_cols(cols_ref)).astype(jnp.float32)
    mask_ref[...] = jnp.zeros_like(mask_ref)
    for n, size in tile_list(child_rows):
        part = mask[:, n * LANES : n * LANES + size]
        if size < LANES:
            part = jnp.concatenate([part, jnp.zeros((capacity, LANES - size), jnp.float32)], axis=1)
        for t in range(tracers):
            mask_ref[n, pl.ds(t, capacity, stride=tracers), :] = part
    return mask


def inner_kernel(
    cols_ref, mix_ref, child_ref, cwet_ref,
    weight_ref, carry_ref, back_ref, inverse_ref, explicit_ref,
    mask_ref, begin_ref, d_ref, c_ref,
):
    levels, capacity, tracers, child_rows = child_ref.shape
    tiles = tile_list(child_rows)
    live = capacity * tracers
    stored = up(live, 8)
    stride = begin_ref.shape[1] // levels
    coefficients(mix_ref, weight_ref, carry_ref, back_ref, inverse_ref, d_ref, c_ref)
    masks(cols_ref, cwet_ref, mask_ref, tracers)
    flat_child = child_ref.reshape(levels * live, child_rows)
    lane = lax.broadcasted_iota(jnp.int32, (stored, LANES), 1)
    gap = jnp.zeros((tracers, LANES), jnp.float32)
    after = stored - live + tracers

    def explicit(l, carry):
        cells = flat_child[pl.ds(pl.multiple_of(l * live, 2), live), :]
        start = pl.multiple_of(l * stride, 8)
        for n, size in tiles:
            part = cells[:, n * LANES : n * LANES + size] * mask_ref[n, :live, :size]
            if size < LANES:
                part = jnp.concatenate([part, jnp.zeros((live, LANES - size), jnp.float32)], axis=1)
            begin_ref[n, pl.ds(start + 8, live), :] = part
            begin_ref[n, pl.ds(start + 8 - tracers, tracers), :] = gap
            begin_ref[n, pl.ds(start + 8 + live, after), :] = jnp.zeros((after, LANES), jnp.float32)
        here = [begin_ref[n, pl.ds(start + 8, stored), :] for n, _ in tiles]
        lower = [pltpu.roll(c, 1, 1) for c in here]
        upper = [pltpu.roll(c, LANES - 1, 1) for c in here]
        for n, size in tiles:
            south = jnp.where(lane == 0, lower[n - 1] if n else 0.0, lower[n])
            if n + 1 < len(tiles):
                north = jnp.where(lane == LANES - 1, upper[n + 1], upper[n])
            else:
                north = jnp.where(lane == size - 1, 0.0, upper[n])
            west = begin_ref[n, pl.ds(start + 8 - tracers, stored), :]
            east = begin_ref[n, pl.ds(start + 8 + tracers, stored), :]
            explicit_ref[n, pl.ds(pl.multiple_of(l * stored, 8), stored), :] = (diffusion * mask_ref[n]) * (
                here[n] + west + east + south + north
            )
        return carry

    lax.fori_loop(0, levels, explicit, 0, unroll=10 if levels % 10 == 0 else 1)


def pack_kernel(
    groups, strips, rows, tracers, levels,
    cols_ref, offset_ref, flat_ref, before_ref, after_ref, left_ref, right_ref, inverse_ref, explicit_ref, cwet_ref,
    *refs,
):
    send_refs = refs[:strips]
    pmid_ref, own_ref, halo_ref, step_ref, wide_ref, turn_ref, end_ref, long_ref, start_ref = refs[strips:]
    capacity, child_rows = cwet_ref.shape
    stored = up(capacity * tracers, 8)
    slot = LANES // tracers
    width = flat_ref.shape[0] // rows
    narrow = capacity // 3
    covered = child_rows // 3
    all_rows = strips * rows
    tiles = tile_list(child_rows)
    level_rows = up(tracers * levels, 8)
    base = len(tiles) * level_rows
    group, member = lax.axis_index("parent"), lax.axis_index("child")
    offset = offset_ref[0]
    cols = my_cols(cols_ref)
    for j, start in enumerate(strip_starts(cols_ref, strips)):
        start_ref[j] = start

    has_before = (member > 0).astype(jnp.float32)
    has_after = (member < strips - 1).astype(jnp.float32)
    has_left = (group > 0).astype(jnp.float32)
    has_right = (group < groups - 1).astype(jnp.float32)
    for x in range(width):
        here = flat_ref[x * rows : (x + 1) * rows, :]
        west = has_left * left_ref[...] if x == 0 else flat_ref[(x - 1) * rows : x * rows, :]
        east = has_right * right_ref[...] if x == width - 1 else flat_ref[(x + 1) * rows : (x + 2) * rows, :]
        south = jnp.concatenate([has_before * before_ref[base + x : base + x + 1, :], here[:-1]], axis=0)
        north = jnp.concatenate([here[1:], has_after * after_ref[base + x : base + x + 1, :]], axis=0)
        wet = here[:, levels : levels + 1]
        laplace = north + south + east + west - 4.0 * here
        step_ref[x * rows : (x + 1) * rows, :] = wet * (here + diffusion * laplace)
    solved = jnp.dot(step_ref[...], inverse_ref[...], precision=HIGH, preferred_element_type=jnp.float32)
    lane = lax.broadcasted_iota(jnp.int32, (width * rows, LANES), 1)
    solved = jnp.where(lane == levels, flat_ref[...], solved)
    wide_ref[: width * rows, :] = solved
    wide_ref[width * rows :, :] = jnp.zeros((narrow * rows, LANES), jnp.float32)
    pmid_ref[...] = solved
    for s in range(strips):
        start = start_ref[member ^ s]
        send_refs[s][: narrow * rows, :] = wide_ref[pl.ds(pl.multiple_of(start * rows, rows), narrow * rows), :]

    column = lax.broadcasted_iota(jnp.int32, (capacity, 1), 0)
    mask = cwet_ref[...].astype(jnp.float32) * (column < 3 * cols).astype(jnp.float32)
    west_mask = (diffusion * jnp.maximum(has_before, has_left)) * mask[:1]
    east_wet = cwet_ref[pl.ds(3 * cols - 1, 1), :].astype(jnp.float32)
    east_mask = (diffusion * jnp.maximum(has_after, has_right)) * east_wet
    halo_ref[...] = jnp.zeros_like(halo_ref)
    for n, size in tiles:
        part = slice(n * LANES, n * LANES + size)
        for l in range(levels):
            edge = slice(n * level_rows + l * tracers, n * level_rows + (l + 1) * tracers)
            halo_ref[n, 8 * l : 8 * l + tracers, :size] = west_mask[:, part] * before_ref[edge, :size]
            halo_ref[n, 8 * l + tracers : 8 * l + 2 * tracers, :size] = east_mask[:, part] * after_ref[edge, :size]

    own_ref[...] = jnp.zeros_like(own_ref)
    turn_ref[...] = jnp.zeros_like(turn_ref)
    end_ref[...] = jnp.zeros_like(end_ref)
    y = lax.broadcasted_iota(jnp.int32, (1, child_rows), 1)
    at_end = ((y == 0) | (y == child_rows - 1)).astype(jnp.float32)
    tail, tail_size = tiles[-1]
    packs = LANES // tail_size
    for q in range(narrow):
        count = (mask[3 * q : 3 * q + 1] + mask[3 * q + 1 : 3 * q + 2] + mask[3 * q + 2 : 3 * q + 3]) * at_end
        is_last = (cols == q + 1).astype(jnp.float32)
        for n, size in tiles:
            into, low = (turn_ref, 0) if n < tail else (end_ref.at[q // packs], (q % packs) * size)
            for t in range(tracers):
                part = is_last * halo_ref[n, pl.ds(tracers + t, levels, stride=8), :]
                if q == 0:
                    part = part + halo_ref[n, pl.ds(t, levels, stride=8), :]
                for dx in range(3):
                    part = part + explicit_ref[n, pl.ds((3 * q + dx) * tracers + t, levels, stride=stored), :]
                into[t * slot : t * slot + levels, low : low + size] = part[:, :size]
            into[levels : levels + 1, low : low + size] = count[:, n * LANES : n * LANES + size]
            if n < tail:
                long_ref[q * child_rows + n * LANES : q * child_rows + n * LANES + size, :] = turn_ref[...].T
    for part in range((narrow + packs - 1) // packs):
        turned = end_ref[part].T
        for q in range(part * packs, min(narrow, (part + 1) * packs)):
            low = (q % packs) * tail_size
            high = (q + 1) * child_rows
            long_ref[high - tail_size : high, :] = turned[low : low + tail_size]
    for q in range(narrow):
        mean = one_ninth * (
            long_ref[pl.ds(q * child_rows, covered, stride=3), :]
            + long_ref[pl.ds(q * child_rows + 1, covered, stride=3), :]
            + long_ref[pl.ds(q * child_rows + 2, covered, stride=3), :]
        )
        own_ref[pl.ds(q * all_rows + offset, covered), :] = mean
    for s in range(strips):
        band = (member ^ s) * rows
        for q in range(narrow):
            send_refs[s][(narrow + q) * rows : (narrow + q + 1) * rows, :] = own_ref[
                pl.ds(pl.multiple_of(q * all_rows + band, rows), rows), :
            ]


def level_kernel(
    tracers, levels, capacity,
    cols_ref, weight_ref, carry_ref, back_ref, inverse_ref, explicit_ref, halo_ref, own_ref,
    cmid_ref, mean_ref,
    d_ref, h_ref,
):
    count = explicit_ref.shape[0]
    stored = explicit_ref.shape[1] // levels
    past = 3 * tracers * my_cols(cols_ref) - tracers

    def by_rows(factor, value):
        return (factor[None] * value.reshape(stored // 8, 8, LANES)).reshape(stored, LANES)

    def forward(l, carry):
        at = pl.ds(pl.multiple_of(l * stored, 8), stored)
        coef = pl.ds(pl.multiple_of(l * 8, 8), 8)
        weight, above = weight_ref[coef, :], carry_ref[coef, :]
        held = []
        for n in range(count):
            d = by_rows(weight, explicit_ref[n, at, :]) + by_rows(above, carry[2 * n])
            h = weight * halo_ref[n, coef, :] + above * carry[2 * n + 1]
            d_ref[n, at, :] = d
            h_ref[n, coef, :] = h
            held += [d, h]
        return tuple(held)

    blank = (jnp.zeros((stored, LANES), jnp.float32), jnp.zeros((8, LANES), jnp.float32)) * count
    unroll = 5 if levels % 5 == 0 else 1
    lax.fori_loop(0, levels, forward, blank, unroll=unroll)

    def backward(step, carry):
        l = levels - 1 - step
        start = pl.multiple_of(l * stored, 8)
        at = pl.ds(start, stored)
        coef = pl.ds(pl.multiple_of(l * 8, 8), 8)
        below = back_ref[coef, :]
        held = []
        for n in range(count):
            x = d_ref[n, at, :] + by_rows(below, carry[2 * n])
            h = h_ref[n, coef, :] + below * carry[2 * n + 1]
            cmid_ref[n, at, :] = x
            first = pl.ds(start, tracers)
            cmid_ref[n, first, :] = cmid_ref[n, first, :] + h[:tracers]
            last = pl.ds(start + past, tracers)
            cmid_ref[n, last, :] = cmid_ref[n, last, :] + h[tracers : 2 * tracers]
            held += [x, h]
        return tuple(held)

    lax.fori_loop(0, levels, backward, blank, unroll=unroll)
    own = own_ref[...]
    solved = jnp.dot(own, inverse_ref[...], precision=HIGH, preferred_element_type=jnp.float32)
    lane = lax.broadcasted_iota(jnp.int32, own.shape, 1)
    mean_ref[...] = jnp.where(lane == levels, own, solved)


def finish_kernel(
    strips, rows, chunks,
    cols_ref, offset_ref, own_ref, pmid_ref, inverse_ref, cmid_ref, cwet_ref,
    *refs,
):
    got_refs = refs[:strips]
    (
        pnext_hbm, cnext_hbm,
        panel_ref, wide_ref, ends_ref, long_ref, end_ref, add_ref, mask_ref, next_ref, pkeep_ref, ckeep_ref,
        start_ref, sems,
    ) = refs[strips:]
    levels, capacity, tracers, child_rows = cnext_hbm.shape
    slot = LANES // tracers
    width = pmid_ref.shape[0] // rows
    narrow = capacity // 3
    covered = child_rows // 3
    all_rows = strips * rows
    tiles = tile_list(child_rows)
    live = capacity * tracers
    stored = up(live, 8)
    padded = up(narrow, 8)
    member = lax.axis_index("child")
    group = lax.axis_index("parent")
    for j, start in enumerate(strip_starts(cols_ref, strips)):
        start_ref[j] = start
    offset = offset_ref[0]
    masks(cols_ref, cwet_ref, mask_ref, tracers)

    ends_ref[...] = jnp.zeros_like(ends_ref)
    for q in range(narrow):
        for s in range(strips):
            at = pl.ds(pl.multiple_of(q * all_rows + (member ^ s) * rows, rows), rows)
            panel_ref[at, :] = got_refs[s][q * rows : (q + 1) * rows, :]
        ends_ref[q : q + 1, :] = panel_ref[pl.ds(q * all_rows + offset, 1), :]
        ends_ref[padded + q : padded + q + 1, :] = panel_ref[pl.ds(q * all_rows + offset + covered - 1, 1), :]
    solved_ends = jnp.dot(ends_ref[...], inverse_ref[...], precision=HIGH, preferred_element_type=jnp.float32)
    f = lax.broadcasted_iota(jnp.int32, (covered, 1), 0)
    first_row = (f == 0).astype(jnp.float32)
    last_row = (f == covered - 1).astype(jnp.float32)
    tail, tail_size = tiles[-1]
    packs = LANES // tail_size

    def spread(turned, n, q):
        for t in range(tracers):
            part = turned[t * slot : t * slot + levels]
            for dx in range(3):
                add_ref[n, pl.ds((3 * q + dx) * tracers + t, levels, stride=stored), :] = part

    for q in range(narrow):
        low = solved_ends[q : q + 1]
        high = solved_ends[padded + q : padded + q + 1]
        panel = panel_ref[pl.ds(q * all_rows + offset, covered), :]
        mean = own_ref[pl.ds(q * all_rows + offset, covered), :]
        coarse = mean + diffusion * mean[:, levels : levels + 1] * (first_row * low + last_row * high)
        gap = nudging * (panel - coarse)
        base = q * child_rows
        for dy in range(3):
            long_ref[pl.ds(base + dy, covered, stride=3), :] = gap
        long_ref[base : base + 1, :] = gap[:1] + diffusion * low
        long_ref[base + child_rows - 1 : base + child_rows, :] = gap[covered - 1 :] + diffusion * high
        for n, size in tiles[:-1]:
            spread(long_ref[base + n * LANES : base + n * LANES + size, :].T, n, q)
        at = (q % packs) * tail_size
        end_ref[q // packs, at : at + tail_size, :] = long_ref[base + child_rows - tail_size : base + child_rows, :]
    for part in range((narrow + packs - 1) // packs):
        turned = end_ref[part].T
        for q in range(part * packs, min(narrow, (part + 1) * packs)):
            shift = (q % packs) * tail_size
            spread(pltpu.roll(turned, (LANES - shift) % LANES, 1) if shift else turned, tail, q)

    flat_next = ckeep_ref.reshape(levels * live, child_rows)

    def write(l, carry):
        at = pl.ds(pl.multiple_of(l * stored, 8), live)
        parts = [
            (mask_ref[n, :live, :] * (cmid_ref[n, at, :] + add_ref[n, at, :]))[:, :size] for n, size in tiles
        ]
        flat_next[pl.ds(pl.multiple_of(l * live, 2), live), :] = jnp.concatenate(parts, axis=1)
        return carry

    sends = []
    step = -(-levels // chunks)
    for c in range(chunks):
        low, high = c * step, min(levels, (c + 1) * step)
        lax.fori_loop(low, high, write, 0, unroll=2)
        part = pl.ds(low, high - low)
        sends.append(pltpu.make_async_copy(ckeep_ref.at[part], cnext_hbm.at[part], sems.at[1 + c]))
        sends[-1].start()

    for s in range(strips):
        j = member ^ s
        start, cols = start_ref[j], cols_ref[group, j]
        for q in range(narrow):
            to = jnp.where(q < cols, start + q, width + q)
            wide_ref[pl.ds(pl.multiple_of(to * rows, rows), rows), :] = got_refs[s][
                (narrow + q) * rows : (narrow + q + 1) * rows, :
            ]
    pmid = pmid_ref[...]
    mean = wide_ref[: width * rows, :]
    mean = mean + diffusion * mean[:, levels : levels + 1] * pmid
    coarse = jnp.dot(mean, inverse_ref[...], precision=HIGH, preferred_element_type=jnp.float32)
    row = member * rows + lax.broadcasted_iota(jnp.int32, (width * rows, 1), 0) % rows
    inside = (row >= offset) & (row < offset + covered)
    next_ref[...] = pmid[:, levels : levels + 1] * jnp.where(inside, coarse, pmid)
    for r in range(rows):
        block = next_ref[pl.ds(r, width, stride=rows), :]
        for t in range(tracers):
            pkeep_ref[t, r] = block[:, t * slot : t * slot + levels]
    send_parent = pltpu.make_async_copy(pkeep_ref, pnext_hbm, sems.at[0])
    send_parent.start()
    sends.append(send_parent)
    for send in sends:
        send.wait()


def ring(block, axes, count, step):
    return lax.ppermute(block, axes, [(i, (i + step) % count) for i in range(count)])


def body(parent_tracer, child_tracer, strip_cols, row_offset, parent_wet, child_wet, vert_mix):
    tracers, levels, rows, width = parent_tracer.shape
    capacity, child_rows = child_wet.shape
    strips = lax.axis_size("child")
    narrow = capacity // 3
    all_rows = rows * strips
    tiles = tile_list(child_rows)
    lane_tiles = len(tiles)
    packed = -(-narrow // (LANES // tiles[-1][1]))
    stored = up(capacity * tracers, 8)
    stride = stored + 16
    chunks = 5
    message = lane_tiles * up(tracers * levels, 8) + width
    f32 = lambda *s: jax.ShapeDtypeStruct(s, jnp.float32)
    mem = lambda *s: pltpu.VMEM(s, jnp.float32)
    parent = jnp.transpose(parent_tracer, (0, 2, 3, 1))
    child = jnp.transpose(child_tracer, (1, 2, 0, 3))

    flat, forth, back, left_edge, right_edge = pl.pallas_call(
        prepare_kernel,
        in_specs=[HBM] * 5,
        out_specs=[VM] * 5,
        out_shape=[
            f32(width * rows, LANES), f32(message, LANES), f32(message, LANES), f32(rows, LANES), f32(rows, LANES),
        ],
        scratch_shapes=[
            pltpu.SMEM(strip_cols.shape, jnp.int32),
            mem(*parent.shape),
            pltpu.VMEM(parent_wet.shape, jnp.int32),
            pltpu.VMEM(child_wet.shape, jnp.int32),
            mem(2, levels, 1, tracers, child_rows),
            mem(LANES, LANES),
            mem(rows, width, LANES),
            pltpu.SemaphoreType.DMA((6,)),
        ],
        compiler_params=params(16),
        name="prepare",
    )(*(in_hbm(x) for x in (strip_cols, parent, parent_wet, child, child_wet)))

    groups = lax.axis_size("parent")
    devices = groups * strips
    right_edge = ring(right_edge, "parent", groups, 1)
    left_edge = ring(left_edge, "parent", groups, -1)
    forth = ring(forth, ("parent", "child"), devices, 1)
    back = ring(back, ("parent", "child"), devices, -1)

    weight, carry, below, inverse, explicit = pl.pallas_call(
        inner_kernel,
        in_specs=[SM, SM, VM, VM],
        out_specs=[VM] * 5,
        out_shape=[f32(8 * levels, LANES)] * 3 + [f32(LANES, LANES), f32(lane_tiles, levels * stored, LANES)],
        scratch_shapes=[
            mem(lane_tiles, stored, LANES),
            mem(lane_tiles, levels * stride, LANES),
            mem(8 * levels, LANES),
            mem(8 * levels, LANES),
        ],
        compiler_params=params(16),
        name="inner",
    )(strip_cols, vert_mix, child, child_wet)

    block = f32(2 * narrow * rows, LANES)
    *blocks, parent_mid, own, halo = pl.pallas_call(
        functools.partial(pack_kernel, groups, strips, rows, tracers, levels),
        in_specs=[SM, SM] + [VM] * 8,
        out_specs=[VM] * (strips + 3),
        out_shape=[block] * strips
        + [f32(width * rows, LANES), f32(narrow * all_rows, LANES), f32(lane_tiles, 8 * levels, LANES)],
        scratch_shapes=[
            mem(width * rows, LANES),
            mem((width + narrow) * rows, LANES),
            mem(LANES, LANES),
            mem(packed, LANES, LANES),
            mem(narrow * child_rows, LANES),
            pltpu.SMEM((strips,), jnp.int32),
        ],
        compiler_params=params(16),
        name="pack",
    )(strip_cols, row_offset, flat, forth, back, right_edge, left_edge, inverse, explicit, child_wet)

    got = [blocks[0]] + [
        lax.ppermute(blocks[s], "child", [(i, i ^ s) for i in range(strips)]) for s in range(1, strips)
    ]

    child_mid, mean = pl.pallas_call(
        functools.partial(level_kernel, tracers, levels, capacity),
        in_specs=[SM] + [VM] * 7,
        out_specs=[VM, VM],
        out_shape=[f32(lane_tiles, levels * stored, LANES), f32(narrow * all_rows, LANES)],
        scratch_shapes=[mem(lane_tiles, levels * stored, LANES), mem(lane_tiles, 8 * levels, LANES)],
        compiler_params=params(16),
        name="levels",
    )(strip_cols, weight, carry, below, inverse, explicit, halo, own)

    parent_next, child_next = pl.pallas_call(
        functools.partial(finish_kernel, strips, rows, chunks),
        in_specs=[SM, SM] + [VM] * (5 + strips),
        out_specs=[HBM, HBM],
        out_shape=[f32(*parent.shape), f32(*child.shape)],
        scratch_shapes=[
            mem(narrow * all_rows, LANES),
            mem((width + narrow) * rows, LANES),
            mem(2 * up(narrow, 8), LANES),
            mem(narrow * child_rows, LANES),
            mem(packed, LANES, LANES),
            mem(lane_tiles, levels * stored, LANES),
            mem(lane_tiles, stored, LANES),
            mem(width * rows, LANES),
            mem(*parent.shape),
            mem(*child.shape),
            pltpu.SMEM((strips,), jnp.int32),
            pltpu.SemaphoreType.DMA((1 + chunks,)),
        ],
        compiler_params=params(24),
        name="finish",
    )(strip_cols, row_offset, mean, parent_mid, inverse, child_mid, child_wet, *got)
    return jnp.transpose(parent_next, (0, 3, 1, 2)), jnp.transpose(child_next, (2, 0, 1, 3))


def solution(mesh):
    return jax.shard_map(
        body,
        mesh=mesh,
        in_specs=(
            P(None, None, "child", "parent"),
            P(None, None, ("parent", "child"), None),
            P(),
            P(),
            P("child", "parent"),
            P(("parent", "child"), None),
            P(),
        ),
        out_specs=(P(None, None, "child", "parent"), P(None, None, ("parent", "child"), None)),
        check_vma=False,
    )
```

```python
import functools

import jax
import jax.numpy as jnp
from jax import lax
from jax.experimental import pallas as pl
from jax.experimental.pallas import tpu as pltpu
from jax.sharding import PartitionSpec as P

diffusion = 0.2
nudging = 0.5
one_ninth = 1.0 / 9.0
LANES = 128
HIGH = lax.Precision.HIGHEST

VM = pl.BlockSpec(memory_space=pltpu.VMEM)
SM = pl.BlockSpec(memory_space=pltpu.SMEM)
HBM = pl.BlockSpec(memory_space=pltpu.HBM)


def params(mib):
    return pltpu.CompilerParams(vmem_limit_bytes=mib << 20)


def in_hbm(x):
    return pltpu.with_memory_space_constraint(x, pltpu.HBM)


def far_first(strips):
    return list(reversed(range(strips)))


def up(n, m):
    return (n + m - 1) // m * m


def tile_list(child_rows):
    return [(t, min(LANES, child_rows - t * LANES)) for t in range((child_rows + LANES - 1) // LANES)]


def my_cols(cols_ref):
    return cols_ref[lax.axis_index("parent"), lax.axis_index("child")]


def strip_starts(cols_ref, strips):
    group = lax.axis_index("parent")
    start = jnp.int32(0)
    starts = []
    for j in range(strips):
        starts.append(start)
        start = start + cols_ref[group, j]
    return starts


def coefficients(mix_ref, weight_ref, carry_ref, back_ref, inverse_ref, d_ref, c_ref):
    tracers, levels = mix_ref.shape[0], mix_ref.shape[1] + 1
    slot = LANES // tracers
    lane = lax.broadcasted_iota(jnp.int32, (8, LANES), 1)
    by_lane = lane // slot
    by_row = lax.broadcasted_iota(jnp.int32, (8, LANES), 0) % tracers
    none = jnp.zeros((8, LANES), jnp.float32)

    def mixed(k, which):
        row = none
        if 0 <= k < levels - 1:
            for t in range(tracers):
                row = jnp.where(which == t, mix_ref[t, k], row)
        return row

    weights = [none, none]
    d = none
    for k in range(levels):
        for n, which in enumerate((by_row, by_lane)):
            above, below = mixed(k - 1, which), mixed(k, which)
            w = 1.0 / (1.0 + above + below - above * (above * weights[n]))
            weights[n] = w
            at = pl.ds(8 * k, 8)
            if n == 0:
                weight_ref[at, :] = w
                carry_ref[at, :] = above * w
                back_ref[at, :] = below * w
            else:
                unit = (lane - which * slot == k).astype(jnp.float32)
                d = (unit + above * d) * w
                d_ref[at, :] = d
                c_ref[at, :] = below * w
    inverse_ref[...] = jnp.zeros_like(inverse_ref)
    x = none
    for k in reversed(range(levels)):
        x = d_ref[pl.ds(8 * k, 8), :] + c_ref[pl.ds(8 * k, 8), :] * x
        for t in range(tracers):
            inverse_ref[t * slot + k : t * slot + k + 1, :] = jnp.where(by_lane == t, x, 0.0)[:1]


def prepare_kernel(
    cols_hbm, mix_hbm, parent_hbm, pwet_hbm, child_hbm, cwet_hbm,
    flat_ref, forth_ref, back_ref, left_ref, right_ref, weight_ref, carry_ref, below_ref, inverse_ref,
    cols_ref, mix_ref, parent_ref, pwet_ref, cwet_ref, edge_ref, turn_ref, row_ref, d_ref, c_ref, sems,
):
    levels, capacity, tracers, child_rows = child_hbm.shape
    rows, width = pwet_ref.shape
    slot = LANES // tracers
    level_rows = up(tracers * levels, 8)
    tiles = tile_list(child_rows)
    fetch_cols = pltpu.make_async_copy(cols_hbm, cols_ref, sems.at[0])
    fetch_pwet = pltpu.make_async_copy(pwet_hbm, pwet_ref, sems.at[1])
    fetch_parent = pltpu.make_async_copy(parent_hbm, parent_ref, sems.at[2])
    fetch_cwet = pltpu.make_async_copy(cwet_hbm, cwet_ref, sems.at[3])
    fetch_first = pltpu.make_async_copy(child_hbm.at[:, pl.ds(0, 1)], edge_ref.at[1], sems.at[4])
    fetch_mix = pltpu.make_async_copy(mix_hbm, mix_ref, sems.at[6])
    for fetch in (fetch_cols, fetch_mix, fetch_pwet, fetch_parent, fetch_first, fetch_cwet):
        fetch.start()
    fetch_cols.wait()
    last = 3 * my_cols(cols_ref) - 1
    fetch_last = pltpu.make_async_copy(child_hbm.at[:, pl.ds(last, 1)], edge_ref.at[0], sems.at[5])
    fetch_last.start()
    row_ref[...] = jnp.zeros_like(row_ref)
    fetch_mix.wait()
    coefficients(mix_ref, weight_ref, carry_ref, below_ref, inverse_ref, d_ref, c_ref)
    fetch_pwet.wait()
    turn_ref[:rows, :width] = pwet_ref[...].astype(jnp.float32)
    wet = turn_ref[...].T
    fetch_parent.wait()
    for r in range(rows):
        cell = wet[:width, r : r + 1]
        for t in range(tracers):
            row_ref[r, :, t * slot : t * slot + levels] = cell * parent_ref[t, r]
        row_ref[r, :, levels : levels + 1] = cell
        flat_ref[pl.ds(r, width, stride=rows), :] = row_ref[r]
    left_ref[...] = flat_ref[:rows, :]
    right_ref[...] = flat_ref[(width - 1) * rows :, :]
    fetch_cwet.wait()
    base = len(tiles) * level_rows
    fetch_first.wait()
    fetch_last.wait()
    for side, (ref, x, r) in enumerate(((forth_ref, last, rows - 1), (back_ref, 0, 0))):
        cell = cwet_ref[pl.ds(x, 1), :].astype(jnp.float32)
        pairs = edge_ref.at[side].reshape(levels * tracers, child_rows)[...] * cell
        for n, size in tiles:
            ref[n * level_rows : n * level_rows + levels * tracers, :size] = pairs[:, n * LANES : n * LANES + size]
        ref[base : base + width, :] = row_ref[r]


def masks(cols_ref, cwet_ref, mask_ref, tracers):
    capacity, child_rows = cwet_ref.shape
    column = lax.broadcasted_iota(jnp.int32, (capacity, 1), 0)
    mask = cwet_ref[...].astype(jnp.float32) * (column < 3 * my_cols(cols_ref)).astype(jnp.float32)
    mask_ref[...] = jnp.zeros_like(mask_ref)
    for n, size in tile_list(child_rows):
        part = mask[:, n * LANES : n * LANES + size]
        if size < LANES:
            part = jnp.concatenate([part, jnp.zeros((capacity, LANES - size), jnp.float32)], axis=1)
        for t in range(tracers):
            mask_ref[n, pl.ds(t, capacity, stride=tracers), :] = part
    return mask


def inner_kernel(
    cols_ref, child_ref, cwet_ref,
    explicit_ref, mask_ref,
    begin_ref,
):
    levels, capacity, tracers, child_rows = child_ref.shape
    tiles = tile_list(child_rows)
    live = capacity * tracers
    stored = up(live, 8)
    stride = begin_ref.shape[1] // levels
    masks(cols_ref, cwet_ref, mask_ref, tracers)
    flat_child = child_ref.reshape(levels * live, child_rows)
    lane = lax.broadcasted_iota(jnp.int32, (stored, LANES), 1)
    gap = jnp.zeros((tracers, LANES), jnp.float32)
    after = stored - live + tracers

    def explicit(l, carry):
        cells = flat_child[pl.ds(pl.multiple_of(l * live, 2), live), :]
        start = pl.multiple_of(l * stride, 8)
        for n, size in tiles:
            part = cells[:, n * LANES : n * LANES + size] * mask_ref[n, :live, :size]
            if size < LANES:
                part = jnp.concatenate([part, jnp.zeros((live, LANES - size), jnp.float32)], axis=1)
            begin_ref[n, pl.ds(start + 8, live), :] = part
            begin_ref[n, pl.ds(start + 8 - tracers, tracers), :] = gap
            begin_ref[n, pl.ds(start + 8 + live, after), :] = jnp.zeros((after, LANES), jnp.float32)
        here = [begin_ref[n, pl.ds(start + 8, stored), :] for n, _ in tiles]
        lower = [pltpu.roll(c, 1, 1) for c in here]
        upper = [pltpu.roll(c, LANES - 1, 1) for c in here]
        for n, size in tiles:
            south = jnp.where(lane == 0, lower[n - 1] if n else 0.0, lower[n])
            if n + 1 < len(tiles):
                north = jnp.where(lane == LANES - 1, upper[n + 1], upper[n])
            else:
                north = jnp.where(lane == size - 1, 0.0, upper[n])
            west = begin_ref[n, pl.ds(start + 8 - tracers, stored), :]
            east = begin_ref[n, pl.ds(start + 8 + tracers, stored), :]
            explicit_ref[n, pl.ds(pl.multiple_of(l * stored, 8), stored), :] = (diffusion * mask_ref[n]) * (
                here[n] + west + east + south + north
            )
        return carry

    lax.fori_loop(0, levels, explicit, 0, unroll=25 if levels % 25 == 0 else 1)


def pack_kernel(
    groups, strips, rows, tracers, levels,
    cols_ref, offset_ref, flat_ref, before_ref, after_ref, left_ref, right_ref, inverse_ref, explicit_ref, cwet_ref,
    *refs,
):
    send_refs = refs[:strips]
    pmid_ref, own_ref, halo_ref, step_ref, wide_ref, turn_ref, end_ref, long_ref, start_ref = refs[strips:]
    capacity, child_rows = cwet_ref.shape
    stored = up(capacity * tracers, 8)
    slot = LANES // tracers
    width = flat_ref.shape[0] // rows
    narrow = capacity // 3
    covered = child_rows // 3
    all_rows = strips * rows
    tiles = tile_list(child_rows)
    level_rows = up(tracers * levels, 8)
    base = len(tiles) * level_rows
    group, member = lax.axis_index("parent"), lax.axis_index("child")
    offset = offset_ref[0]
    cols = my_cols(cols_ref)
    for j, start in enumerate(strip_starts(cols_ref, strips)):
        start_ref[j] = start

    has_before = (member > 0).astype(jnp.float32)
    has_after = (member < strips - 1).astype(jnp.float32)
    has_left = (group > 0).astype(jnp.float32)
    has_right = (group < groups - 1).astype(jnp.float32)
    for x in range(width):
        here = flat_ref[x * rows : (x + 1) * rows, :]
        west = has_left * left_ref[...] if x == 0 else flat_ref[(x - 1) * rows : x * rows, :]
        east = has_right * right_ref[...] if x == width - 1 else flat_ref[(x + 1) * rows : (x + 2) * rows, :]
        south = jnp.concatenate([has_before * before_ref[base + x : base + x + 1, :], here[:-1]], axis=0)
        north = jnp.concatenate([here[1:], has_after * after_ref[base + x : base + x + 1, :]], axis=0)
        wet = here[:, levels : levels + 1]
        laplace = north + south + east + west - 4.0 * here
        step_ref[x * rows : (x + 1) * rows, :] = wet * (here + diffusion * laplace)
    solved = jnp.dot(step_ref[...], inverse_ref[...], precision=HIGH, preferred_element_type=jnp.float32)
    lane = lax.broadcasted_iota(jnp.int32, (width * rows, LANES), 1)
    solved = jnp.where(lane == levels, flat_ref[...], solved)
    wide_ref[: width * rows, :] = solved
    wide_ref[width * rows :, :] = jnp.zeros((narrow * rows, LANES), jnp.float32)
    pmid_ref[...] = solved
    for s in range(strips):
        start = start_ref[member ^ s]
        send_refs[s][: narrow * rows, :] = wide_ref[pl.ds(pl.multiple_of(start * rows, rows), narrow * rows), :]

    column = lax.broadcasted_iota(jnp.int32, (capacity, 1), 0)
    mask = cwet_ref[...].astype(jnp.float32) * (column < 3 * cols).astype(jnp.float32)
    west_mask = (diffusion * jnp.maximum(has_before, has_left)) * mask[:1]
    east_wet = cwet_ref[pl.ds(3 * cols - 1, 1), :].astype(jnp.float32)
    east_mask = (diffusion * jnp.maximum(has_after, has_right)) * east_wet
    halo_ref[...] = jnp.zeros_like(halo_ref)
    for n, size in tiles:
        part = slice(n * LANES, n * LANES + size)
        for l in range(levels):
            edge = slice(n * level_rows + l * tracers, n * level_rows + (l + 1) * tracers)
            halo_ref[n, 8 * l : 8 * l + tracers, :size] = west_mask[:, part] * before_ref[edge, :size]
            halo_ref[n, 8 * l + tracers : 8 * l + 2 * tracers, :size] = east_mask[:, part] * after_ref[edge, :size]

    own_ref[...] = jnp.zeros_like(own_ref)
    turn_ref[...] = jnp.zeros_like(turn_ref)
    end_ref[...] = jnp.zeros_like(end_ref)
    y = lax.broadcasted_iota(jnp.int32, (1, child_rows), 1)
    at_end = ((y == 0) | (y == child_rows - 1)).astype(jnp.float32)
    tail, tail_size = tiles[-1]
    packs = LANES // tail_size
    for q in range(narrow):
        count = (mask[3 * q : 3 * q + 1] + mask[3 * q + 1 : 3 * q + 2] + mask[3 * q + 2 : 3 * q + 3]) * at_end
        is_last = (cols == q + 1).astype(jnp.float32)
        for n, size in tiles:
            into, low = (turn_ref, 0) if n < tail else (end_ref.at[q // packs], (q % packs) * size)
            for t in range(tracers):
                part = is_last * halo_ref[n, pl.ds(tracers + t, levels, stride=8), :]
                if q == 0:
                    part = part + halo_ref[n, pl.ds(t, levels, stride=8), :]
                for dx in range(3):
                    part = part + explicit_ref[n, pl.ds((3 * q + dx) * tracers + t, levels, stride=stored), :]
                into[t * slot : t * slot + levels, low : low + size] = part[:, :size]
            into[levels : levels + 1, low : low + size] = count[:, n * LANES : n * LANES + size]
            if n < tail:
                long_ref[q * child_rows + n * LANES : q * child_rows + n * LANES + size, :] = turn_ref[...].T
    for part in range((narrow + packs - 1) // packs):
        turned = end_ref[part].T
        for q in range(part * packs, min(narrow, (part + 1) * packs)):
            low = (q % packs) * tail_size
            high = (q + 1) * child_rows
            long_ref[high - tail_size : high, :] = turned[low : low + tail_size]
    for q in range(narrow):
        mean = one_ninth * (
            long_ref[pl.ds(q * child_rows, covered, stride=3), :]
            + long_ref[pl.ds(q * child_rows + 1, covered, stride=3), :]
            + long_ref[pl.ds(q * child_rows + 2, covered, stride=3), :]
        )
        own_ref[pl.ds(q * all_rows + offset, covered), :] = mean
    for s in range(strips):
        band = (member ^ s) * rows
        for q in range(narrow):
            send_refs[s][(narrow + q) * rows : (narrow + q + 1) * rows, :] = own_ref[
                pl.ds(pl.multiple_of(q * all_rows + band, rows), rows), :
            ]


def level_kernel(
    tracers, levels, capacity,
    cols_ref, weight_ref, carry_ref, back_ref, inverse_ref, explicit_ref, halo_ref, own_ref,
    cmid_ref, mean_ref,
    d_ref, h_ref,
):
    count = explicit_ref.shape[0]
    stored = explicit_ref.shape[1] // levels
    past = 3 * tracers * my_cols(cols_ref) - tracers

    def by_rows(factor, value):
        return (factor[None] * value.reshape(stored // 8, 8, LANES)).reshape(stored, LANES)

    def forward(l, carry):
        at = pl.ds(pl.multiple_of(l * stored, 8), stored)
        coef = pl.ds(pl.multiple_of(l * 8, 8), 8)
        weight, above = weight_ref[coef, :], carry_ref[coef, :]
        held = []
        for n in range(count):
            d = by_rows(weight, explicit_ref[n, at, :]) + by_rows(above, carry[2 * n])
            h = weight * halo_ref[n, coef, :] + above * carry[2 * n + 1]
            d_ref[n, at, :] = d
            h_ref[n, coef, :] = h
            held += [d, h]
        return tuple(held)

    blank = (jnp.zeros((stored, LANES), jnp.float32), jnp.zeros((8, LANES), jnp.float32)) * count
    unroll = 5 if levels % 5 == 0 else 1
    lax.fori_loop(0, levels, forward, blank, unroll=unroll)

    def backward(step, carry):
        l = levels - 1 - step
        start = pl.multiple_of(l * stored, 8)
        at = pl.ds(start, stored)
        coef = pl.ds(pl.multiple_of(l * 8, 8), 8)
        below = back_ref[coef, :]
        held = []
        for n in range(count):
            x = d_ref[n, at, :] + by_rows(below, carry[2 * n])
            h = h_ref[n, coef, :] + below * carry[2 * n + 1]
            cmid_ref[n, at, :] = x
            first = pl.ds(start, tracers)
            cmid_ref[n, first, :] = cmid_ref[n, first, :] + h[:tracers]
            last = pl.ds(start + past, tracers)
            cmid_ref[n, last, :] = cmid_ref[n, last, :] + h[tracers : 2 * tracers]
            held += [x, h]
        return tuple(held)

    lax.fori_loop(0, levels, backward, blank, unroll=unroll)
    own = own_ref[...]
    solved = jnp.dot(own, inverse_ref[...], precision=HIGH, preferred_element_type=jnp.float32)
    lane = lax.broadcasted_iota(jnp.int32, own.shape, 1)
    mean_ref[...] = jnp.where(lane == levels, own, solved)


def finish_kernel(
    strips, rows, chunks,
    cols_ref, offset_ref, own_ref, pmid_ref, inverse_ref, cmid_ref, mask_ref,
    *refs,
):
    got_refs = {s: ref for s, ref in zip(far_first(strips), refs)}
    (
        pnext_hbm, cnext_hbm,
        panel_ref, wide_ref, ends_ref, long_ref, end_ref, add_ref, next_ref, pkeep_ref, ckeep_ref,
        start_ref, sems,
    ) = refs[strips:]
    levels, capacity, tracers, child_rows = cnext_hbm.shape
    slot = LANES // tracers
    width = pmid_ref.shape[0] // rows
    narrow = capacity // 3
    covered = child_rows // 3
    all_rows = strips * rows
    tiles = tile_list(child_rows)
    live = capacity * tracers
    stored = up(live, 8)
    padded = up(narrow, 8)
    member = lax.axis_index("child")
    group = lax.axis_index("parent")
    for j, start in enumerate(strip_starts(cols_ref, strips)):
        start_ref[j] = start
    offset = offset_ref[0]
    ends_ref[...] = jnp.zeros_like(ends_ref)
    for q in range(narrow):
        for s in range(strips):
            at = pl.ds(pl.multiple_of(q * all_rows + (member ^ s) * rows, rows), rows)
            panel_ref[at, :] = got_refs[s][q * rows : (q + 1) * rows, :]
        ends_ref[q : q + 1, :] = panel_ref[pl.ds(q * all_rows + offset, 1), :]
        ends_ref[padded + q : padded + q + 1, :] = panel_ref[pl.ds(q * all_rows + offset + covered - 1, 1), :]
    solved_ends = jnp.dot(ends_ref[...], inverse_ref[...], precision=HIGH, preferred_element_type=jnp.float32)
    f = lax.broadcasted_iota(jnp.int32, (covered, 1), 0)
    first_row = (f == 0).astype(jnp.float32)
    last_row = (f == covered - 1).astype(jnp.float32)
    tail, tail_size = tiles[-1]
    packs = LANES // tail_size

    def spread(turned, n, q):
        for t in range(tracers):
            part = turned[t * slot : t * slot + levels]
            for dx in range(3):
                add_ref[n, pl.ds((3 * q + dx) * tracers + t, levels, stride=stored), :] = part

    for q in range(narrow):
        low = solved_ends[q : q + 1]
        high = solved_ends[padded + q : padded + q + 1]
        panel = panel_ref[pl.ds(q * all_rows + offset, covered), :]
        mean = own_ref[pl.ds(q * all_rows + offset, covered), :]
        coarse = mean + diffusion * mean[:, levels : levels + 1] * (first_row * low + last_row * high)
        gap = nudging * (panel - coarse)
        base = q * child_rows
        for dy in range(3):
            long_ref[pl.ds(base + dy, covered, stride=3), :] = gap
        long_ref[base : base + 1, :] = gap[:1] + diffusion * low
        long_ref[base + child_rows - 1 : base + child_rows, :] = gap[covered - 1 :] + diffusion * high
        for n, size in tiles[:-1]:
            spread(long_ref[base + n * LANES : base + n * LANES + size, :].T, n, q)
        at = (q % packs) * tail_size
        end_ref[q // packs, at : at + tail_size, :] = long_ref[base + child_rows - tail_size : base + child_rows, :]
    for part in range((narrow + packs - 1) // packs):
        turned = end_ref[part].T
        for q in range(part * packs, min(narrow, (part + 1) * packs)):
            shift = (q % packs) * tail_size
            spread(pltpu.roll(turned, (LANES - shift) % LANES, 1) if shift else turned, tail, q)

    flat_next = ckeep_ref.reshape(levels * live, child_rows)

    def write(l, carry):
        at = pl.ds(pl.multiple_of(l * stored, 8), live)
        parts = [
            (mask_ref[n, :live, :] * (cmid_ref[n, at, :] + add_ref[n, at, :]))[:, :size] for n, size in tiles
        ]
        flat_next[pl.ds(pl.multiple_of(l * live, 2), live), :] = jnp.concatenate(parts, axis=1)
        return carry

    sends = []
    step = -(-levels // chunks)
    for c in range(chunks):
        low, high = c * step, min(levels, (c + 1) * step)
        lax.fori_loop(low, high, write, 0, unroll=2)
        part = pl.ds(low, high - low)
        sends.append(pltpu.make_async_copy(ckeep_ref.at[part], cnext_hbm.at[part], sems.at[1 + c]))
        sends[-1].start()

    for s in range(strips):
        j = member ^ s
        start, cols = start_ref[j], cols_ref[group, j]
        for q in range(narrow):
            to = jnp.where(q < cols, start + q, width + q)
            wide_ref[pl.ds(pl.multiple_of(to * rows, rows), rows), :] = got_refs[s][
                (narrow + q) * rows : (narrow + q + 1) * rows, :
            ]
    pmid = pmid_ref[...]
    mean = wide_ref[: width * rows, :]
    mean = mean + diffusion * mean[:, levels : levels + 1] * pmid
    coarse = jnp.dot(mean, inverse_ref[...], precision=HIGH, preferred_element_type=jnp.float32)
    row = member * rows + lax.broadcasted_iota(jnp.int32, (width * rows, 1), 0) % rows
    inside = (row >= offset) & (row < offset + covered)
    next_ref[...] = pmid[:, levels : levels + 1] * jnp.where(inside, coarse, pmid)
    for r in range(rows):
        block = next_ref[pl.ds(r, width, stride=rows), :]
        for t in range(tracers):
            pkeep_ref[t, r] = block[:, t * slot : t * slot + levels]
    send_parent = pltpu.make_async_copy(pkeep_ref, pnext_hbm, sems.at[0])
    send_parent.start()
    sends.append(send_parent)
    for send in sends:
        send.wait()


def ring(block, axes, count, step):
    return lax.ppermute(block, axes, [(i, (i + step) % count) for i in range(count)])


def body(parent_tracer, child_tracer, strip_cols, row_offset, parent_wet, child_wet, vert_mix):
    tracers, levels, rows, width = parent_tracer.shape
    capacity, child_rows = child_wet.shape
    strips = lax.axis_size("child")
    narrow = capacity // 3
    all_rows = rows * strips
    tiles = tile_list(child_rows)
    lane_tiles = len(tiles)
    packed = -(-narrow // (LANES // tiles[-1][1]))
    stored = up(capacity * tracers, 8)
    stride = stored + 16
    chunks = 5
    message = lane_tiles * up(tracers * levels, 8) + width
    f32 = lambda *s: jax.ShapeDtypeStruct(s, jnp.float32)
    mem = lambda *s: pltpu.VMEM(s, jnp.float32)
    parent = jnp.transpose(parent_tracer, (0, 2, 3, 1))
    child = jnp.transpose(child_tracer, (1, 2, 0, 3))

    flat, forth, back, left_edge, right_edge, weight, carry, below, inverse = pl.pallas_call(
        prepare_kernel,
        in_specs=[HBM] * 6,
        out_specs=[VM] * 9,
        out_shape=[
            f32(width * rows, LANES), f32(message, LANES), f32(message, LANES), f32(rows, LANES), f32(rows, LANES),
            f32(8 * levels, LANES), f32(8 * levels, LANES), f32(8 * levels, LANES), f32(LANES, LANES),
        ],
        scratch_shapes=[
            pltpu.SMEM(strip_cols.shape, jnp.int32),
            pltpu.SMEM(vert_mix.shape, jnp.float32),
            mem(*parent.shape),
            pltpu.VMEM(parent_wet.shape, jnp.int32),
            pltpu.VMEM(child_wet.shape, jnp.int32),
            mem(2, levels, 1, tracers, child_rows),
            mem(LANES, LANES),
            mem(rows, width, LANES),
            mem(8 * levels, LANES),
            mem(8 * levels, LANES),
            pltpu.SemaphoreType.DMA((7,)),
        ],
        compiler_params=params(16),
        name="prepare",
    )(*(in_hbm(x) for x in (strip_cols, vert_mix, parent, parent_wet, child, child_wet)))

    groups = lax.axis_size("parent")
    devices = groups * strips
    right_edge = ring(right_edge, "parent", groups, 1)
    left_edge = ring(left_edge, "parent", groups, -1)
    forth = ring(forth, ("parent", "child"), devices, 1)
    back = ring(back, ("parent", "child"), devices, -1)

    explicit, mask = pl.pallas_call(
        inner_kernel,
        in_specs=[SM, VM, VM],
        out_specs=[VM] * 2,
        out_shape=[f32(lane_tiles, levels * stored, LANES), f32(lane_tiles, stored, LANES)],
        scratch_shapes=[mem(lane_tiles, levels * stride, LANES)],
        compiler_params=params(16),
        name="inner",
    )(strip_cols, child, child_wet)

    block = f32(2 * narrow * rows, LANES)
    *blocks, parent_mid, own, halo = pl.pallas_call(
        functools.partial(pack_kernel, groups, strips, rows, tracers, levels),
        in_specs=[SM, SM] + [VM] * 8,
        out_specs=[VM] * (strips + 3),
        out_shape=[block] * strips
        + [f32(width * rows, LANES), f32(narrow * all_rows, LANES), f32(lane_tiles, 8 * levels, LANES)],
        scratch_shapes=[
            mem(width * rows, LANES),
            mem((width + narrow) * rows, LANES),
            mem(LANES, LANES),
            mem(packed, LANES, LANES),
            mem(narrow * child_rows, LANES),
            pltpu.SMEM((strips,), jnp.int32),
        ],
        compiler_params=params(16),
        name="pack",
    )(strip_cols, row_offset, flat, forth, back, right_edge, left_edge, inverse, explicit, child_wet)

    got = {0: blocks[0]}
    for s in far_first(strips)[:-1]:
        got[s] = lax.ppermute(blocks[s], "child", [(i, i ^ s) for i in range(strips)])
    got = [got[s] for s in far_first(strips)]

    child_mid, mean = pl.pallas_call(
        functools.partial(level_kernel, tracers, levels, capacity),
        in_specs=[SM] + [VM] * 7,
        out_specs=[VM, VM],
        out_shape=[f32(lane_tiles, levels * stored, LANES), f32(narrow * all_rows, LANES)],
        scratch_shapes=[mem(lane_tiles, levels * stored, LANES), mem(lane_tiles, 8 * levels, LANES)],
        compiler_params=params(16),
        name="levels",
    )(strip_cols, weight, carry, below, inverse, explicit, halo, own)

    parent_next, child_next = pl.pallas_call(
        functools.partial(finish_kernel, strips, rows, chunks),
        in_specs=[SM, SM] + [VM] * (5 + strips),
        out_specs=[HBM, HBM],
        out_shape=[f32(*parent.shape), f32(*child.shape)],
        scratch_shapes=[
            mem(narrow * all_rows, LANES),
            mem((width + narrow) * rows, LANES),
            mem(2 * up(narrow, 8), LANES),
            mem(narrow * child_rows, LANES),
            mem(packed, LANES, LANES),
            mem(lane_tiles, levels * stored, LANES),
            mem(width * rows, LANES),
            mem(*parent.shape),
            mem(*child.shape),
            pltpu.SMEM((strips,), jnp.int32),
            pltpu.SemaphoreType.DMA((1 + chunks,)),
        ],
        compiler_params=params(24),
        name="finish",
    )(strip_cols, row_offset, mean, parent_mid, inverse, child_mid, mask, *got)
    return jnp.transpose(parent_next, (0, 3, 1, 2)), jnp.transpose(child_next, (2, 0, 1, 3))


def solution(mesh):
    return jax.shard_map(
        body,
        mesh=mesh,
        in_specs=(
            P(None, None, "child", "parent"),
            P(None, None, ("parent", "child"), None),
            P(),
            P(),
            P("child", "parent"),
            P(("parent", "child"), None),
            P(),
        ),
        out_specs=(P(None, None, "child", "parent"), P(None, None, ("parent", "child"), None)),
        check_vma=False,
    )
```

```python
import functools

import jax
import jax.numpy as jnp
from jax import lax
from jax.experimental import pallas as pl
from jax.experimental.pallas import tpu as pltpu
from jax.sharding import PartitionSpec as P

diffusion = 0.2
nudging = 0.5
one_ninth = 1.0 / 9.0
LANES = 128
HIGH = lax.Precision.HIGHEST

VM = pl.BlockSpec(memory_space=pltpu.VMEM)
SM = pl.BlockSpec(memory_space=pltpu.SMEM)
HBM = pl.BlockSpec(memory_space=pltpu.HBM)


def params(mib):
    return pltpu.CompilerParams(vmem_limit_bytes=mib << 20)


def in_hbm(x):
    return pltpu.with_memory_space_constraint(x, pltpu.HBM)


def far_first(strips):
    return list(reversed(range(strips)))


def up(n, m):
    return (n + m - 1) // m * m


def tile_list(child_rows):
    return [(t, min(LANES, child_rows - t * LANES)) for t in range((child_rows + LANES - 1) // LANES)]


def my_cols(cols_ref):
    return cols_ref[lax.axis_index("parent"), lax.axis_index("child")]


def strip_starts(cols_ref, strips):
    group = lax.axis_index("parent")
    start = jnp.int32(0)
    starts = []
    for j in range(strips):
        starts.append(start)
        start = start + cols_ref[group, j]
    return starts


def coefficients(mix_ref, weight_ref, carry_ref, back_ref, inverse_ref, d_ref, c_ref):
    tracers, levels = mix_ref.shape[0], mix_ref.shape[1] + 1
    slot = LANES // tracers
    lane = lax.broadcasted_iota(jnp.int32, (8, LANES), 1)
    by_lane = lane // slot
    by_row = lax.broadcasted_iota(jnp.int32, (8, LANES), 0) % tracers
    none = jnp.zeros((8, LANES), jnp.float32)

    def mixed(k, which):
        row = none
        if 0 <= k < levels - 1:
            for t in range(tracers):
                row = jnp.where(which == t, mix_ref[t, k], row)
        return row

    weights = [none, none]
    d = none
    for k in range(levels):
        for n, which in enumerate((by_row, by_lane)):
            above, below = mixed(k - 1, which), mixed(k, which)
            w = 1.0 / (1.0 + above + below - above * (above * weights[n]))
            weights[n] = w
            at = pl.ds(8 * k, 8)
            if n == 0:
                weight_ref[at, :] = w
                carry_ref[at, :] = above * w
                back_ref[at, :] = below * w
            else:
                unit = (lane - which * slot == k).astype(jnp.float32)
                d = (unit + above * d) * w
                d_ref[at, :] = d
                c_ref[at, :] = below * w
    inverse_ref[...] = jnp.zeros_like(inverse_ref)
    x = none
    for k in reversed(range(levels)):
        x = d_ref[pl.ds(8 * k, 8), :] + c_ref[pl.ds(8 * k, 8), :] * x
        for t in range(tracers):
            inverse_ref[t * slot + k : t * slot + k + 1, :] = jnp.where(by_lane == t, x, 0.0)[:1]


def prepare_kernel(
    cols_hbm, mix_hbm, parent_hbm, pwet_hbm, child_hbm, cwet_hbm,
    flat_ref, forth_ref, back_ref, left_ref, right_ref, weight_ref, carry_ref, below_ref, inverse_ref, again_ref,
    cols_ref, mix_ref, parent_ref, pwet_ref, cwet_ref, edge_ref, turn_ref, row_ref, d_ref, c_ref, sems,
):
    levels, capacity, tracers, child_rows = child_hbm.shape
    rows, width = pwet_ref.shape
    slot = LANES // tracers
    level_rows = up(tracers * levels, 8)
    tiles = tile_list(child_rows)
    fetch_cols = pltpu.make_async_copy(cols_hbm, cols_ref, sems.at[0])
    fetch_pwet = pltpu.make_async_copy(pwet_hbm, pwet_ref, sems.at[1])
    fetch_parent = pltpu.make_async_copy(parent_hbm, parent_ref, sems.at[2])
    fetch_cwet = pltpu.make_async_copy(cwet_hbm, cwet_ref, sems.at[3])
    fetch_first = pltpu.make_async_copy(child_hbm.at[:, pl.ds(0, 1)], edge_ref.at[1], sems.at[4])
    fetch_mix = pltpu.make_async_copy(mix_hbm, mix_ref, sems.at[6])
    fetch_again = pltpu.make_async_copy(cols_hbm, again_ref, sems.at[7])
    for fetch in (fetch_cols, fetch_mix, fetch_again, fetch_pwet, fetch_parent, fetch_first, fetch_cwet):
        fetch.start()
    fetch_cols.wait()
    last = 3 * my_cols(cols_ref) - 1
    fetch_last = pltpu.make_async_copy(child_hbm.at[:, pl.ds(last, 1)], edge_ref.at[0], sems.at[5])
    fetch_last.start()
    row_ref[...] = jnp.zeros_like(row_ref)
    fetch_mix.wait()
    coefficients(mix_ref, weight_ref, carry_ref, below_ref, inverse_ref, d_ref, c_ref)
    fetch_pwet.wait()
    turn_ref[:rows, :width] = pwet_ref[...].astype(jnp.float32)
    wet = turn_ref[...].T
    fetch_parent.wait()
    for r in range(rows):
        cell = wet[:width, r : r + 1]
        for t in range(tracers):
            row_ref[r, :, t * slot : t * slot + levels] = cell * parent_ref[t, r]
        row_ref[r, :, levels : levels + 1] = cell
        flat_ref[pl.ds(r, width, stride=rows), :] = row_ref[r]
    left_ref[...] = flat_ref[:rows, :]
    right_ref[...] = flat_ref[(width - 1) * rows :, :]
    fetch_cwet.wait()
    fetch_again.wait()
    base = len(tiles) * level_rows
    fetch_first.wait()
    fetch_last.wait()
    for side, (ref, x, r) in enumerate(((forth_ref, last, rows - 1), (back_ref, 0, 0))):
        cell = cwet_ref[pl.ds(x, 1), :].astype(jnp.float32)
        pairs = edge_ref.at[side].reshape(levels * tracers, child_rows)[...] * cell
        for n, size in tiles:
            ref[n * level_rows : n * level_rows + levels * tracers, :size] = pairs[:, n * LANES : n * LANES + size]
        ref[base : base + width, :] = row_ref[r]


def masks(cols_ref, cwet_ref, mask_ref, tracers):
    capacity, child_rows = cwet_ref.shape
    column = lax.broadcasted_iota(jnp.int32, (capacity, 1), 0)
    mask = cwet_ref[...].astype(jnp.float32) * (column < 3 * my_cols(cols_ref)).astype(jnp.float32)
    mask_ref[...] = jnp.zeros_like(mask_ref)
    for n, size in tile_list(child_rows):
        part = mask[:, n * LANES : n * LANES + size]
        if size < LANES:
            part = jnp.concatenate([part, jnp.zeros((capacity, LANES - size), jnp.float32)], axis=1)
        for t in range(tracers):
            mask_ref[n, pl.ds(t, capacity, stride=tracers), :] = part
    return mask


def inner_kernel(
    cols_ref, child_ref, cwet_ref,
    explicit_ref, mask_ref,
    begin_ref,
):
    levels, capacity, tracers, child_rows = child_ref.shape
    tiles = tile_list(child_rows)
    live = capacity * tracers
    stored = up(live, 8)
    stride = begin_ref.shape[1] // levels
    masks(cols_ref, cwet_ref, mask_ref, tracers)
    flat_child = child_ref.reshape(levels * live, child_rows)
    lane = lax.broadcasted_iota(jnp.int32, (stored, LANES), 1)
    gap = jnp.zeros((tracers, LANES), jnp.float32)
    after = stored - live + tracers

    def explicit(l, carry):
        cells = flat_child[pl.ds(pl.multiple_of(l * live, 2), live), :]
        start = pl.multiple_of(l * stride, 8)
        for n, size in tiles:
            part = cells[:, n * LANES : n * LANES + size] * mask_ref[n, :live, :size]
            if size < LANES:
                part = jnp.concatenate([part, jnp.zeros((live, LANES - size), jnp.float32)], axis=1)
            begin_ref[n, pl.ds(start + 8, live), :] = part
            begin_ref[n, pl.ds(start + 8 - tracers, tracers), :] = gap
            begin_ref[n, pl.ds(start + 8 + live, after), :] = jnp.zeros((after, LANES), jnp.float32)
        here = [begin_ref[n, pl.ds(start + 8, stored), :] for n, _ in tiles]
        lower = [pltpu.roll(c, 1, 1) for c in here]
        upper = [pltpu.roll(c, LANES - 1, 1) for c in here]
        for n, size in tiles:
            south = jnp.where(lane == 0, lower[n - 1] if n else 0.0, lower[n])
            if n + 1 < len(tiles):
                north = jnp.where(lane == LANES - 1, upper[n + 1], upper[n])
            else:
                north = jnp.where(lane == size - 1, 0.0, upper[n])
            west = begin_ref[n, pl.ds(start + 8 - tracers, stored), :]
            east = begin_ref[n, pl.ds(start + 8 + tracers, stored), :]
            explicit_ref[n, pl.ds(pl.multiple_of(l * stored, 8), stored), :] = (diffusion * mask_ref[n, :stored, :]) * (
                here[n] + west + east + south + north
            )
        return carry

    lax.fori_loop(0, levels, explicit, 0, unroll=25 if levels % 25 == 0 else 1)


def pack_kernel(
    groups, strips, rows, tracers, levels,
    cols_ref, offset_ref, flat_ref, before_ref, after_ref, left_ref, right_ref, inverse_ref, explicit_ref, cwet_ref,
    *refs,
):
    send_refs = refs[:strips]
    pmid_ref, own_ref, halo_ref, step_ref, wide_ref, turn_ref, end_ref, long_ref, start_ref = refs[strips:]
    capacity, child_rows = cwet_ref.shape
    stored = up(capacity * tracers, 8)
    slot = LANES // tracers
    width = flat_ref.shape[0] // rows
    narrow = capacity // 3
    covered = child_rows // 3
    all_rows = strips * rows
    tiles = tile_list(child_rows)
    level_rows = up(tracers * levels, 8)
    base = len(tiles) * level_rows
    group, member = lax.axis_index("parent"), lax.axis_index("child")
    offset = offset_ref[0]
    cols = my_cols(cols_ref)
    for j, start in enumerate(strip_starts(cols_ref, strips)):
        start_ref[j] = start

    has_before = (member > 0).astype(jnp.float32)
    has_after = (member < strips - 1).astype(jnp.float32)
    has_left = (group > 0).astype(jnp.float32)
    has_right = (group < groups - 1).astype(jnp.float32)
    for x in range(width):
        here = flat_ref[x * rows : (x + 1) * rows, :]
        west = has_left * left_ref[...] if x == 0 else flat_ref[(x - 1) * rows : x * rows, :]
        east = has_right * right_ref[...] if x == width - 1 else flat_ref[(x + 1) * rows : (x + 2) * rows, :]
        south = jnp.concatenate([has_before * before_ref[base + x : base + x + 1, :], here[:-1]], axis=0)
        north = jnp.concatenate([here[1:], has_after * after_ref[base + x : base + x + 1, :]], axis=0)
        wet = here[:, levels : levels + 1]
        laplace = north + south + east + west - 4.0 * here
        step_ref[x * rows : (x + 1) * rows, :] = wet * (here + diffusion * laplace)
    solved = jnp.dot(step_ref[...], inverse_ref[...], precision=HIGH, preferred_element_type=jnp.float32)
    lane = lax.broadcasted_iota(jnp.int32, (width * rows, LANES), 1)
    solved = jnp.where(lane == levels, flat_ref[...], solved)
    wide_ref[: width * rows, :] = solved
    wide_ref[width * rows :, :] = jnp.zeros((narrow * rows, LANES), jnp.float32)
    pmid_ref[...] = solved
    for s in range(strips):
        start = start_ref[member ^ s]
        send_refs[s][: narrow * rows, :] = wide_ref[pl.ds(pl.multiple_of(start * rows, rows), narrow * rows), :]

    column = lax.broadcasted_iota(jnp.int32, (capacity, 1), 0)
    mask = cwet_ref[...].astype(jnp.float32) * (column < 3 * cols).astype(jnp.float32)
    west_mask = (diffusion * jnp.maximum(has_before, has_left)) * mask[:1]
    east_wet = cwet_ref[pl.ds(3 * cols - 1, 1), :].astype(jnp.float32)
    east_mask = (diffusion * jnp.maximum(has_after, has_right)) * east_wet
    halo_ref[...] = jnp.zeros_like(halo_ref)
    for n, size in tiles:
        part = slice(n * LANES, n * LANES + size)
        for l in range(levels):
            edge = slice(n * level_rows + l * tracers, n * level_rows + (l + 1) * tracers)
            halo_ref[n, 8 * l : 8 * l + tracers, :size] = west_mask[:, part] * before_ref[edge, :size]
            halo_ref[n, 8 * l + tracers : 8 * l + 2 * tracers, :size] = east_mask[:, part] * after_ref[edge, :size]

    own_ref[...] = jnp.zeros_like(own_ref)
    turn_ref[...] = jnp.zeros_like(turn_ref)
    end_ref[...] = jnp.zeros_like(end_ref)
    y = lax.broadcasted_iota(jnp.int32, (1, child_rows), 1)
    at_end = ((y == 0) | (y == child_rows - 1)).astype(jnp.float32)
    tail, tail_size = tiles[-1]
    packs = LANES // tail_size
    for q in range(narrow):
        count = (mask[3 * q : 3 * q + 1] + mask[3 * q + 1 : 3 * q + 2] + mask[3 * q + 2 : 3 * q + 3]) * at_end
        is_last = (cols == q + 1).astype(jnp.float32)
        for n, size in tiles:
            into, low = (turn_ref, 0) if n < tail else (end_ref.at[q // packs], (q % packs) * size)
            for t in range(tracers):
                part = is_last * halo_ref[n, pl.ds(tracers + t, levels, stride=8), :]
                if q == 0:
                    part = part + halo_ref[n, pl.ds(t, levels, stride=8), :]
                for dx in range(3):
                    part = part + explicit_ref[n, pl.ds((3 * q + dx) * tracers + t, levels, stride=stored), :]
                into[t * slot : t * slot + levels, low : low + size] = part[:, :size]
            into[levels : levels + 1, low : low + size] = count[:, n * LANES : n * LANES + size]
            if n < tail:
                long_ref[q * child_rows + n * LANES : q * child_rows + n * LANES + size, :] = turn_ref[...].T
    for part in range((narrow + packs - 1) // packs):
        turned = end_ref[part].T
        for q in range(part * packs, min(narrow, (part + 1) * packs)):
            low = (q % packs) * tail_size
            high = (q + 1) * child_rows
            long_ref[high - tail_size : high, :] = turned[low : low + tail_size]
    for q in range(narrow):
        mean = one_ninth * (
            long_ref[pl.ds(q * child_rows, covered, stride=3), :]
            + long_ref[pl.ds(q * child_rows + 1, covered, stride=3), :]
            + long_ref[pl.ds(q * child_rows + 2, covered, stride=3), :]
        )
        own_ref[pl.ds(q * all_rows + offset, covered), :] = mean
    for s in range(strips):
        band = (member ^ s) * rows
        for q in range(narrow):
            send_refs[s][(narrow + q) * rows : (narrow + q + 1) * rows, :] = own_ref[
                pl.ds(pl.multiple_of(q * all_rows + band, rows), rows), :
            ]


def level_kernel(
    tracers, levels, capacity,
    cols_ref, weight_ref, carry_ref, back_ref, inverse_ref, explicit_ref, halo_ref, own_ref,
    cmid_ref, mean_ref,
    d_ref, h_ref,
):
    count = explicit_ref.shape[0]
    stored = up(capacity * tracers, 8)
    past = 3 * tracers * my_cols(cols_ref) - tracers

    def by_rows(factor, value):
        return (factor[None] * value.reshape(stored // 8, 8, LANES)).reshape(stored, LANES)

    def forward(l, carry):
        at = pl.ds(pl.multiple_of(l * stored, 8), stored)
        coef = pl.ds(pl.multiple_of(l * 8, 8), 8)
        weight, above = weight_ref[coef, :], carry_ref[coef, :]
        held = []
        for n in range(count):
            d = by_rows(weight, explicit_ref[n, at, :]) + by_rows(above, carry[2 * n])
            h = weight * halo_ref[n, coef, :] + above * carry[2 * n + 1]
            d_ref[n, at, :] = d
            h_ref[n, coef, :] = h
            held += [d, h]
        return tuple(held)

    blank = (jnp.zeros((stored, LANES), jnp.float32), jnp.zeros((8, LANES), jnp.float32)) * count
    unroll = 5 if levels % 5 == 0 else 1
    lax.fori_loop(0, levels, forward, blank, unroll=unroll)

    def backward(step, carry):
        l = levels - 1 - step
        start = pl.multiple_of(l * stored, 8)
        at = pl.ds(start, stored)
        coef = pl.ds(pl.multiple_of(l * 8, 8), 8)
        below = back_ref[coef, :]
        held = []
        for n in range(count):
            x = d_ref[n, at, :] + by_rows(below, carry[2 * n])
            h = h_ref[n, coef, :] + below * carry[2 * n + 1]
            cmid_ref[n, at, :] = x
            first = pl.ds(start, tracers)
            cmid_ref[n, first, :] = cmid_ref[n, first, :] + h[:tracers]
            last = pl.ds(start + past, tracers)
            cmid_ref[n, last, :] = cmid_ref[n, last, :] + h[tracers : 2 * tracers]
            held += [x, h]
        return tuple(held)

    lax.fori_loop(0, levels, backward, blank, unroll=unroll)
    own = own_ref[...]
    solved = jnp.dot(own, inverse_ref[...], precision=HIGH, preferred_element_type=jnp.float32)
    lane = lax.broadcasted_iota(jnp.int32, own.shape, 1)
    mean_ref[...] = jnp.where(lane == levels, own, solved)


def finish_kernel(
    strips, rows, chunks,
    cols_ref, offset_ref, own_ref, pmid_ref, inverse_ref, cmid_ref, mask_ref,
    *refs,
):
    got_refs = {s: ref for s, ref in zip(far_first(strips), refs)}
    (
        pnext_hbm, cnext_hbm,
        panel_ref, wide_ref, ends_ref, long_ref, end_ref, add_ref, next_ref, pkeep_ref, ckeep_ref,
        start_ref, sems,
    ) = refs[strips:]
    levels, capacity, tracers, child_rows = cnext_hbm.shape
    slot = LANES // tracers
    width = pmid_ref.shape[0] // rows
    narrow = capacity // 3
    covered = child_rows // 3
    all_rows = strips * rows
    tiles = tile_list(child_rows)
    live = capacity * tracers
    stored = up(live, 8)
    padded = up(narrow, 8)
    member = lax.axis_index("child")
    group = lax.axis_index("parent")
    for j, start in enumerate(strip_starts(cols_ref, strips)):
        start_ref[j] = start
    offset = offset_ref[0]
    ends_ref[...] = jnp.zeros_like(ends_ref)
    for q in range(narrow):
        for s in range(strips):
            at = pl.ds(pl.multiple_of(q * all_rows + (member ^ s) * rows, rows), rows)
            panel_ref[at, :] = got_refs[s][q * rows : (q + 1) * rows, :]
        ends_ref[q : q + 1, :] = panel_ref[pl.ds(q * all_rows + offset, 1), :]
        ends_ref[padded + q : padded + q + 1, :] = panel_ref[pl.ds(q * all_rows + offset + covered - 1, 1), :]
    solved_ends = jnp.dot(ends_ref[...], inverse_ref[...], precision=HIGH, preferred_element_type=jnp.float32)
    f = lax.broadcasted_iota(jnp.int32, (covered, 1), 0)
    first_row = (f == 0).astype(jnp.float32)
    last_row = (f == covered - 1).astype(jnp.float32)
    tail, tail_size = tiles[-1]
    packs = LANES // tail_size

    def spread(turned, n, q):
        for t in range(tracers):
            part = turned[t * slot : t * slot + levels]
            for dx in range(3):
                add_ref[n, pl.ds((3 * q + dx) * tracers + t, levels, stride=stored), :] = part

    for q in range(narrow):
        low = solved_ends[q : q + 1]
        high = solved_ends[padded + q : padded + q + 1]
        panel = panel_ref[pl.ds(q * all_rows + offset, covered), :]
        mean = own_ref[pl.ds(q * all_rows + offset, covered), :]
        coarse = mean + diffusion * mean[:, levels : levels + 1] * (first_row * low + last_row * high)
        gap = nudging * (panel - coarse)
        base = q * child_rows
        for dy in range(3):
            long_ref[pl.ds(base + dy, covered, stride=3), :] = gap
        long_ref[base : base + 1, :] = gap[:1] + diffusion * low
        long_ref[base + child_rows - 1 : base + child_rows, :] = gap[covered - 1 :] + diffusion * high
        for n, size in tiles[:-1]:
            spread(long_ref[base + n * LANES : base + n * LANES + size, :].T, n, q)
        at = (q % packs) * tail_size
        end_ref[q // packs, at : at + tail_size, :] = long_ref[base + child_rows - tail_size : base + child_rows, :]
    for part in range((narrow + packs - 1) // packs):
        turned = end_ref[part].T
        for q in range(part * packs, min(narrow, (part + 1) * packs)):
            shift = (q % packs) * tail_size
            spread(pltpu.roll(turned, (LANES - shift) % LANES, 1) if shift else turned, tail, q)

    flat_next = ckeep_ref.reshape((levels + 1) * live, child_rows)

    def write(l, carry):
        at = pl.ds(pl.multiple_of(l * stored, 8), live)
        parts = [
            (mask_ref[n, :live, :] * (cmid_ref[n, at, :] + add_ref[n, at, :]))[:, :size] for n, size in tiles
        ]
        flat_next[pl.ds(pl.multiple_of(l * live, 2), live), :] = jnp.concatenate(parts, axis=1)
        return carry

    sends = []
    step = -(-levels // chunks)
    for c in range(chunks):
        low, high = c * step, min(levels, (c + 1) * step)
        lax.fori_loop(low, high, write, 0, unroll=2)
        part = pl.ds(low, high - low)
        sends.append(pltpu.make_async_copy(ckeep_ref.at[part], cnext_hbm.at[part], sems.at[1 + c]))
        sends[-1].start()

    for s in range(strips):
        j = member ^ s
        start, cols = start_ref[j], cols_ref[group, j]
        for q in range(narrow):
            to = jnp.where(q < cols, start + q, width + q)
            wide_ref[pl.ds(pl.multiple_of(to * rows, rows), rows), :] = got_refs[s][
                (narrow + q) * rows : (narrow + q + 1) * rows, :
            ]
    pmid = pmid_ref[...]
    mean = wide_ref[: width * rows, :]
    mean = mean + diffusion * mean[:, levels : levels + 1] * pmid
    coarse = jnp.dot(mean, inverse_ref[...], precision=HIGH, preferred_element_type=jnp.float32)
    row = member * rows + lax.broadcasted_iota(jnp.int32, (width * rows, 1), 0) % rows
    inside = (row >= offset) & (row < offset + covered)
    next_ref[...] = pmid[:, levels : levels + 1] * jnp.where(inside, coarse, pmid)
    for r in range(rows):
        block = next_ref[pl.ds(r, width, stride=rows), :]
        for t in range(tracers):
            pkeep_ref[t, r] = block[:, t * slot : t * slot + levels]
    send_parent = pltpu.make_async_copy(pkeep_ref, pnext_hbm, sems.at[0])
    send_parent.start()
    sends.append(send_parent)
    for send in sends:
        send.wait()


def ring(block, axes, count, step):
    return lax.ppermute(block, axes, [(i, (i + step) % count) for i in range(count)])


def body(parent_tracer, child_tracer, strip_cols, row_offset, parent_wet, child_wet, vert_mix):
    tracers, levels, rows, width = parent_tracer.shape
    capacity, child_rows = child_wet.shape
    strips = lax.axis_size("child")
    narrow = capacity // 3
    all_rows = rows * strips
    tiles = tile_list(child_rows)
    lane_tiles = len(tiles)
    packed = -(-narrow // (LANES // tiles[-1][1]))
    stored = up(capacity * tracers, 8)
    stride = stored + 16
    plane = up(levels, 8) * stored
    chunks = 5
    message = lane_tiles * up(tracers * levels, 8) + width
    f32 = lambda *s: jax.ShapeDtypeStruct(s, jnp.float32)
    mem = lambda *s: pltpu.VMEM(s, jnp.float32)
    parent = jnp.transpose(parent_tracer, (0, 2, 3, 1))
    child = jnp.transpose(child_tracer, (1, 2, 0, 3))

    flat, forth, back, left_edge, right_edge, weight, carry, below, inverse, cols = pl.pallas_call(
        prepare_kernel,
        in_specs=[HBM] * 6,
        out_specs=[VM] * 10,
        out_shape=[
            f32(width * rows, LANES), f32(message, LANES), f32(message, LANES), f32(rows, LANES), f32(rows, LANES),
            f32(8 * levels, LANES), f32(8 * levels, LANES), f32(8 * levels, LANES), f32(LANES, LANES),
            jax.ShapeDtypeStruct(strip_cols.shape, jnp.int32),
        ],
        scratch_shapes=[
            pltpu.SMEM(strip_cols.shape, jnp.int32),
            pltpu.SMEM(vert_mix.shape, jnp.float32),
            mem(*parent.shape),
            pltpu.VMEM(parent_wet.shape, jnp.int32),
            pltpu.VMEM(child_wet.shape, jnp.int32),
            mem(2, levels, 1, tracers, child_rows),
            mem(LANES, LANES),
            mem(rows, width, LANES),
            mem(8 * levels, LANES),
            mem(8 * levels, LANES),
            pltpu.SemaphoreType.DMA((8,)),
        ],
        compiler_params=params(16),
        name="prepare",
    )(*(in_hbm(x) for x in (strip_cols, vert_mix, parent, parent_wet, child, child_wet)))

    groups = lax.axis_size("parent")
    devices = groups * strips
    right_edge = ring(right_edge, "parent", groups, 1)
    left_edge = ring(left_edge, "parent", groups, -1)
    forth = ring(forth, ("parent", "child"), devices, 1)
    back = ring(back, ("parent", "child"), devices, -1)

    explicit, mask = pl.pallas_call(
        inner_kernel,
        in_specs=[SM, VM, VM],
        out_specs=[VM] * 2,
        out_shape=[f32(lane_tiles, plane, LANES), f32(lane_tiles, stored + 8, LANES)],
        scratch_shapes=[mem(lane_tiles, levels * stride, LANES)],
        compiler_params=params(16),
        name="inner",
    )(cols, child, child_wet)

    block = f32(2 * narrow * rows, LANES)
    *blocks, parent_mid, own, halo = pl.pallas_call(
        functools.partial(pack_kernel, groups, strips, rows, tracers, levels),
        in_specs=[SM, SM] + [VM] * 8,
        out_specs=[VM] * (strips + 3),
        out_shape=[block] * strips
        + [f32(width * rows, LANES), f32(narrow * all_rows, LANES), f32(lane_tiles, 8 * up(levels, 8), LANES)],
        scratch_shapes=[
            mem(width * rows, LANES),
            mem((width + narrow) * rows, LANES),
            mem(LANES, LANES),
            mem(packed, LANES, LANES),
            mem(narrow * child_rows, LANES),
            pltpu.SMEM((strips,), jnp.int32),
        ],
        compiler_params=params(16),
        name="pack",
    )(cols, row_offset, flat, forth, back, right_edge, left_edge, inverse, explicit, child_wet)

    got = {0: blocks[0]}
    for s in far_first(strips)[:-1]:
        got[s] = lax.ppermute(blocks[s], "child", [(i, i ^ s) for i in range(strips)])
    got = [got[s] for s in far_first(strips)]

    child_mid, mean = pl.pallas_call(
        functools.partial(level_kernel, tracers, levels, capacity),
        in_specs=[SM] + [VM] * 7,
        out_specs=[VM, VM],
        out_shape=[f32(lane_tiles, plane, LANES), f32(narrow * all_rows, LANES)],
        scratch_shapes=[mem(lane_tiles, levels * stored, LANES), mem(lane_tiles, 8 * levels, LANES)],
        compiler_params=params(16),
        name="levels",
    )(cols, weight, carry, below, inverse, explicit, halo, own)

    parent_next, child_next = pl.pallas_call(
        functools.partial(finish_kernel, strips, rows, chunks),
        in_specs=[SM, SM] + [VM] * (5 + strips),
        out_specs=[HBM, HBM],
        out_shape=[f32(*parent.shape), f32(*child.shape)],
        scratch_shapes=[
            mem(narrow * all_rows, LANES),
            mem((width + narrow) * rows, LANES),
            mem(2 * up(narrow, 8), LANES),
            mem(narrow * child_rows, LANES),
            mem(packed, LANES, LANES),
            mem(lane_tiles, plane, LANES),
            mem(width * rows, LANES),
            mem(*parent.shape),
            mem(levels + 1, *child.shape[1:]),
            pltpu.SMEM((strips,), jnp.int32),
            pltpu.SemaphoreType.DMA((1 + chunks,)),
        ],
        compiler_params=params(24),
        name="finish",
    )(cols, row_offset, mean, parent_mid, inverse, child_mid, mask, *got)
    return jnp.transpose(parent_next, (0, 3, 1, 2)), jnp.transpose(child_next, (2, 0, 1, 3))


def solution(mesh):
    return jax.shard_map(
        body,
        mesh=mesh,
        in_specs=(
            P(None, None, "child", "parent"),
            P(None, None, ("parent", "child"), None),
            P(),
            P(),
            P("child", "parent"),
            P(("parent", "child"), None),
            P(),
        ),
        out_specs=(P(None, None, "child", "parent"), P(None, None, ("parent", "child"), None)),
        check_vma=False,
    )
```

```python
import functools

import jax
import jax.numpy as jnp
from jax import lax
from jax.experimental import pallas as pl
from jax.experimental.pallas import tpu as pltpu
from jax.sharding import PartitionSpec as P

diffusion = 0.2
nudging = 0.5
one_ninth = 1.0 / 9.0
LANES = 128
HIGH = lax.Precision.HIGHEST

VM = pl.BlockSpec(memory_space=pltpu.VMEM)
SM = pl.BlockSpec(memory_space=pltpu.SMEM)
HBM = pl.BlockSpec(memory_space=pltpu.HBM)


def params(mib):
    return pltpu.CompilerParams(vmem_limit_bytes=mib << 20)


def in_hbm(x):
    return pltpu.with_memory_space_constraint(x, pltpu.HBM)


def far_first(strips):
    return list(reversed(range(strips)))


def up(n, m):
    return (n + m - 1) // m * m


def tile_list(child_rows):
    return [(t, min(LANES, child_rows - t * LANES)) for t in range((child_rows + LANES - 1) // LANES)]


def my_cols(cols_ref):
    return cols_ref[lax.axis_index("parent"), lax.axis_index("child")]


def strip_starts(cols_ref, strips):
    group = lax.axis_index("parent")
    start = jnp.int32(0)
    starts = []
    for j in range(strips):
        starts.append(start)
        start = start + cols_ref[group, j]
    return starts


def coefficients(mix_ref, weight_ref, carry_ref, back_ref, inverse_ref, d_ref, c_ref):
    tracers, levels = mix_ref.shape[0], mix_ref.shape[1] + 1
    slot = LANES // tracers
    lane = lax.broadcasted_iota(jnp.int32, (8, LANES), 1)
    by_lane = lane // slot
    by_row = lax.broadcasted_iota(jnp.int32, (8, LANES), 0) % tracers
    none = jnp.zeros((8, LANES), jnp.float32)

    def mixed(k, which):
        row = none
        if 0 <= k < levels - 1:
            for t in range(tracers):
                row = jnp.where(which == t, mix_ref[t, k], row)
        return row

    weights = [none, none]
    d = none
    for k in range(levels):
        for n, which in enumerate((by_row, by_lane)):
            above, below = mixed(k - 1, which), mixed(k, which)
            w = 1.0 / (1.0 + above + below - above * (above * weights[n]))
            weights[n] = w
            at = pl.ds(8 * k, 8)
            if n == 0:
                weight_ref[at, :] = w
                carry_ref[at, :] = above * w
                back_ref[at, :] = below * w
            else:
                unit = (lane - which * slot == k).astype(jnp.float32)
                d = (unit + above * d) * w
                d_ref[at, :] = d
                c_ref[at, :] = below * w
    inverse_ref[...] = jnp.zeros_like(inverse_ref)
    x = none
    for k in reversed(range(levels)):
        x = d_ref[pl.ds(8 * k, 8), :] + c_ref[pl.ds(8 * k, 8), :] * x
        for t in range(tracers):
            inverse_ref[t * slot + k : t * slot + k + 1, :] = jnp.where(by_lane == t, x, 0.0)[:1]


def prepare_kernel(
    cols_hbm, mix_hbm, parent_hbm, pwet_hbm, child_hbm, cwet_hbm,
    flat_ref, forth_ref, back_ref, left_ref, right_ref, weight_ref, carry_ref, below_ref, inverse_ref, again_ref,
    mask_ref,
    cols_ref, mix_ref, parent_ref, pwet_ref, cwet_ref, edge_ref, turn_ref, row_ref, d_ref, c_ref, sems,
):
    levels, capacity, tracers, child_rows = child_hbm.shape
    rows, width = pwet_ref.shape
    slot = LANES // tracers
    level_rows = up(tracers * levels, 8)
    tiles = tile_list(child_rows)
    fetch_cols = pltpu.make_async_copy(cols_hbm, cols_ref, sems.at[0])
    fetch_pwet = pltpu.make_async_copy(pwet_hbm, pwet_ref, sems.at[1])
    fetch_parent = pltpu.make_async_copy(parent_hbm, parent_ref, sems.at[2])
    fetch_cwet = pltpu.make_async_copy(cwet_hbm, cwet_ref, sems.at[3])
    fetch_first = pltpu.make_async_copy(child_hbm.at[:, pl.ds(0, 1)], edge_ref.at[1], sems.at[4])
    fetch_mix = pltpu.make_async_copy(mix_hbm, mix_ref, sems.at[6])
    fetch_again = pltpu.make_async_copy(cols_hbm, again_ref, sems.at[7])
    for fetch in (fetch_cols, fetch_mix, fetch_again, fetch_pwet, fetch_parent, fetch_first, fetch_cwet):
        fetch.start()
    fetch_cols.wait()
    last = 3 * my_cols(cols_ref) - 1
    fetch_last = pltpu.make_async_copy(child_hbm.at[:, pl.ds(last, 1)], edge_ref.at[0], sems.at[5])
    fetch_last.start()
    row_ref[...] = jnp.zeros_like(row_ref)
    fetch_mix.wait()
    coefficients(mix_ref, weight_ref, carry_ref, below_ref, inverse_ref, d_ref, c_ref)
    fetch_pwet.wait()
    turn_ref[:rows, :width] = pwet_ref[...].astype(jnp.float32)
    wet = turn_ref[...].T
    fetch_parent.wait()
    for r in range(rows):
        cell = wet[:width, r : r + 1]
        for t in range(tracers):
            row_ref[r, :, t * slot : t * slot + levels] = cell * parent_ref[t, r]
        row_ref[r, :, levels : levels + 1] = cell
        flat_ref[pl.ds(r, width, stride=rows), :] = row_ref[r]
    left_ref[...] = flat_ref[:rows, :]
    right_ref[...] = flat_ref[(width - 1) * rows :, :]
    fetch_cwet.wait()
    masks(cols_ref, cwet_ref, mask_ref, tracers)
    fetch_again.wait()
    base = len(tiles) * level_rows
    fetch_first.wait()
    fetch_last.wait()
    for side, (ref, x, r) in enumerate(((forth_ref, last, rows - 1), (back_ref, 0, 0))):
        cell = cwet_ref[pl.ds(x, 1), :].astype(jnp.float32)
        pairs = edge_ref.at[side].reshape(levels * tracers, child_rows)[...] * cell
        for n, size in tiles:
            ref[n * level_rows : n * level_rows + levels * tracers, :size] = pairs[:, n * LANES : n * LANES + size]
        ref[base : base + width, :] = row_ref[r]


def masks(cols_ref, cwet_ref, mask_ref, tracers):
    capacity, child_rows = cwet_ref.shape
    column = lax.broadcasted_iota(jnp.int32, (capacity, 1), 0)
    mask = cwet_ref[...].astype(jnp.float32) * (column < 3 * my_cols(cols_ref)).astype(jnp.float32)
    mask_ref[...] = jnp.zeros_like(mask_ref)
    for n, size in tile_list(child_rows):
        part = mask[:, n * LANES : n * LANES + size]
        if size < LANES:
            part = jnp.concatenate([part, jnp.zeros((capacity, LANES - size), jnp.float32)], axis=1)
        for t in range(tracers):
            mask_ref[n, pl.ds(t, capacity, stride=tracers), :] = part
    return mask


def inner_kernel(
    child_ref, mask_ref,
    explicit_ref,
    begin_ref,
):
    levels, capacity, tracers, child_rows = child_ref.shape
    tiles = tile_list(child_rows)
    live = capacity * tracers
    stored = up(live, 8)
    stride = begin_ref.shape[1] // levels
    flat_child = child_ref.reshape(levels * live, child_rows)
    lane = lax.broadcasted_iota(jnp.int32, (stored, LANES), 1)
    gap = jnp.zeros((tracers, LANES), jnp.float32)
    after = stored - live + tracers

    def explicit(l, carry):
        cells = flat_child[pl.ds(pl.multiple_of(l * live, 2), live), :]
        start = pl.multiple_of(l * stride, 8)
        for n, size in tiles:
            part = cells[:, n * LANES : n * LANES + size] * mask_ref[n, :live, :size]
            if size < LANES:
                part = jnp.concatenate([part, jnp.zeros((live, LANES - size), jnp.float32)], axis=1)
            begin_ref[n, pl.ds(start + 8, live), :] = part
            begin_ref[n, pl.ds(start + 8 - tracers, tracers), :] = gap
            begin_ref[n, pl.ds(start + 8 + live, after), :] = jnp.zeros((after, LANES), jnp.float32)
        here = [begin_ref[n, pl.ds(start + 8, stored), :] for n, _ in tiles]
        lower = [pltpu.roll(c, 1, 1) for c in here]
        upper = [pltpu.roll(c, LANES - 1, 1) for c in here]
        for n, size in tiles:
            south = jnp.where(lane == 0, lower[n - 1] if n else 0.0, lower[n])
            if n + 1 < len(tiles):
                north = jnp.where(lane == LANES - 1, upper[n + 1], upper[n])
            else:
                north = jnp.where(lane == size - 1, 0.0, upper[n])
            west = begin_ref[n, pl.ds(start + 8 - tracers, stored), :]
            east = begin_ref[n, pl.ds(start + 8 + tracers, stored), :]
            explicit_ref[n, pl.ds(pl.multiple_of(l * stored, 8), stored), :] = (diffusion * mask_ref[n, :stored, :]) * (
                here[n] + west + east + south + north
            )
        return carry

    lax.fori_loop(0, levels, explicit, 0, unroll=25 if levels % 25 == 0 else 1)


def pack_kernel(
    groups, strips, rows, tracers, levels,
    cols_ref, offset_ref, flat_ref, before_ref, after_ref, left_ref, right_ref, inverse_ref, explicit_ref, cwet_ref,
    *refs,
):
    send_refs = refs[:strips]
    pmid_ref, own_ref, halo_ref, step_ref, wide_ref, turn_ref, end_ref, long_ref, start_ref = refs[strips:]
    capacity, child_rows = cwet_ref.shape
    stored = up(capacity * tracers, 8)
    slot = LANES // tracers
    width = flat_ref.shape[0] // rows
    narrow = capacity // 3
    covered = child_rows // 3
    all_rows = strips * rows
    tiles = tile_list(child_rows)
    level_rows = up(tracers * levels, 8)
    base = len(tiles) * level_rows
    group, member = lax.axis_index("parent"), lax.axis_index("child")
    offset = offset_ref[0]
    cols = my_cols(cols_ref)
    for j, start in enumerate(strip_starts(cols_ref, strips)):
        start_ref[j] = start

    has_before = (member > 0).astype(jnp.float32)
    has_after = (member < strips - 1).astype(jnp.float32)
    has_left = (group > 0).astype(jnp.float32)
    has_right = (group < groups - 1).astype(jnp.float32)
    for x in range(width):
        here = flat_ref[x * rows : (x + 1) * rows, :]
        west = has_left * left_ref[...] if x == 0 else flat_ref[(x - 1) * rows : x * rows, :]
        east = has_right * right_ref[...] if x == width - 1 else flat_ref[(x + 1) * rows : (x + 2) * rows, :]
        south = jnp.concatenate([has_before * before_ref[base + x : base + x + 1, :], here[:-1]], axis=0)
        north = jnp.concatenate([here[1:], has_after * after_ref[base + x : base + x + 1, :]], axis=0)
        wet = here[:, levels : levels + 1]
        laplace = north + south + east + west - 4.0 * here
        step_ref[x * rows : (x + 1) * rows, :] = wet * (here + diffusion * laplace)
    solved = jnp.dot(step_ref[...], inverse_ref[...], precision=HIGH, preferred_element_type=jnp.float32)
    lane = lax.broadcasted_iota(jnp.int32, (width * rows, LANES), 1)
    solved = jnp.where(lane == levels, flat_ref[...], solved)
    wide_ref[: width * rows, :] = solved
    wide_ref[width * rows :, :] = jnp.zeros((narrow * rows, LANES), jnp.float32)
    pmid_ref[...] = solved
    for s in range(strips):
        start = start_ref[member ^ s]
        send_refs[s][: narrow * rows, :] = wide_ref[pl.ds(pl.multiple_of(start * rows, rows), narrow * rows), :]

    column = lax.broadcasted_iota(jnp.int32, (capacity, 1), 0)
    mask = cwet_ref[...].astype(jnp.float32) * (column < 3 * cols).astype(jnp.float32)
    west_mask = (diffusion * jnp.maximum(has_before, has_left)) * mask[:1]
    east_wet = cwet_ref[pl.ds(3 * cols - 1, 1), :].astype(jnp.float32)
    east_mask = (diffusion * jnp.maximum(has_after, has_right)) * east_wet
    halo_ref[...] = jnp.zeros_like(halo_ref)
    for n, size in tiles:
        part = slice(n * LANES, n * LANES + size)
        for l in range(levels):
            edge = slice(n * level_rows + l * tracers, n * level_rows + (l + 1) * tracers)
            halo_ref[n, 8 * l : 8 * l + tracers, :size] = west_mask[:, part] * before_ref[edge, :size]
            halo_ref[n, 8 * l + tracers : 8 * l + 2 * tracers, :size] = east_mask[:, part] * after_ref[edge, :size]

    own_ref[...] = jnp.zeros_like(own_ref)
    turn_ref[...] = jnp.zeros_like(turn_ref)
    end_ref[...] = jnp.zeros_like(end_ref)
    y = lax.broadcasted_iota(jnp.int32, (1, child_rows), 1)
    at_end = ((y == 0) | (y == child_rows - 1)).astype(jnp.float32)
    tail, tail_size = tiles[-1]
    packs = LANES // tail_size
    for q in range(narrow):
        count = (mask[3 * q : 3 * q + 1] + mask[3 * q + 1 : 3 * q + 2] + mask[3 * q + 2 : 3 * q + 3]) * at_end
        is_last = (cols == q + 1).astype(jnp.float32)
        for n, size in tiles:
            into, low = (turn_ref, 0) if n < tail else (end_ref.at[q // packs], (q % packs) * size)
            for t in range(tracers):
                part = is_last * halo_ref[n, pl.ds(tracers + t, levels, stride=8), :]
                if q == 0:
                    part = part + halo_ref[n, pl.ds(t, levels, stride=8), :]
                for dx in range(3):
                    part = part + explicit_ref[n, pl.ds((3 * q + dx) * tracers + t, levels, stride=stored), :]
                into[t * slot : t * slot + levels, low : low + size] = part[:, :size]
            into[levels : levels + 1, low : low + size] = count[:, n * LANES : n * LANES + size]
            if n < tail:
                long_ref[q * child_rows + n * LANES : q * child_rows + n * LANES + size, :] = turn_ref[...].T
    for part in range((narrow + packs - 1) // packs):
        turned = end_ref[part].T
        for q in range(part * packs, min(narrow, (part + 1) * packs)):
            low = (q % packs) * tail_size
            high = (q + 1) * child_rows
            long_ref[high - tail_size : high, :] = turned[low : low + tail_size]
    for q in range(narrow):
        mean = one_ninth * (
            long_ref[pl.ds(q * child_rows, covered, stride=3), :]
            + long_ref[pl.ds(q * child_rows + 1, covered, stride=3), :]
            + long_ref[pl.ds(q * child_rows + 2, covered, stride=3), :]
        )
        own_ref[pl.ds(q * all_rows + offset, covered), :] = mean
    for s in range(strips):
        band = (member ^ s) * rows
        for q in range(narrow):
            send_refs[s][(narrow + q) * rows : (narrow + q + 1) * rows, :] = own_ref[
                pl.ds(pl.multiple_of(q * all_rows + band, rows), rows), :
            ]


def level_kernel(
    tracers, levels, capacity,
    cols_ref, weight_ref, carry_ref, back_ref, inverse_ref, explicit_ref, halo_ref, own_ref,
    cmid_ref, mean_ref,
    d_ref, h_ref,
):
    count = explicit_ref.shape[0]
    stored = up(capacity * tracers, 8)
    past = 3 * tracers * my_cols(cols_ref) - tracers

    def by_rows(factor, value):
        return (factor[None] * value.reshape(stored // 8, 8, LANES)).reshape(stored, LANES)

    def forward(l, carry):
        at = pl.ds(pl.multiple_of(l * stored, 8), stored)
        coef = pl.ds(pl.multiple_of(l * 8, 8), 8)
        weight, above = weight_ref[coef, :], carry_ref[coef, :]
        held = []
        for n in range(count):
            d = by_rows(weight, explicit_ref[n, at, :]) + by_rows(above, carry[2 * n])
            h = weight * halo_ref[n, coef, :] + above * carry[2 * n + 1]
            d_ref[n, at, :] = d
            h_ref[n, coef, :] = h
            held += [d, h]
        return tuple(held)

    blank = (jnp.zeros((stored, LANES), jnp.float32), jnp.zeros((8, LANES), jnp.float32)) * count
    unroll = 5 if levels % 5 == 0 else 1
    lax.fori_loop(0, levels, forward, blank, unroll=unroll)

    def backward(step, carry):
        l = levels - 1 - step
        start = pl.multiple_of(l * stored, 8)
        at = pl.ds(start, stored)
        coef = pl.ds(pl.multiple_of(l * 8, 8), 8)
        below = back_ref[coef, :]
        held = []
        for n in range(count):
            x = d_ref[n, at, :] + by_rows(below, carry[2 * n])
            h = h_ref[n, coef, :] + below * carry[2 * n + 1]
            cmid_ref[n, at, :] = x
            first = pl.ds(start, tracers)
            cmid_ref[n, first, :] = cmid_ref[n, first, :] + h[:tracers]
            last = pl.ds(start + past, tracers)
            cmid_ref[n, last, :] = cmid_ref[n, last, :] + h[tracers : 2 * tracers]
            held += [x, h]
        return tuple(held)

    lax.fori_loop(0, levels, backward, blank, unroll=unroll)
    own = own_ref[...]
    solved = jnp.dot(own, inverse_ref[...], precision=HIGH, preferred_element_type=jnp.float32)
    lane = lax.broadcasted_iota(jnp.int32, own.shape, 1)
    mean_ref[...] = jnp.where(lane == levels, own, solved)


def finish_kernel(
    strips, rows, chunks,
    cols_ref, offset_ref, own_ref, pmid_ref, inverse_ref, cmid_ref, mask_ref,
    *refs,
):
    got_refs = {s: ref for s, ref in zip(far_first(strips), refs)}
    (
        pnext_hbm, cnext_hbm,
        panel_ref, wide_ref, ends_ref, long_ref, end_ref, add_ref, next_ref, pkeep_ref, ckeep_ref,
        start_ref, sems,
    ) = refs[strips:]
    levels, capacity, tracers, child_rows = cnext_hbm.shape
    slot = LANES // tracers
    width = pmid_ref.shape[0] // rows
    narrow = capacity // 3
    covered = child_rows // 3
    all_rows = strips * rows
    tiles = tile_list(child_rows)
    live = capacity * tracers
    stored = up(live, 8)
    padded = up(narrow, 8)
    member = lax.axis_index("child")
    group = lax.axis_index("parent")
    for j, start in enumerate(strip_starts(cols_ref, strips)):
        start_ref[j] = start
    offset = offset_ref[0]
    ends_ref[...] = jnp.zeros_like(ends_ref)
    for q in range(narrow):
        for s in range(strips):
            at = pl.ds(pl.multiple_of(q * all_rows + (member ^ s) * rows, rows), rows)
            panel_ref[at, :] = got_refs[s][q * rows : (q + 1) * rows, :]
        ends_ref[q : q + 1, :] = panel_ref[pl.ds(q * all_rows + offset, 1), :]
        ends_ref[padded + q : padded + q + 1, :] = panel_ref[pl.ds(q * all_rows + offset + covered - 1, 1), :]
    solved_ends = jnp.dot(ends_ref[...], inverse_ref[...], precision=HIGH, preferred_element_type=jnp.float32)
    f = lax.broadcasted_iota(jnp.int32, (covered, 1), 0)
    first_row = (f == 0).astype(jnp.float32)
    last_row = (f == covered - 1).astype(jnp.float32)
    tail, tail_size = tiles[-1]
    packs = LANES // tail_size

    def spread(turned, n, q):
        for t in range(tracers):
            part = turned[t * slot : t * slot + levels]
            for dx in range(3):
                add_ref[n, pl.ds((3 * q + dx) * tracers + t, levels, stride=stored), :] = part

    for q in range(narrow):
        low = solved_ends[q : q + 1]
        high = solved_ends[padded + q : padded + q + 1]
        panel = panel_ref[pl.ds(q * all_rows + offset, covered), :]
        mean = own_ref[pl.ds(q * all_rows + offset, covered), :]
        coarse = mean + diffusion * mean[:, levels : levels + 1] * (first_row * low + last_row * high)
        gap = nudging * (panel - coarse)
        base = q * child_rows
        for dy in range(3):
            long_ref[pl.ds(base + dy, covered, stride=3), :] = gap
        long_ref[base : base + 1, :] = gap[:1] + diffusion * low
        long_ref[base + child_rows - 1 : base + child_rows, :] = gap[covered - 1 :] + diffusion * high
        for n, size in tiles[:-1]:
            spread(long_ref[base + n * LANES : base + n * LANES + size, :].T, n, q)
        at = (q % packs) * tail_size
        end_ref[q // packs, at : at + tail_size, :] = long_ref[base + child_rows - tail_size : base + child_rows, :]
    for part in range((narrow + packs - 1) // packs):
        turned = end_ref[part].T
        for q in range(part * packs, min(narrow, (part + 1) * packs)):
            shift = (q % packs) * tail_size
            spread(pltpu.roll(turned, (LANES - shift) % LANES, 1) if shift else turned, tail, q)

    flat_next = ckeep_ref.reshape((levels + 1) * live, child_rows)

    def write(l, carry):
        at = pl.ds(pl.multiple_of(l * stored, 8), live)
        parts = [
            (mask_ref[n, :live, :] * (cmid_ref[n, at, :] + add_ref[n, at, :]))[:, :size] for n, size in tiles
        ]
        flat_next[pl.ds(pl.multiple_of(l * live, 2), live), :] = jnp.concatenate(parts, axis=1)
        return carry

    sends = []
    step = -(-levels // chunks)
    for c in range(chunks):
        low, high = c * step, min(levels, (c + 1) * step)
        lax.fori_loop(low, high, write, 0, unroll=2)
        part = pl.ds(low, high - low)
        sends.append(pltpu.make_async_copy(ckeep_ref.at[part], cnext_hbm.at[part], sems.at[1 + c]))
        sends[-1].start()

    for s in range(strips):
        j = member ^ s
        start, cols = start_ref[j], cols_ref[group, j]
        for q in range(narrow):
            to = jnp.where(q < cols, start + q, width + q)
            wide_ref[pl.ds(pl.multiple_of(to * rows, rows), rows), :] = got_refs[s][
                (narrow + q) * rows : (narrow + q + 1) * rows, :
            ]
    pmid = pmid_ref[...]
    mean = wide_ref[: width * rows, :]
    mean = mean + diffusion * mean[:, levels : levels + 1] * pmid
    coarse = jnp.dot(mean, inverse_ref[...], precision=HIGH, preferred_element_type=jnp.float32)
    row = member * rows + lax.broadcasted_iota(jnp.int32, (width * rows, 1), 0) % rows
    inside = (row >= offset) & (row < offset + covered)
    next_ref[...] = pmid[:, levels : levels + 1] * jnp.where(inside, coarse, pmid)
    for r in range(rows):
        block = next_ref[pl.ds(r, width, stride=rows), :]
        for t in range(tracers):
            pkeep_ref[t, r] = block[:, t * slot : t * slot + levels]
    send_parent = pltpu.make_async_copy(pkeep_ref, pnext_hbm, sems.at[0])
    send_parent.start()
    sends.append(send_parent)
    for send in sends:
        send.wait()


def ring(block, axes, count, step):
    return lax.ppermute(block, axes, [(i, (i + step) % count) for i in range(count)])


def body(parent_tracer, child_tracer, strip_cols, row_offset, parent_wet, child_wet, vert_mix):
    tracers, levels, rows, width = parent_tracer.shape
    capacity, child_rows = child_wet.shape
    strips = lax.axis_size("child")
    narrow = capacity // 3
    all_rows = rows * strips
    tiles = tile_list(child_rows)
    lane_tiles = len(tiles)
    packed = -(-narrow // (LANES // tiles[-1][1]))
    stored = up(capacity * tracers, 8)
    stride = stored + 16
    plane = up(levels, 8) * stored
    chunks = 5
    message = lane_tiles * up(tracers * levels, 8) + width
    f32 = lambda *s: jax.ShapeDtypeStruct(s, jnp.float32)
    mem = lambda *s: pltpu.VMEM(s, jnp.float32)
    parent = jnp.transpose(parent_tracer, (0, 2, 3, 1))
    child = jnp.transpose(child_tracer, (1, 2, 0, 3))

    flat, forth, back, left_edge, right_edge, weight, carry, below, inverse, cols, mask = pl.pallas_call(
        prepare_kernel,
        in_specs=[HBM] * 6,
        out_specs=[VM] * 11,
        out_shape=[
            f32(width * rows, LANES), f32(message, LANES), f32(message, LANES), f32(rows, LANES), f32(rows, LANES),
            f32(8 * levels, LANES), f32(8 * levels, LANES), f32(8 * levels, LANES), f32(LANES, LANES),
            jax.ShapeDtypeStruct(strip_cols.shape, jnp.int32), f32(lane_tiles, stored + 8, LANES),
        ],
        scratch_shapes=[
            pltpu.SMEM(strip_cols.shape, jnp.int32),
            pltpu.SMEM(vert_mix.shape, jnp.float32),
            mem(*parent.shape),
            pltpu.VMEM(parent_wet.shape, jnp.int32),
            pltpu.VMEM(child_wet.shape, jnp.int32),
            mem(2, levels, 1, tracers, child_rows),
            mem(LANES, LANES),
            mem(rows, width, LANES),
            mem(8 * levels, LANES),
            mem(8 * levels, LANES),
            pltpu.SemaphoreType.DMA((8,)),
        ],
        compiler_params=params(16),
        name="prepare",
    )(*(in_hbm(x) for x in (strip_cols, vert_mix, parent, parent_wet, child, child_wet)))

    groups = lax.axis_size("parent")
    devices = groups * strips
    right_edge = ring(right_edge, "parent", groups, 1)
    left_edge = ring(left_edge, "parent", groups, -1)
    forth = ring(forth, ("parent", "child"), devices, 1)
    back = ring(back, ("parent", "child"), devices, -1)

    explicit = pl.pallas_call(
        inner_kernel,
        in_specs=[VM, VM],
        out_specs=VM,
        out_shape=f32(lane_tiles, plane, LANES),
        scratch_shapes=[mem(lane_tiles, levels * stride, LANES)],
        compiler_params=params(16),
        name="inner",
    )(child, mask)

    block = f32(2 * narrow * rows, LANES)
    *blocks, parent_mid, own, halo = pl.pallas_call(
        functools.partial(pack_kernel, groups, strips, rows, tracers, levels),
        in_specs=[SM, SM] + [VM] * 8,
        out_specs=[VM] * (strips + 3),
        out_shape=[block] * strips
        + [f32(width * rows, LANES), f32(narrow * all_rows, LANES), f32(lane_tiles, 8 * up(levels, 8), LANES)],
        scratch_shapes=[
            mem(width * rows, LANES),
            mem((width + narrow) * rows, LANES),
            mem(LANES, LANES),
            mem(packed, LANES, LANES),
            mem(narrow * child_rows, LANES),
            pltpu.SMEM((strips,), jnp.int32),
        ],
        compiler_params=params(16),
        name="pack",
    )(cols, row_offset, flat, forth, back, right_edge, left_edge, inverse, explicit, child_wet)

    got = {0: blocks[0]}
    for s in far_first(strips)[:-1]:
        got[s] = lax.ppermute(blocks[s], "child", [(i, i ^ s) for i in range(strips)])
    got = [got[s] for s in far_first(strips)]

    child_mid, mean = pl.pallas_call(
        functools.partial(level_kernel, tracers, levels, capacity),
        in_specs=[SM] + [VM] * 7,
        out_specs=[VM, VM],
        out_shape=[f32(lane_tiles, plane, LANES), f32(narrow * all_rows, LANES)],
        scratch_shapes=[mem(lane_tiles, levels * stored, LANES), mem(lane_tiles, 8 * levels, LANES)],
        compiler_params=params(16),
        name="levels",
    )(cols, weight, carry, below, inverse, explicit, halo, own)

    parent_next, child_next = pl.pallas_call(
        functools.partial(finish_kernel, strips, rows, chunks),
        in_specs=[SM, SM] + [VM] * (5 + strips),
        out_specs=[HBM, HBM],
        out_shape=[f32(*parent.shape), f32(*child.shape)],
        scratch_shapes=[
            mem(narrow * all_rows, LANES),
            mem((width + narrow) * rows, LANES),
            mem(2 * up(narrow, 8), LANES),
            mem(narrow * child_rows, LANES),
            mem(packed, LANES, LANES),
            mem(lane_tiles, plane, LANES),
            mem(width * rows, LANES),
            mem(*parent.shape),
            mem(levels + 1, *child.shape[1:]),
            pltpu.SMEM((strips,), jnp.int32),
            pltpu.SemaphoreType.DMA((1 + chunks,)),
        ],
        compiler_params=params(24),
        name="finish",
    )(cols, row_offset, mean, parent_mid, inverse, child_mid, mask, *got)
    return jnp.transpose(parent_next, (0, 3, 1, 2)), jnp.transpose(child_next, (2, 0, 1, 3))


def solution(mesh):
    return jax.shard_map(
        body,
        mesh=mesh,
        in_specs=(
            P(None, None, "child", "parent"),
            P(None, None, ("parent", "child"), None),
            P(),
            P(),
            P("child", "parent"),
            P(("parent", "child"), None),
            P(),
        ),
        out_specs=(P(None, None, "child", "parent"), P(None, None, ("parent", "child"), None)),
        check_vma=False,
    )
```

```python
import functools

import jax
import jax.numpy as jnp
from jax import lax
from jax.experimental import pallas as pl
from jax.experimental.pallas import tpu as pltpu
from jax.sharding import PartitionSpec as P

diffusion = 0.2
nudging = 0.5
one_ninth = 1.0 / 9.0
LANES = 128
HIGH = lax.Precision.HIGHEST

VM = pl.BlockSpec(memory_space=pltpu.VMEM)
SM = pl.BlockSpec(memory_space=pltpu.SMEM)
HBM = pl.BlockSpec(memory_space=pltpu.HBM)


def params(mib):
    return pltpu.CompilerParams(vmem_limit_bytes=mib << 20)


def in_hbm(x):
    return pltpu.with_memory_space_constraint(x, pltpu.HBM)


def far_first(strips):
    return list(reversed(range(strips)))


def up(n, m):
    return (n + m - 1) // m * m


def tile_list(child_rows):
    return [(t, min(LANES, child_rows - t * LANES)) for t in range((child_rows + LANES - 1) // LANES)]


def my_cols(cols_ref):
    return cols_ref[lax.axis_index("parent"), lax.axis_index("child")]


def strip_starts(cols_ref, strips):
    group = lax.axis_index("parent")
    start = jnp.int32(0)
    starts = []
    for j in range(strips):
        starts.append(start)
        start = start + cols_ref[group, j]
    return starts


def coefficients(mix_ref, weight_ref, carry_ref, back_ref, inverse_ref, d_ref, c_ref):
    tracers, levels = mix_ref.shape[0], mix_ref.shape[1] + 1
    slot = LANES // tracers
    lane = lax.broadcasted_iota(jnp.int32, (8, LANES), 1)
    by_lane = lane // slot
    by_row = lax.broadcasted_iota(jnp.int32, (8, LANES), 0) % tracers
    none = jnp.zeros((8, LANES), jnp.float32)

    def mixed(k, which):
        row = none
        if 0 <= k < levels - 1:
            for t in range(tracers):
                row = jnp.where(which == t, mix_ref[t, k], row)
        return row

    weights = [none, none]
    d = none
    for k in range(levels):
        for n, which in enumerate((by_row, by_lane)):
            above, below = mixed(k - 1, which), mixed(k, which)
            w = 1.0 / (1.0 + above + below - above * (above * weights[n]))
            weights[n] = w
            at = pl.ds(8 * k, 8)
            if n == 0:
                weight_ref[at, :] = w
                carry_ref[at, :] = above * w
                back_ref[at, :] = below * w
            else:
                unit = (lane - which * slot == k).astype(jnp.float32)
                d = (unit + above * d) * w
                d_ref[at, :] = d
                c_ref[at, :] = below * w
    inverse_ref[...] = jnp.zeros_like(inverse_ref)
    x = none
    for k in reversed(range(levels)):
        x = d_ref[pl.ds(8 * k, 8), :] + c_ref[pl.ds(8 * k, 8), :] * x
        for t in range(tracers):
            inverse_ref[t * slot + k : t * slot + k + 1, :] = jnp.where(by_lane == t, x, 0.0)[:1]


def prepare_kernel(
    cols_hbm, mix_hbm, parent_hbm, pwet_hbm, child_hbm, cwet_hbm,
    flat_ref, forth_ref, back_ref, left_ref, right_ref, weight_ref, carry_ref, below_ref, inverse_ref, again_ref,
    mask_ref,
    cols_ref, mix_ref, parent_ref, pwet_ref, cwet_ref, edge_ref, turn_ref, row_ref, d_ref, c_ref, sems,
):
    levels, capacity, tracers, child_rows = child_hbm.shape
    rows, width = pwet_ref.shape
    slot = LANES // tracers
    level_rows = up(tracers * levels, 8)
    tiles = tile_list(child_rows)
    fetch_cols = pltpu.make_async_copy(cols_hbm, cols_ref, sems.at[0])
    fetch_pwet = pltpu.make_async_copy(pwet_hbm, pwet_ref, sems.at[1])
    fetch_parent = pltpu.make_async_copy(parent_hbm, parent_ref, sems.at[2])
    fetch_cwet = pltpu.make_async_copy(cwet_hbm, cwet_ref, sems.at[3])
    fetch_first = pltpu.make_async_copy(child_hbm.at[:, pl.ds(0, 1)], edge_ref.at[1], sems.at[4])
    fetch_mix = pltpu.make_async_copy(mix_hbm, mix_ref, sems.at[6])
    fetch_again = pltpu.make_async_copy(cols_hbm, again_ref, sems.at[7])
    for fetch in (fetch_cols, fetch_mix, fetch_again, fetch_pwet, fetch_parent, fetch_first, fetch_cwet):
        fetch.start()
    fetch_cols.wait()
    last = 3 * my_cols(cols_ref) - 1
    fetch_last = pltpu.make_async_copy(child_hbm.at[:, pl.ds(last, 1)], edge_ref.at[0], sems.at[5])
    fetch_last.start()
    row_ref[...] = jnp.zeros_like(row_ref)
    fetch_mix.wait()
    coefficients(mix_ref, weight_ref, carry_ref, below_ref, inverse_ref, d_ref, c_ref)
    fetch_pwet.wait()
    turn_ref[:rows, :width] = pwet_ref[...].astype(jnp.float32)
    wet = turn_ref[...].T
    fetch_parent.wait()
    for r in range(rows):
        cell = wet[:width, r : r + 1]
        for t in range(tracers):
            row_ref[r, :, t * slot : t * slot + levels] = cell * parent_ref[t, r]
        row_ref[r, :, levels : levels + 1] = cell
        flat_ref[pl.ds(r, width, stride=rows), :] = row_ref[r]
    left_ref[...] = flat_ref[:rows, :]
    right_ref[...] = flat_ref[(width - 1) * rows :, :]
    fetch_cwet.wait()
    masks(cols_ref, cwet_ref, mask_ref, tracers)
    fetch_again.wait()
    base = len(tiles) * level_rows
    fetch_first.wait()
    fetch_last.wait()
    for side, (ref, x, r) in enumerate(((forth_ref, last, rows - 1), (back_ref, 0, 0))):
        cell = cwet_ref[pl.ds(x, 1), :].astype(jnp.float32)
        pairs = edge_ref.at[side].reshape(levels * tracers, child_rows)[...] * cell
        for n, size in tiles:
            ref[n * level_rows : n * level_rows + levels * tracers, :size] = pairs[:, n * LANES : n * LANES + size]
        ref[base : base + width, :] = row_ref[r]


def masks(cols_ref, cwet_ref, mask_ref, tracers):
    capacity, child_rows = cwet_ref.shape
    column = lax.broadcasted_iota(jnp.int32, (capacity, 1), 0)
    mask = cwet_ref[...].astype(jnp.float32) * (column < 3 * my_cols(cols_ref)).astype(jnp.float32)
    mask_ref[...] = jnp.zeros_like(mask_ref)
    for n, size in tile_list(child_rows):
        part = mask[:, n * LANES : n * LANES + size]
        if size < LANES:
            part = jnp.concatenate([part, jnp.zeros((capacity, LANES - size), jnp.float32)], axis=1)
        for t in range(tracers):
            mask_ref[n, pl.ds(t, capacity, stride=tracers), :] = part
    return mask


def inner_kernel(
    child_ref, mask_ref,
    explicit_ref,
    begin_ref,
):
    levels, capacity, tracers, child_rows = child_ref.shape
    tiles = tile_list(child_rows)
    live = capacity * tracers
    stored = up(live, 8)
    stride = begin_ref.shape[1] // levels
    flat_child = child_ref.reshape(levels * live, child_rows)
    lane = lax.broadcasted_iota(jnp.int32, (stored, LANES), 1)
    gap = jnp.zeros((tracers, LANES), jnp.float32)
    after = stored - live + tracers

    def explicit(l, carry):
        cells = flat_child[pl.ds(pl.multiple_of(l * live, 2), live), :]
        start = pl.multiple_of(l * stride, 8)
        for n, size in tiles:
            part = cells[:, n * LANES : n * LANES + size] * mask_ref[n, :live, :size]
            if size < LANES:
                part = jnp.concatenate([part, jnp.zeros((live, LANES - size), jnp.float32)], axis=1)
            begin_ref[n, pl.ds(start + 8, live), :] = part
            begin_ref[n, pl.ds(start + 8 - tracers, tracers), :] = gap
            begin_ref[n, pl.ds(start + 8 + live, after), :] = jnp.zeros((after, LANES), jnp.float32)
        here = [begin_ref[n, pl.ds(start + 8, stored), :] for n, _ in tiles]
        lower = [pltpu.roll(c, 1, 1) for c in here]
        upper = [pltpu.roll(c, LANES - 1, 1) for c in here]
        for n, size in tiles:
            south = jnp.where(lane == 0, lower[n - 1] if n else 0.0, lower[n])
            if n + 1 < len(tiles):
                north = jnp.where(lane == LANES - 1, upper[n + 1], upper[n])
            else:
                north = jnp.where(lane == size - 1, 0.0, upper[n])
            west = begin_ref[n, pl.ds(start + 8 - tracers, stored), :]
            east = begin_ref[n, pl.ds(start + 8 + tracers, stored), :]
            explicit_ref[n, pl.ds(pl.multiple_of(l * stored, 8), stored), :] = (diffusion * mask_ref[n, :stored, :]) * (
                here[n] + west + east + south + north
            )
        return carry

    lax.fori_loop(0, levels, explicit, 0, unroll=25 if levels % 25 == 0 else 1)


def pack_kernel(
    groups, strips, rows, tracers, levels,
    cols_hbm, offset_ref, flat_ref, before_ref, after_ref, left_ref, right_ref, inverse_ref, explicit_ref, cwet_ref,
    *refs,
):
    send_refs = refs[:strips]
    pmid_ref, own_ref, halo_ref, step_ref, wide_ref, turn_ref, end_ref, long_ref, start_ref, cols_ref, sem = refs[strips:]
    fetch_cols = pltpu.make_async_copy(cols_hbm, cols_ref, sem)
    fetch_cols.start()
    capacity, child_rows = cwet_ref.shape
    stored = up(capacity * tracers, 8)
    slot = LANES // tracers
    width = flat_ref.shape[0] // rows
    narrow = capacity // 3
    covered = child_rows // 3
    all_rows = strips * rows
    tiles = tile_list(child_rows)
    level_rows = up(tracers * levels, 8)
    base = len(tiles) * level_rows
    group, member = lax.axis_index("parent"), lax.axis_index("child")
    offset = offset_ref[0]

    has_before = (member > 0).astype(jnp.float32)
    has_after = (member < strips - 1).astype(jnp.float32)
    has_left = (group > 0).astype(jnp.float32)
    has_right = (group < groups - 1).astype(jnp.float32)
    for x in range(width):
        here = flat_ref[x * rows : (x + 1) * rows, :]
        west = has_left * left_ref[...] if x == 0 else flat_ref[(x - 1) * rows : x * rows, :]
        east = has_right * right_ref[...] if x == width - 1 else flat_ref[(x + 1) * rows : (x + 2) * rows, :]
        south = jnp.concatenate([has_before * before_ref[base + x : base + x + 1, :], here[:-1]], axis=0)
        north = jnp.concatenate([here[1:], has_after * after_ref[base + x : base + x + 1, :]], axis=0)
        wet = here[:, levels : levels + 1]
        laplace = north + south + east + west - 4.0 * here
        step_ref[x * rows : (x + 1) * rows, :] = wet * (here + diffusion * laplace)
    solved = jnp.dot(step_ref[...], inverse_ref[...], precision=HIGH, preferred_element_type=jnp.float32)
    lane = lax.broadcasted_iota(jnp.int32, (width * rows, LANES), 1)
    solved = jnp.where(lane == levels, flat_ref[...], solved)
    wide_ref[: width * rows, :] = solved
    wide_ref[width * rows :, :] = jnp.zeros((narrow * rows, LANES), jnp.float32)
    pmid_ref[...] = solved
    fetch_cols.wait()
    cols = my_cols(cols_ref)
    for j, start in enumerate(strip_starts(cols_ref, strips)):
        start_ref[j] = start
    for s in range(strips):
        start = start_ref[member ^ s]
        send_refs[s][: narrow * rows, :] = wide_ref[pl.ds(pl.multiple_of(start * rows, rows), narrow * rows), :]

    column = lax.broadcasted_iota(jnp.int32, (capacity, 1), 0)
    mask = cwet_ref[...].astype(jnp.float32) * (column < 3 * cols).astype(jnp.float32)
    west_mask = (diffusion * jnp.maximum(has_before, has_left)) * mask[:1]
    east_wet = cwet_ref[pl.ds(3 * cols - 1, 1), :].astype(jnp.float32)
    east_mask = (diffusion * jnp.maximum(has_after, has_right)) * east_wet
    halo_ref[...] = jnp.zeros_like(halo_ref)
    for n, size in tiles:
        part = slice(n * LANES, n * LANES + size)
        for l in range(levels):
            edge = slice(n * level_rows + l * tracers, n * level_rows + (l + 1) * tracers)
            halo_ref[n, 8 * l : 8 * l + tracers, :size] = west_mask[:, part] * before_ref[edge, :size]
            halo_ref[n, 8 * l + tracers : 8 * l + 2 * tracers, :size] = east_mask[:, part] * after_ref[edge, :size]

    own_ref[...] = jnp.zeros_like(own_ref)
    turn_ref[...] = jnp.zeros_like(turn_ref)
    end_ref[...] = jnp.zeros_like(end_ref)
    y = lax.broadcasted_iota(jnp.int32, (1, child_rows), 1)
    at_end = ((y == 0) | (y == child_rows - 1)).astype(jnp.float32)
    tail, tail_size = tiles[-1]
    packs = LANES // tail_size
    for q in range(narrow):
        count = (mask[3 * q : 3 * q + 1] + mask[3 * q + 1 : 3 * q + 2] + mask[3 * q + 2 : 3 * q + 3]) * at_end
        is_last = (cols == q + 1).astype(jnp.float32)
        for n, size in tiles:
            into, low = (turn_ref, 0) if n < tail else (end_ref.at[q // packs], (q % packs) * size)
            for t in range(tracers):
                part = is_last * halo_ref[n, pl.ds(tracers + t, levels, stride=8), :]
                if q == 0:
                    part = part + halo_ref[n, pl.ds(t, levels, stride=8), :]
                for dx in range(3):
                    part = part + explicit_ref[n, pl.ds((3 * q + dx) * tracers + t, levels, stride=stored), :]
                into[t * slot : t * slot + levels, low : low + size] = part[:, :size]
            into[levels : levels + 1, low : low + size] = count[:, n * LANES : n * LANES + size]
            if n < tail:
                long_ref[q * child_rows + n * LANES : q * child_rows + n * LANES + size, :] = turn_ref[...].T
    for part in range((narrow + packs - 1) // packs):
        turned = end_ref[part].T
        for q in range(part * packs, min(narrow, (part + 1) * packs)):
            low = (q % packs) * tail_size
            high = (q + 1) * child_rows
            long_ref[high - tail_size : high, :] = turned[low : low + tail_size]
    for q in range(narrow):
        mean = one_ninth * (
            long_ref[pl.ds(q * child_rows, covered, stride=3), :]
            + long_ref[pl.ds(q * child_rows + 1, covered, stride=3), :]
            + long_ref[pl.ds(q * child_rows + 2, covered, stride=3), :]
        )
        own_ref[pl.ds(q * all_rows + offset, covered), :] = mean
    for s in range(strips):
        band = (member ^ s) * rows
        for q in range(narrow):
            send_refs[s][(narrow + q) * rows : (narrow + q + 1) * rows, :] = own_ref[
                pl.ds(pl.multiple_of(q * all_rows + band, rows), rows), :
            ]


def level_kernel(
    tracers, levels, capacity,
    cols_ref, weight_ref, carry_ref, back_ref, inverse_ref, explicit_ref, halo_ref, own_ref,
    cmid_ref, mean_ref,
    d_ref, h_ref,
):
    count = explicit_ref.shape[0]
    stored = up(capacity * tracers, 8)
    past = 3 * tracers * my_cols(cols_ref) - tracers

    def by_rows(factor, value):
        return (factor[None] * value.reshape(stored // 8, 8, LANES)).reshape(stored, LANES)

    def forward(l, carry):
        at = pl.ds(pl.multiple_of(l * stored, 8), stored)
        coef = pl.ds(pl.multiple_of(l * 8, 8), 8)
        weight, above = weight_ref[coef, :], carry_ref[coef, :]
        held = []
        for n in range(count):
            d = by_rows(weight, explicit_ref[n, at, :]) + by_rows(above, carry[2 * n])
            h = weight * halo_ref[n, coef, :] + above * carry[2 * n + 1]
            d_ref[n, at, :] = d
            h_ref[n, coef, :] = h
            held += [d, h]
        return tuple(held)

    blank = (jnp.zeros((stored, LANES), jnp.float32), jnp.zeros((8, LANES), jnp.float32)) * count
    unroll = 5 if levels % 5 == 0 else 1
    lax.fori_loop(0, levels, forward, blank, unroll=unroll)

    def backward(step, carry):
        l = levels - 1 - step
        start = pl.multiple_of(l * stored, 8)
        at = pl.ds(start, stored)
        coef = pl.ds(pl.multiple_of(l * 8, 8), 8)
        below = back_ref[coef, :]
        held = []
        for n in range(count):
            x = d_ref[n, at, :] + by_rows(below, carry[2 * n])
            h = h_ref[n, coef, :] + below * carry[2 * n + 1]
            cmid_ref[n, at, :] = x
            first = pl.ds(start, tracers)
            cmid_ref[n, first, :] = cmid_ref[n, first, :] + h[:tracers]
            last = pl.ds(start + past, tracers)
            cmid_ref[n, last, :] = cmid_ref[n, last, :] + h[tracers : 2 * tracers]
            held += [x, h]
        return tuple(held)

    lax.fori_loop(0, levels, backward, blank, unroll=unroll)
    own = own_ref[...]
    solved = jnp.dot(own, inverse_ref[...], precision=HIGH, preferred_element_type=jnp.float32)
    lane = lax.broadcasted_iota(jnp.int32, own.shape, 1)
    mean_ref[...] = jnp.where(lane == levels, own, solved)


def finish_kernel(
    strips, rows, chunks,
    cols_hbm, offset_ref, own_ref, pmid_ref, inverse_ref, cmid_ref, mask_ref,
    *refs,
):
    got_refs = {s: ref for s, ref in zip(far_first(strips), refs)}
    (
        pnext_hbm, cnext_hbm,
        panel_ref, wide_ref, ends_ref, long_ref, end_ref, add_ref, next_ref, pkeep_ref, ckeep_ref,
        start_ref, cols_ref, sems,
    ) = refs[strips:]
    fetch_cols = pltpu.make_async_copy(cols_hbm, cols_ref, sems.at[1 + chunks])
    fetch_cols.start()
    levels, capacity, tracers, child_rows = cnext_hbm.shape
    slot = LANES // tracers
    width = pmid_ref.shape[0] // rows
    narrow = capacity // 3
    covered = child_rows // 3
    all_rows = strips * rows
    tiles = tile_list(child_rows)
    live = capacity * tracers
    stored = up(live, 8)
    padded = up(narrow, 8)
    member = lax.axis_index("child")
    group = lax.axis_index("parent")
    offset = offset_ref[0]
    ends_ref[...] = jnp.zeros_like(ends_ref)
    for q in range(narrow):
        for s in range(strips):
            at = pl.ds(pl.multiple_of(q * all_rows + (member ^ s) * rows, rows), rows)
            panel_ref[at, :] = got_refs[s][q * rows : (q + 1) * rows, :]
        ends_ref[q : q + 1, :] = panel_ref[pl.ds(q * all_rows + offset, 1), :]
        ends_ref[padded + q : padded + q + 1, :] = panel_ref[pl.ds(q * all_rows + offset + covered - 1, 1), :]
    solved_ends = jnp.dot(ends_ref[...], inverse_ref[...], precision=HIGH, preferred_element_type=jnp.float32)
    f = lax.broadcasted_iota(jnp.int32, (covered, 1), 0)
    first_row = (f == 0).astype(jnp.float32)
    last_row = (f == covered - 1).astype(jnp.float32)
    tail, tail_size = tiles[-1]
    packs = LANES // tail_size

    def spread(turned, n, q):
        for t in range(tracers):
            part = turned[t * slot : t * slot + levels]
            for dx in range(3):
                add_ref[n, pl.ds((3 * q + dx) * tracers + t, levels, stride=stored), :] = part

    for q in range(narrow):
        low = solved_ends[q : q + 1]
        high = solved_ends[padded + q : padded + q + 1]
        panel = panel_ref[pl.ds(q * all_rows + offset, covered), :]
        mean = own_ref[pl.ds(q * all_rows + offset, covered), :]
        coarse = mean + diffusion * mean[:, levels : levels + 1] * (first_row * low + last_row * high)
        gap = nudging * (panel - coarse)
        base = q * child_rows
        for dy in range(3):
            long_ref[pl.ds(base + dy, covered, stride=3), :] = gap
        long_ref[base : base + 1, :] = gap[:1] + diffusion * low
        long_ref[base + child_rows - 1 : base + child_rows, :] = gap[covered - 1 :] + diffusion * high
        for n, size in tiles[:-1]:
            spread(long_ref[base + n * LANES : base + n * LANES + size, :].T, n, q)
        at = (q % packs) * tail_size
        end_ref[q // packs, at : at + tail_size, :] = long_ref[base + child_rows - tail_size : base + child_rows, :]
    for part in range((narrow + packs - 1) // packs):
        turned = end_ref[part].T
        for q in range(part * packs, min(narrow, (part + 1) * packs)):
            shift = (q % packs) * tail_size
            spread(pltpu.roll(turned, (LANES - shift) % LANES, 1) if shift else turned, tail, q)

    flat_next = ckeep_ref.reshape((levels + 1) * live, child_rows)

    def write(l, carry):
        at = pl.ds(pl.multiple_of(l * stored, 8), live)
        parts = [
            (mask_ref[n, :live, :] * (cmid_ref[n, at, :] + add_ref[n, at, :]))[:, :size] for n, size in tiles
        ]
        flat_next[pl.ds(pl.multiple_of(l * live, 2), live), :] = jnp.concatenate(parts, axis=1)
        return carry

    sends = []
    step = -(-levels // chunks)
    for c in range(chunks):
        low, high = c * step, min(levels, (c + 1) * step)
        lax.fori_loop(low, high, write, 0, unroll=2)
        part = pl.ds(low, high - low)
        sends.append(pltpu.make_async_copy(ckeep_ref.at[part], cnext_hbm.at[part], sems.at[1 + c]))
        sends[-1].start()

    fetch_cols.wait()
    for j, start in enumerate(strip_starts(cols_ref, strips)):
        start_ref[j] = start
    for s in range(strips):
        j = member ^ s
        start, cols = start_ref[j], cols_ref[group, j]
        for q in range(narrow):
            to = jnp.where(q < cols, start + q, width + q)
            wide_ref[pl.ds(pl.multiple_of(to * rows, rows), rows), :] = got_refs[s][
                (narrow + q) * rows : (narrow + q + 1) * rows, :
            ]
    pmid = pmid_ref[...]
    mean = wide_ref[: width * rows, :]
    mean = mean + diffusion * mean[:, levels : levels + 1] * pmid
    coarse = jnp.dot(mean, inverse_ref[...], precision=HIGH, preferred_element_type=jnp.float32)
    row = member * rows + lax.broadcasted_iota(jnp.int32, (width * rows, 1), 0) % rows
    inside = (row >= offset) & (row < offset + covered)
    next_ref[...] = pmid[:, levels : levels + 1] * jnp.where(inside, coarse, pmid)
    for r in range(rows):
        block = next_ref[pl.ds(r, width, stride=rows), :]
        for t in range(tracers):
            pkeep_ref[t, r] = block[:, t * slot : t * slot + levels]
    send_parent = pltpu.make_async_copy(pkeep_ref, pnext_hbm, sems.at[0])
    send_parent.start()
    sends.append(send_parent)
    for send in sends:
        send.wait()


def ring(block, axes, count, step):
    return lax.ppermute(block, axes, [(i, (i + step) % count) for i in range(count)])


def body(parent_tracer, child_tracer, strip_cols, row_offset, parent_wet, child_wet, vert_mix):
    tracers, levels, rows, width = parent_tracer.shape
    capacity, child_rows = child_wet.shape
    strips = lax.axis_size("child")
    narrow = capacity // 3
    all_rows = rows * strips
    tiles = tile_list(child_rows)
    lane_tiles = len(tiles)
    packed = -(-narrow // (LANES // tiles[-1][1]))
    stored = up(capacity * tracers, 8)
    stride = stored + 16
    plane = up(levels, 8) * stored
    chunks = 5
    message = lane_tiles * up(tracers * levels, 8) + width
    f32 = lambda *s: jax.ShapeDtypeStruct(s, jnp.float32)
    mem = lambda *s: pltpu.VMEM(s, jnp.float32)
    parent = jnp.transpose(parent_tracer, (0, 2, 3, 1))
    child = jnp.transpose(child_tracer, (1, 2, 0, 3))

    flat, forth, back, left_edge, right_edge, weight, carry, below, inverse, cols, mask = pl.pallas_call(
        prepare_kernel,
        in_specs=[HBM] * 6,
        out_specs=[VM] * 11,
        out_shape=[
            f32(width * rows, LANES), f32(message, LANES), f32(message, LANES), f32(rows, LANES), f32(rows, LANES),
            f32(8 * levels, LANES), f32(8 * levels, LANES), f32(8 * levels, LANES), f32(LANES, LANES),
            jax.ShapeDtypeStruct(strip_cols.shape, jnp.int32), f32(lane_tiles, stored + 8, LANES),
        ],
        scratch_shapes=[
            pltpu.SMEM(strip_cols.shape, jnp.int32),
            pltpu.SMEM(vert_mix.shape, jnp.float32),
            mem(*parent.shape),
            pltpu.VMEM(parent_wet.shape, jnp.int32),
            pltpu.VMEM(child_wet.shape, jnp.int32),
            mem(2, levels, 1, tracers, child_rows),
            mem(LANES, LANES),
            mem(rows, width, LANES),
            mem(8 * levels, LANES),
            mem(8 * levels, LANES),
            pltpu.SemaphoreType.DMA((8,)),
        ],
        compiler_params=params(16),
        name="prepare",
    )(*(in_hbm(x) for x in (strip_cols, vert_mix, parent, parent_wet, child, child_wet)))

    groups = lax.axis_size("parent")
    devices = groups * strips
    right_edge = ring(right_edge, "parent", groups, 1)
    left_edge = ring(left_edge, "parent", groups, -1)
    forth = ring(forth, ("parent", "child"), devices, 1)
    back = ring(back, ("parent", "child"), devices, -1)

    explicit = pl.pallas_call(
        inner_kernel,
        in_specs=[VM, VM],
        out_specs=VM,
        out_shape=f32(lane_tiles, plane, LANES),
        scratch_shapes=[mem(lane_tiles, levels * stride, LANES)],
        compiler_params=params(16),
        name="inner",
    )(child, mask)

    block = f32(2 * narrow * rows, LANES)
    *blocks, parent_mid, own, halo = pl.pallas_call(
        functools.partial(pack_kernel, groups, strips, rows, tracers, levels),
        in_specs=[HBM, SM] + [VM] * 8,
        out_specs=[VM] * (strips + 3),
        out_shape=[block] * strips
        + [f32(width * rows, LANES), f32(narrow * all_rows, LANES), f32(lane_tiles, 8 * up(levels, 8), LANES)],
        scratch_shapes=[
            mem(width * rows, LANES),
            mem((width + narrow) * rows, LANES),
            mem(LANES, LANES),
            mem(packed, LANES, LANES),
            mem(narrow * child_rows, LANES),
            pltpu.SMEM((strips,), jnp.int32),
            pltpu.SMEM(strip_cols.shape, jnp.int32),
            pltpu.SemaphoreType.DMA(()),
        ],
        compiler_params=params(16),
        name="pack",
    )(in_hbm(strip_cols), row_offset, flat, forth, back, right_edge, left_edge, inverse, explicit, child_wet)

    got = {0: blocks[0]}
    for s in far_first(strips)[:-1]:
        got[s] = lax.ppermute(blocks[s], "child", [(i, i ^ s) for i in range(strips)])
    got = [got[s] for s in far_first(strips)]

    child_mid, mean = pl.pallas_call(
        functools.partial(level_kernel, tracers, levels, capacity),
        in_specs=[SM] + [VM] * 7,
        out_specs=[VM, VM],
        out_shape=[f32(lane_tiles, plane, LANES), f32(narrow * all_rows, LANES)],
        scratch_shapes=[mem(lane_tiles, levels * stored, LANES), mem(lane_tiles, 8 * levels, LANES)],
        compiler_params=params(16),
        name="levels",
    )(cols, weight, carry, below, inverse, explicit, halo, own)

    parent_next, child_next = pl.pallas_call(
        functools.partial(finish_kernel, strips, rows, chunks),
        in_specs=[HBM, SM] + [VM] * (5 + strips),
        out_specs=[HBM, HBM],
        out_shape=[f32(*parent.shape), f32(*child.shape)],
        scratch_shapes=[
            mem(narrow * all_rows, LANES),
            mem((width + narrow) * rows, LANES),
            mem(2 * up(narrow, 8), LANES),
            mem(narrow * child_rows, LANES),
            mem(packed, LANES, LANES),
            mem(lane_tiles, plane, LANES),
            mem(width * rows, LANES),
            mem(*parent.shape),
            mem(levels + 1, *child.shape[1:]),
            pltpu.SMEM((strips,), jnp.int32),
            pltpu.SMEM(strip_cols.shape, jnp.int32),
            pltpu.SemaphoreType.DMA((2 + chunks,)),
        ],
        compiler_params=params(24),
        name="finish",
    )(in_hbm(strip_cols), row_offset, mean, parent_mid, inverse, child_mid, mask, *got)
    return jnp.transpose(parent_next, (0, 3, 1, 2)), jnp.transpose(child_next, (2, 0, 1, 3))


def solution(mesh):
    return jax.shard_map(
        body,
        mesh=mesh,
        in_specs=(
            P(None, None, "child", "parent"),
            P(None, None, ("parent", "child"), None),
            P(),
            P(),
            P("child", "parent"),
            P(("parent", "child"), None),
            P(),
        ),
        out_specs=(P(None, None, "child", "parent"), P(None, None, ("parent", "child"), None)),
        check_vma=False,
    )
```
